32 devices in a mesh: xi: 4 (over x, core), eta: 4 (over z), zeta: 2 (over y).
Axes of the slice: x: 2, y: 2, z: 4, core: 2. Of those that a mesh axis runs over, the one named last changes fastest.
Arguments:
- conserved_solution: float32 [5, 64, 64, 256], P(None, 'xi', 'eta', 'zeta'), may hold values from -1.2 to 6, as said below
- metrics: float32 [3, 3, 64, 64, 256], P(None, None, 'xi', 'eta', 'zeta'), may hold values from -0.4 to 1.4, as said below
- jacobian: float32 [64, 64, 256], P('xi', 'eta', 'zeta'), may hold values from 0.7 to 1.4
Outputs:
- filtered: float32 [5, 64, 64, 256], P(None, 'xi', 'eta', 'zeta')
The draws below stay inside these ranges and needn't reach their ends.
Inputs may be any that keep to these rules, and one draw needn't show every extreme that they name: conserved_solution[0] (density) lies between 0.5 and 2, and the pressure 0.4 (conserved_solution[4] - (conserved_solution[1]^2 + conserved_solution[2]^2 + conserved_solution[3]^2) / (2 conserved_solution[0])) lies between 0.5 and 1.5. The entries metrics[k, k] lie between 0.7 and 1.4, the others between -0.4 and 0.4.
All inputs are finite; a program needn't handle non-finite values.
Results may differ from the reference program's by a relative error of at most 0.00005.
Values sent between devices are 32-bit elements; how exact they have to be, the bound alone decides.
No kernel may reach another device: no remote copies, remote signals or barrier semaphores. Data moves between devices by JAX's collectives and lax.ppermute only.
A program may use at most 64 MiB of HBM per device.

```python
import math
import jax
import jax.numpy as jnp
import numpy as np
from jax import lax

CX = 16
CY = 16
CZ = 128
WIDTH = 5
NX = 64
NY = 64
NZ = 256
N_XI = 4
N_ETA = 4
N_ZETA = 2


def draw_conserved_solution(key, part):
    subkeys = jax.random.split(key, 3)
    density = jnp.exp(jax.random.uniform(subkeys[0], (NX, NY, NZ), jnp.float32, math.log(0.5), math.log(2.0)))
    fluid_speed_vector = jax.random.uniform(subkeys[1], (3, NX, NY, NZ), jnp.float32, -0.6, 0.6)
    thermodynamic_stress_scalar = jax.random.uniform(subkeys[2], (NX, NY, NZ), jnp.float32, 0.5, 1.5)
    momentum_density = density * fluid_speed_vector
    energy = thermodynamic_stress_scalar / 0.4 + 0.5 * jnp.sum(momentum_density * fluid_speed_vector, axis=0)
    return jnp.concatenate([density[None], momentum_density, energy[None]], axis=0)


def draw_metrics(key, part):
    subkeys = jax.random.split(key, 2)
    spread = 0.3
    diagonal = jnp.exp(jax.random.uniform(subkeys[0], (3, 3, NX, NY, NZ), jnp.float32, math.log(0.7), math.log(1.4)))
    offside = jax.random.uniform(subkeys[1], (3, 3, NX, NY, NZ), jnp.float32, -spread, spread)
    identity = jnp.eye(3, dtype=jnp.float32)[:, :, None, None, None] > 0.5
    return jnp.where(identity, diagonal, offside)


def block_levels(key, dims, cuts, least, high):
    factor_of, own = 1.0, jax.random.fold_in(key, 6)
    for dim, shards_of in cuts:
        heights = jnp.exp(jax.random.uniform(jax.random.fold_in(own, dim), (shards_of,), jnp.float32, least / len(cuts), high / len(cuts)))
        factor_of = factor_of * jnp.repeat(heights, dims[dim] // shards_of).reshape([-1 if axis == dim else 1 for axis in range(len(dims))])
    return factor_of


def setup_inputs(seed: int = 0) -> dict:
    arg_keys = jax.random.split(jax.random.key(seed), 4)
    return {
        "conserved_solution": draw_conserved_solution(jax.random.fold_in(arg_keys[3], 71), 0),
        "metrics": draw_metrics(jax.random.fold_in(arg_keys[3], 71), 0),
        "jacobian": jnp.clip(jnp.exp(math.log(1.4) - 0.6931472 * jax.random.uniform(arg_keys[2], (NX, NY, NZ), jnp.float32) ** block_levels(arg_keys[2], (NX, NY, NZ), ((0, 4), (1, 4), (2, 2)), -0.2, 0.2)), 0.7, 1.4),
    }


viscosity = 0.15
conduction = 0.15 * 1.4 / (0.4 * 0.72)
step_duration = 0.08


def banded_solve(system, source):
    extent = system.shape[0]
    lower = np.zeros(extent)
    upper = np.zeros(extent)
    middle = np.array([float(system[index, index]) for index in range(extent)])
    for index in range(1, extent):
        lower[index] = system[index, index - 1]
        upper[index - 1] = system[index - 1, index]
    rights = np.array(source)
    for index in range(1, extent):
        factor = lower[index] / middle[index - 1]
        middle[index] = middle[index] - factor * upper[index - 1]
        rights[index] = rights[index] - factor * rights[index - 1]
    answer = np.zeros(rights.shape)
    answer[extent - 1] = rights[extent - 1] / middle[extent - 1]
    for index in range(extent - 2, -1, -1):
        answer[index] = (rights[index] - upper[index] * answer[index + 1]) / middle[index]
    return answer


def derivative_table(length):
    extent = length + 2 * WIDTH
    system = np.eye(extent)
    source = np.zeros((extent, extent))
    for position in range(2, extent - 2):
        system[position, position - 1] = 1.0 / 3.0
        system[position, position + 1] = 1.0 / 3.0
        source[position, position + 1] = 7.0 / 9.0
        source[position, position - 1] = -7.0 / 9.0
        source[position, position + 2] = 1.0 / 36.0
        source[position, position - 2] = -1.0 / 36.0
    source[1, 2] = 0.5
    source[1, 0] = -0.5
    source[extent - 2, extent - 1] = 0.5
    source[extent - 2, extent - 3] = -0.5
    source[0, 1] = 1.0
    source[0, 0] = -1.0
    source[extent - 1, extent - 1] = 1.0
    source[extent - 1, extent - 2] = -1.0
    return banded_solve(system, source)[WIDTH:WIDTH + length]


def filter_table(length):
    strength = 0.4
    coeffs = [(193.0 + 126.0 * strength) / 256.0, (105.0 + 302.0 * strength) / 256.0,
              15.0 * (2.0 * strength - 1.0) / 64.0, 45.0 * (1.0 - 2.0 * strength) / 512.0,
              5.0 * (2.0 * strength - 1.0) / 256.0, (1.0 - 2.0 * strength) / 512.0]
    extent = length + 2 * WIDTH
    system = np.eye(extent)
    source = np.eye(extent)
    for position in range(5, extent - 5):
        system[position, position - 1] = strength
        system[position, position + 1] = strength
        source[position, position] = coeffs[0]
        for offset in range(1, 6):
            source[position, position + offset] = coeffs[offset] / 2.0
            source[position, position - offset] = coeffs[offset] / 2.0
    return banded_solve(system, source)[WIDTH:WIDTH + length]


def apply_lines(values, matrix, sweep_direction, blocks):
    moved = jnp.moveaxis(values, sweep_direction, -1)
    padded = jnp.concatenate([moved[..., -WIDTH:], moved, moved[..., :WIDTH]], axis=-1)
    length = matrix.shape[0]
    window = np.arange(blocks)[:, None] * length + np.arange(length + 2 * WIDTH)[None, :]
    subdomain_parts = padded[..., window]
    mapped = jnp.einsum('...bl,al->...ba', subdomain_parts, matrix, precision=lax.Precision.HIGHEST)
    return jnp.moveaxis(mapped.reshape(moved.shape), -1, sweep_direction)


def basic_quantities(conserved_solution):
    density = conserved_solution[0]
    fluid_speed_vector = conserved_solution[1:4] / density
    thermodynamic_stress_scalar = 0.4 * (conserved_solution[4] - 0.5 * jnp.sum(conserved_solution[1:4] * fluid_speed_vector, axis=0))
    return fluid_speed_vector, thermodynamic_stress_scalar, thermodynamic_stress_scalar / density


def fluxes(conserved_solution, fluid_speed_vector, thermodynamic_stress_scalar, slopes, metrics, jacobian):
    physical = [[jacobian * (metrics[0, column] * slopes[0][member] + metrics[1, column] * slopes[1][member]
                             + metrics[2, column] * slopes[2][member]) for column in range(3)] for member in range(4)]
    spread = physical[0][0] + physical[1][1] + physical[2][2]
    totals = []
    for column in range(3):
        stress = [viscosity * (physical[member][column] + physical[column][member]) for member in range(3)]
        stress[column] = stress[column] - (2.0 / 3.0) * viscosity * spread
        subdomain_parts = [conserved_solution[1 + column]]
        for member in range(3):
            carried = conserved_solution[1 + member] * fluid_speed_vector[column] - stress[member]
            if member == column:
                carried = carried + thermodynamic_stress_scalar
            subdomain_parts.append(carried)
        worked = fluid_speed_vector[0] * stress[0] + fluid_speed_vector[1] * stress[1] + fluid_speed_vector[2] * stress[2]
        subdomain_parts.append((conserved_solution[4] + thermodynamic_stress_scalar) * fluid_speed_vector[column] - worked - conduction * physical[3][column])
        totals.append(jnp.stack(subdomain_parts))
    return [metrics[direction, 0] * totals[0] + metrics[direction, 1] * totals[1] + metrics[direction, 2] * totals[2]
            for direction in range(3)]


def reference(conserved_solution, metrics, jacobian):
    blocks = (N_XI, N_ETA, N_ZETA)
    lengths = (CX, CY, CZ)
    derive = [jnp.asarray(derivative_table(length), dtype=jnp.float32) for length in lengths]
    smooth = [jnp.asarray(filter_table(length), dtype=jnp.float32) for length in lengths]
    fluid_speed_vector, thermodynamic_stress_scalar, thermal_level = basic_quantities(conserved_solution)
    basic_quantity = jnp.concatenate([fluid_speed_vector, thermal_level[None]], axis=0)
    slopes = [apply_lines(basic_quantity, derive[direction], direction + 1, blocks[direction]) for direction in range(3)]
    contra = fluxes(conserved_solution, fluid_speed_vector, thermodynamic_stress_scalar, slopes, metrics, jacobian)
    divergence = apply_lines(contra[0], derive[0], 1, blocks[0])
    divergence = divergence + apply_lines(contra[1], derive[1], 2, blocks[1])
    divergence = divergence + apply_lines(contra[2], derive[2], 3, blocks[2])
    sectioned = conserved_solution - step_duration * jacobian * divergence
    result = apply_lines(sectioned, smooth[0], 1, blocks[0])
    result = apply_lines(result, smooth[1], 2, blocks[1])
    return apply_lines(result, smooth[2], 3, blocks[2])
```

```python
import functools

import jax
import jax.numpy as jnp
import numpy as np
from jax import lax
from jax.experimental import pallas as pl
from jax.experimental.pallas import tpu as pltpu
from jax.sharding import PartitionSpec as P

WIDTH = 5
LANES = 128
TILE = 8

viscosity = 0.15
conduction = 0.15 * 1.4 / (0.4 * 0.72)
step_duration = 0.08


def derivative_system(length):
    extent = length + 2 * WIDTH
    system = np.eye(extent)
    source = np.zeros((extent, extent))
    for position in range(2, extent - 2):
        system[position, position - 1] = 1.0 / 3.0
        system[position, position + 1] = 1.0 / 3.0
        source[position, position + 1] = 7.0 / 9.0
        source[position, position - 1] = -7.0 / 9.0
        source[position, position + 2] = 1.0 / 36.0
        source[position, position - 2] = -1.0 / 36.0
    source[1, 2] = 0.5
    source[1, 0] = -0.5
    source[extent - 2, extent - 1] = 0.5
    source[extent - 2, extent - 3] = -0.5
    source[0, 1] = 1.0
    source[0, 0] = -1.0
    source[extent - 1, extent - 1] = 1.0
    source[extent - 1, extent - 2] = -1.0
    return system, source


def filter_coefficients():
    strength = 0.4
    return [
        (193.0 + 126.0 * strength) / 256.0,
        (105.0 + 302.0 * strength) / 256.0,
        15.0 * (2.0 * strength - 1.0) / 64.0,
        45.0 * (1.0 - 2.0 * strength) / 512.0,
        5.0 * (2.0 * strength - 1.0) / 256.0,
        (1.0 - 2.0 * strength) / 512.0,
    ]


def filter_system(length):
    strength = 0.4
    coeffs = filter_coefficients()
    extent = length + 2 * WIDTH
    system = np.eye(extent)
    source = np.eye(extent)
    for position in range(5, extent - 5):
        system[position, position - 1] = strength
        system[position, position + 1] = strength
        source[position, position] = coeffs[0]
        for offset in range(1, 6):
            source[position, position + offset] = coeffs[offset] / 2.0
            source[position, position - offset] = coeffs[offset] / 2.0
    return system, source


def own_rows(system, source, length):
    return np.linalg.solve(system, source)[WIDTH : WIDTH + length]


def derivative_parts(length):
    system, source = derivative_system(length)
    halo = np.linalg.solve(system[:WIDTH, :WIDTH], source[:WIDTH])
    row = source[WIDTH] - system[WIDTH, WIDTH - 1] * halo[WIDTH - 1]
    pivots = [1.0]
    for position in range(3, WIDTH + length):
        pivots.append(1.0 - 1.0 / 9.0 / pivots[-1])
    return pivots[WIDTH - 2 :], row[:WIDTH], row[WIDTH : WIDTH + 3]


def split_weights(table):
    table = np.asarray(table, np.float32)
    high = table.astype(jnp.bfloat16)
    low = (table - high.astype(np.float32)).astype(jnp.bfloat16)
    return np.block([[high, low], [high, np.zeros_like(low)]]).astype(jnp.bfloat16)


def pad_rows(table):
    return np.concatenate([table, np.zeros((LANES - table.shape[0], table.shape[1]))], axis=0)


def pad_columns(table):
    return np.concatenate([table, np.zeros((table.shape[0], LANES - table.shape[1]))], axis=1)


def zeta_tables(length):
    system, source = derivative_system(length)
    table = own_rows(system, source, length)
    _, edge, _ = derivative_parts(length)
    inverse = np.linalg.inv(system)
    extent = length + 2 * WIDTH
    sums = np.zeros((length, 4))
    sums[length - WIDTH :, 0] = edge
    sums[length - 1, 1] = 1.0
    sums[:WIDTH, 2] = -edge[::-1]
    sums[0, 3] = 1.0
    own = slice(WIDTH, WIDTH + length)
    back = np.stack(
        [
            inverse[own, WIDTH],
            -1.0 / 36.0 * inverse[own, WIDTH + 1],
            inverse[own, extent - WIDTH - 1],
            1.0 / 36.0 * inverse[own, extent - WIDTH - 2],
        ]
    )
    smooth = own_rows(*filter_system(length), length)
    ends = np.concatenate([smooth[:, :WIDTH], smooth[:, WIDTH + length :]], axis=1)
    return {
        "derive": split_weights(table[:, own].T),
        "sums": split_weights(pad_columns(sums)),
        "back": split_weights(pad_rows(back)),
        "smooth": split_weights(smooth[:, own].T),
        "ends": split_weights(pad_rows(ends.T)),
    }


def twisted_solve(rights, pivots, off):
    count = len(rights)
    half = count // 2
    low = [rights[0]]
    high = [rights[count - 1]]
    for step in range(1, half):
        factor = off / pivots[step - 1]
        low.append(rights[step] - factor * low[-1])
        high.append(rights[count - 1 - step] - factor * high[-1])
    middle = pivots[half - 1]
    det = middle * middle - off * off
    first, second = low[-1], high[-1]
    answer = [None] * count
    answer[half - 1] = (middle / det) * first - (off / det) * second
    answer[half] = (middle / det) * second - (off / det) * first
    for step in range(half - 2, -1, -1):
        scale = 1.0 / pivots[step]
        factor = off / pivots[step]
        answer[step] = scale * low[step] - factor * answer[step + 1]
        answer[count - 1 - step] = scale * high[step] - factor * answer[count - 2 - step]
    return answer


def derive_line(cells, below, above):
    count = len(cells)
    pivots, _, edge = derivative_parts(count)
    near, far = 7.0 / 9.0, 1.0 / 36.0
    rights = [None] * count
    rights[0] = below[0] + edge[0] * cells[0] + edge[1] * cells[1] + edge[2] * cells[2]
    rights[1] = near * (cells[2] - cells[0]) + far * (cells[3] - below[1])
    for step in range(2, count - 2):
        rights[step] = near * (cells[step + 1] - cells[step - 1]) + far * (
            cells[step + 2] - cells[step - 2]
        )
    rights[count - 2] = near * (cells[count - 1] - cells[count - 3]) + far * (
        above[1] - cells[count - 4]
    )
    rights[count - 1] = above[0] - (
        edge[0] * cells[count - 1] + edge[1] * cells[count - 2] + edge[2] * cells[count - 3]
    )
    return twisted_solve(rights, pivots, 1.0 / 3.0)


def end_sums(cells):
    _, edge, _ = derivative_parts(16)
    total = edge[WIDTH - 1] * cells[0]
    for step in range(1, WIDTH):
        total = total + edge[WIDTH - 1 - step] * cells[step]
    return total, cells[0]


def smooth_line(cells):
    count = len(cells) - 2 * WIDTH
    coeffs = filter_coefficients()
    pivots = [1.0]
    for _ in range(count):
        pivots.append(1.0 - 0.16 / pivots[-1])
    rights = []
    for step in range(WIDTH, WIDTH + count):
        total = coeffs[0] * cells[step]
        for offset in range(1, WIDTH + 1):
            total = total + (0.5 * coeffs[offset]) * (cells[step + offset] + cells[step - offset])
        rights.append(total)
    rights[0] = rights[0] - 0.4 * cells[WIDTH - 1]
    rights[-1] = rights[-1] - 0.4 * cells[WIDTH + count]
    return twisted_solve(rights, pivots, 0.4)


def split_values(values):
    high = values.astype(jnp.bfloat16)
    low = (values - high.astype(jnp.float32)).astype(jnp.bfloat16)
    return jnp.concatenate([high, low], axis=1)


def lane_product(values, weights):
    both = jnp.dot(split_values(values), weights, preferred_element_type=jnp.float32)
    return both[:, :LANES] + both[:, LANES:]


class Grid:
    def __init__(self, nx, ny):
        self.nx, self.ny, self.rows = nx, ny, nx * ny
        self.eta_groups = ny // TILE
        self.xi_groups = nx // TILE

    def xi_tile(self, position, group):
        return pl.ds(position * self.ny + group * TILE, TILE)

    def eta_tile(self, position, group):
        return pl.ds(position + group * TILE * self.ny, TILE, stride=self.ny)


def group_rows(group):
    return pl.ds(group * TILE, TILE)


def odd(axis):
    return lax.rem(lax.axis_index(axis), 2) == 1


def send_sums(read, groups, count, flag, first_ref, second_ref, field):
    for group in range(groups):
        top = end_sums([read(count - 1 - step, group) for step in range(WIDTH)])
        low = end_sums([read(step, group) for step in range(WIDTH)])
        low = (-low[0], low[1])
        for part in range(2):
            first_ref[2 * field + part, group_rows(group), :] = jnp.where(flag, low[part], top[part])
            second_ref[2 * field + part, group_rows(group), :] = jnp.where(flag, top[part], low[part])


def take_sums(first_ref, second_ref, flag, field, group):
    below, above = [], []
    for part in range(2):
        first = first_ref[2 * field + part, group_rows(group), :]
        second = second_ref[2 * field + part, group_rows(group), :]
        below.append(jnp.where(flag, first, second))
        above.append(jnp.where(flag, second, first))
    return below, above


def pack_sums(values, weights, grid):
    sums = lane_product(values, weights)
    packed = None
    for group in range(grid.rows // TILE):
        part = sums[group * TILE : (group + 1) * TILE]
        if group:
            part = pltpu.roll(part, 4 * group, axis=1)
        packed = part if packed is None else packed + part
    return packed


def unpack_sums(below, above, grid):
    lane = lax.broadcasted_iota(jnp.int32, below.shape, 1)
    packed = jnp.where(lax.rem(lane, 4) < 2, below, above)
    parts = [packed]
    for group in range(1, grid.rows // TILE):
        parts.append(pltpu.roll(packed, LANES - 4 * group, axis=1))
    return jnp.concatenate(parts, axis=0)


def primitive_kernel(
    grid, u_ref, sums_ref, prim_ref, eta_first, eta_second, xi_first, xi_second, zeta_ref
):
    step = 4 * TILE

    def body(index, carry):
        rows = pl.ds(pl.multiple_of(index * step, step), step)
        inverse = 1.0 / u_ref[0, rows, :]
        work = None
        for c in range(3):
            momentum = u_ref[1 + c, rows, :]
            speed = momentum * inverse
            prim_ref[c, rows, :] = speed
            work = momentum * speed if work is None else work + momentum * speed
        pressure = 0.4 * (u_ref[4, rows, :] - 0.5 * work)
        prim_ref[3, rows, :] = pressure * inverse
        return carry

    lax.fori_loop(0, grid.rows // step, body, 0)
    for field in range(4):
        send_sums(
            lambda position, group: prim_ref[field, grid.eta_tile(position, group), :],
            grid.xi_groups, grid.ny, odd("eta"), eta_first, eta_second, field,
        )
        send_sums(
            lambda position, group: prim_ref[field, grid.xi_tile(position, group), :],
            grid.eta_groups, grid.nx, odd("xi"), xi_first, xi_second, field,
        )
        zeta_ref[field] = pack_sums(prim_ref[field], sums_ref[...], grid)


def flux_kernel(
    grid,
    u_ref, prim_ref, metrics_ref, jacobian_ref,
    eta_a, eta_b, xi_a, xi_b, zeta_below, zeta_above,
    derive_ref, back_ref, sums_ref,
    contra_ref, eta_first, eta_second, xi_first, xi_second, zeta_ref,
    slope_ref,
):
    for field in range(4):
        for group in range(grid.eta_groups):
            below, above = take_sums(xi_a, xi_b, odd("xi"), field, group)
            cells = [prim_ref[field, grid.xi_tile(i, group), :] for i in range(grid.nx)]
            for i, value in enumerate(derive_line(cells, below, above)):
                slope_ref[0, field, grid.xi_tile(i, group), :] = value
        for group in range(grid.xi_groups):
            below, above = take_sums(eta_a, eta_b, odd("eta"), field, group)
            cells = [prim_ref[field, grid.eta_tile(i, group), :] for i in range(grid.ny)]
            for i, value in enumerate(derive_line(cells, below, above)):
                slope_ref[1, field, grid.eta_tile(i, group), :] = value
        halo = unpack_sums(zeta_below[field], zeta_above[field], grid)
        slope_ref[2, field] = lane_product(prim_ref[field], derive_ref[...]) + lane_product(
            halo, back_ref[...]
        )

    step = TILE

    def body(index, carry):
        rows = pl.ds(pl.multiple_of(index * step, step), step)
        u = [u_ref[c, rows, :] for c in range(5)]
        speed = [prim_ref[c, rows, :] for c in range(3)]
        pressure = prim_ref[3, rows, :] * u[0]
        jacobian = jacobian_ref[rows, :]
        metrics = [[metrics_ref[3 * k + j, rows, :] for j in range(3)] for k in range(3)]
        physical = []
        for c in range(4):
            slopes = [slope_ref[k, c, rows, :] for k in range(3)]
            physical.append(
                [
                    jacobian
                    * (
                        metrics[0][j] * slopes[0] + metrics[1][j] * slopes[1] + metrics[2][j] * slopes[2]
                    )
                    for j in range(3)
                ]
            )
        spread = (2.0 / 3.0 * viscosity) * (physical[0][0] + physical[1][1] + physical[2][2])
        stress = [[None] * 3 for _ in range(3)]
        for c in range(3):
            stress[c][c] = (2.0 * viscosity) * physical[c][c] - spread
            for j in range(c):
                stress[c][j] = stress[j][c] = viscosity * (physical[c][j] + physical[j][c])
        total = u[4] + pressure
        fluxes = []
        for j in range(3):
            parts = [u[1 + j]]
            for c in range(3):
                carried = u[1 + c] * speed[j] - stress[c][j]
                if c == j:
                    carried = carried + pressure
                parts.append(carried)
            worked = speed[0] * stress[0][j] + speed[1] * stress[1][j] + speed[2] * stress[2][j]
            parts.append(total * speed[j] - worked - conduction * physical[3][j])
            fluxes.append(parts)
        for k in range(3):
            for f in range(5):
                contra_ref[k, f, rows, :] = (
                    metrics[k][0] * fluxes[0][f]
                    + metrics[k][1] * fluxes[1][f]
                    + metrics[k][2] * fluxes[2][f]
                )
        return carry

    lax.fori_loop(0, grid.rows // step, body, 0)
    for field in range(5):
        send_sums(
            lambda position, group: contra_ref[1, field, grid.eta_tile(position, group), :],
            grid.xi_groups, grid.ny, odd("eta"), eta_first, eta_second, field,
        )
        send_sums(
            lambda position, group: contra_ref[0, field, grid.xi_tile(position, group), :],
            grid.eta_groups, grid.nx, odd("xi"), xi_first, xi_second, field,
        )
        zeta_ref[field] = pack_sums(contra_ref[2, field], sums_ref[...], grid)


def step_kernel(
    grid,
    u_ref, jacobian_ref, contra_ref,
    eta_a, eta_b, xi_a, xi_b, zeta_below, zeta_above,
    derive_ref, back_ref,
    state_ref, eta_first, eta_second,
):
    flag = odd("eta")
    for field in range(5):
        halo = unpack_sums(zeta_below[field], zeta_above[field], grid)
        state_ref[field] = lane_product(contra_ref[2, field], derive_ref[...]) + lane_product(
            halo, back_ref[...]
        )
        for group in range(grid.xi_groups):
            below, above = take_sums(eta_a, eta_b, flag, field, group)
            cells = [contra_ref[1, field, grid.eta_tile(i, group), :] for i in range(grid.ny)]
            for i, value in enumerate(derive_line(cells, below, above)):
                rows = grid.eta_tile(i, group)
                state_ref[field, rows, :] = state_ref[field, rows, :] + value
        for group in range(grid.eta_groups):
            below, above = take_sums(xi_a, xi_b, odd("xi"), field, group)
            cells = [contra_ref[0, field, grid.xi_tile(i, group), :] for i in range(grid.nx)]
            for i, value in enumerate(derive_line(cells, below, above)):
                rows = grid.xi_tile(i, group)
                total = state_ref[field, rows, :] + value
                state_ref[field, rows, :] = u_ref[field, rows, :] - (
                    step_duration * jacobian_ref[rows, :]
                ) * total
        send_cells(
            lambda position, group: state_ref[field, grid.eta_tile(position, group), :],
            grid.xi_groups, grid.ny, flag, eta_first, eta_second, field,
        )


def send_cells(read, groups, count, flag, first_ref, second_ref, field):
    for group in range(groups):
        for step in range(WIDTH):
            low = read(step, group)
            top = read(count - 1 - step, group)
            index = WIDTH * field + step
            first_ref[index, group_rows(group), :] = jnp.where(flag, low, top)
            second_ref[index, group_rows(group), :] = jnp.where(flag, top, low)


def take_cells(first_ref, second_ref, flag, field, group):
    below, above = [], []
    for step in range(WIDTH):
        first = first_ref[WIDTH * field + step, group_rows(group), :]
        second = second_ref[WIDTH * field + step, group_rows(group), :]
        below.insert(0, jnp.where(flag, first, second))
        above.append(jnp.where(flag, second, first))
    return below, above


def eta_filter_kernel(grid, state_ref, eta_a, eta_b, result_ref, xi_first, xi_second):
    flag = odd("eta")
    for field in range(5):
        for group in range(grid.xi_groups):
            below, above = take_cells(eta_a, eta_b, flag, field, group)
            cells = [state_ref[field, grid.eta_tile(i, group), :] for i in range(grid.ny)]
            for i, value in enumerate(smooth_line(below + cells + above)):
                result_ref[field, grid.eta_tile(i, group), :] = value
        send_cells(
            lambda position, group: result_ref[field, grid.xi_tile(position, group), :],
            grid.eta_groups, grid.nx, odd("xi"), xi_first, xi_second, field,
        )


PACKED = 12


def xi_filter_kernel(grid, state_ref, xi_a, xi_b, result_ref, zeta_ref):
    flag = odd("xi")
    tiles = grid.rows // TILE
    for field in range(5):
        for group in range(grid.eta_groups):
            below, above = take_cells(xi_a, xi_b, flag, field, group)
            cells = [state_ref[field, grid.xi_tile(i, group), :] for i in range(grid.nx)]
            for i, value in enumerate(smooth_line(below + cells + above)):
                result_ref[field, grid.xi_tile(i, group), :] = value
        lane = lax.broadcasted_iota(jnp.int32, (TILE, LANES), 1)
        for start in range(0, tiles, PACKED):
            packed = None
            for slot in range(min(PACKED, tiles - start)):
                part = result_ref[field, group_rows(start + slot), :]
                part = pltpu.roll(part, WIDTH + 2 * WIDTH * slot, axis=1)
                packed = part if packed is None else jnp.where(lane >= 2 * WIDTH * slot, part, packed)
            zeta_ref[field, group_rows(start // PACKED), :] = packed


def zeta_filter_kernel(grid, state_ref, below_ref, above_ref, smooth_ref, ends_ref, result_ref):
    tiles = grid.rows // TILE
    lane = lax.broadcasted_iota(jnp.int32, (TILE, LANES), 1)
    for field in range(5):
        parts = []
        for start in range(0, tiles, PACKED):
            rows = group_rows(start // PACKED)
            packed = jnp.where(
                lax.rem(lane, 2 * WIDTH) < WIDTH, below_ref[field, rows, :], above_ref[field, rows, :]
            )
            for slot in range(min(PACKED, tiles - start)):
                parts.append(pltpu.roll(packed, LANES - 2 * WIDTH * slot, axis=1) if slot else packed)
        halo = jnp.concatenate(parts, axis=0)
        result_ref[field] = lane_product(state_ref[field], smooth_ref[...]) + lane_product(
            halo, ends_ref[...]
        )


def pair_swap(value, axis, parity):
    count = lax.axis_size(axis)
    pairs = []
    for index in range(count):
        step = 1 if index % 2 == parity else -1
        pairs.append((index, (index + step) % count))
    return lax.ppermute(value, axis, pairs)


def ring_swap(value, axis):
    count = lax.axis_size(axis)
    if count == 2:
        other = lax.ppermute(value, axis, [(0, 1), (1, 0)])
        return other, other
    up = [(index, (index + 1) % count) for index in range(count)]
    down = [(index, (index - 1) % count) for index in range(count)]
    return lax.ppermute(value, axis, up), lax.ppermute(value, axis, down)


def call(kernel, outs, *operands, scratch=()):
    shapes = [jax.ShapeDtypeStruct(shape, jnp.float32) for shape in outs]
    return pl.pallas_call(
        kernel,
        out_shape=shapes,
        scratch_shapes=[pltpu.VMEM(shape, jnp.float32) for shape in scratch],
        compiler_params=pltpu.CompilerParams(vmem_limit_bytes=20 * 2**20),
    )(*operands)


def local(conserved_solution, metrics, jacobian):
    _, nx, ny, nz = conserved_solution.shape
    grid = Grid(nx, ny)
    rows = grid.rows
    u = conserved_solution.reshape(5, rows, nz)
    metrics = metrics.reshape(9, rows, nz)
    jacobian = jacobian.reshape(rows, nz)
    tables = {name: jnp.asarray(table) for name, table in zeta_tables(nz).items()}
    packs = -(-(rows // TILE) // PACKED)

    def exchange(eta_first, eta_second, xi_first, xi_second, zeta):
        eta_b = pair_swap(eta_second, "eta", 1)
        eta_a = pair_swap(eta_first, "eta", 0)
        xi_b = pair_swap(xi_second, "xi", 1)
        below, above = ring_swap(zeta, "zeta")
        xi_a = pair_swap(xi_first, "xi", 0)
        return eta_a, eta_b, xi_a, xi_b, below, above

    def sums_shapes(fields):
        return [(2 * fields, nx, nz)] * 2 + [(2 * fields, ny, nz)] * 2 + [(fields, TILE, LANES)]

    prim, *sends = call(
        functools.partial(primitive_kernel, grid),
        [(4, rows, nz)] + sums_shapes(4),
        u, tables["sums"],
    )
    got = exchange(*sends)
    contra, *sends = call(
        functools.partial(flux_kernel, grid),
        [(3, 5, rows, nz)] + sums_shapes(5),
        u, prim, metrics, jacobian, *got, tables["derive"], tables["back"], tables["sums"],
        scratch=[(3, 4, rows, nz)],
    )
    got = exchange(*sends)
    state, eta_first, eta_second = call(
        functools.partial(step_kernel, grid),
        [(5, rows, nz)] + [(5 * WIDTH, nx, nz)] * 2,
        u, jacobian, contra, *got, tables["derive"], tables["back"],
    )
    eta_b = pair_swap(eta_second, "eta", 1)
    eta_a = pair_swap(eta_first, "eta", 0)
    state, xi_first, xi_second = call(
        functools.partial(eta_filter_kernel, grid),
        [(5, rows, nz)] + [(5 * WIDTH, ny, nz)] * 2,
        state, eta_a, eta_b,
    )
    xi_b = pair_swap(xi_second, "xi", 1)
    xi_a = pair_swap(xi_first, "xi", 0)
    state, zeta = call(
        functools.partial(xi_filter_kernel, grid),
        [(5, rows, nz), (5, packs * TILE, LANES)],
        state, xi_a, xi_b,
    )
    below, above = ring_swap(zeta, "zeta")
    (result,) = call(
        functools.partial(zeta_filter_kernel, grid),
        [(5, rows, nz)],
        state, below, above, tables["smooth"], tables["ends"],
    )
    return result.reshape(5, nx, ny, nz)


def solution(mesh):
    in_specs = (
        P(None, "xi", "eta", "zeta"),
        P(None, None, "xi", "eta", "zeta"),
        P("xi", "eta", "zeta"),
    )
    out_specs = P(None, "xi", "eta", "zeta")
    return jax.shard_map(local, mesh=mesh, in_specs=in_specs, out_specs=out_specs, check_vma=False)
```

```python
import functools

import jax
import jax.numpy as jnp
import numpy as np
from jax import lax
from jax.experimental import pallas as pl
from jax.experimental.pallas import tpu as pltpu
from jax.sharding import PartitionSpec as P

WIDTH = 5
LANES = 128
TILE = 8

viscosity = 0.15
conduction = 0.15 * 1.4 / (0.4 * 0.72)
step_duration = 0.08


def derivative_system(length):
    extent = length + 2 * WIDTH
    system = np.eye(extent)
    source = np.zeros((extent, extent))
    for position in range(2, extent - 2):
        system[position, position - 1] = 1.0 / 3.0
        system[position, position + 1] = 1.0 / 3.0
        source[position, position + 1] = 7.0 / 9.0
        source[position, position - 1] = -7.0 / 9.0
        source[position, position + 2] = 1.0 / 36.0
        source[position, position - 2] = -1.0 / 36.0
    source[1, 2] = 0.5
    source[1, 0] = -0.5
    source[extent - 2, extent - 1] = 0.5
    source[extent - 2, extent - 3] = -0.5
    source[0, 1] = 1.0
    source[0, 0] = -1.0
    source[extent - 1, extent - 1] = 1.0
    source[extent - 1, extent - 2] = -1.0
    return system, source


def filter_coefficients():
    strength = 0.4
    return [
        (193.0 + 126.0 * strength) / 256.0,
        (105.0 + 302.0 * strength) / 256.0,
        15.0 * (2.0 * strength - 1.0) / 64.0,
        45.0 * (1.0 - 2.0 * strength) / 512.0,
        5.0 * (2.0 * strength - 1.0) / 256.0,
        (1.0 - 2.0 * strength) / 512.0,
    ]


def filter_system(length):
    strength = 0.4
    coeffs = filter_coefficients()
    extent = length + 2 * WIDTH
    system = np.eye(extent)
    source = np.eye(extent)
    for position in range(5, extent - 5):
        system[position, position - 1] = strength
        system[position, position + 1] = strength
        source[position, position] = coeffs[0]
        for offset in range(1, 6):
            source[position, position + offset] = coeffs[offset] / 2.0
            source[position, position - offset] = coeffs[offset] / 2.0
    return system, source


def own_rows(system, source, length):
    return np.linalg.solve(system, source)[WIDTH : WIDTH + length]


def derivative_parts(length):
    system, source = derivative_system(length)
    halo = np.linalg.solve(system[:WIDTH, :WIDTH], source[:WIDTH])
    row = source[WIDTH] - system[WIDTH, WIDTH - 1] * halo[WIDTH - 1]
    pivots = [1.0]
    for position in range(3, WIDTH + length):
        pivots.append(1.0 - 1.0 / 9.0 / pivots[-1])
    return pivots[WIDTH - 2 :], row[:WIDTH], row[WIDTH : WIDTH + 3]


def split_weights(table):
    table = np.asarray(table, np.float32)
    high = table.astype(jnp.bfloat16)
    low = (table - high.astype(np.float32)).astype(jnp.bfloat16)
    return np.block([[high, low], [high, np.zeros_like(low)]]).astype(jnp.bfloat16)


def pad_rows(table):
    return np.concatenate([table, np.zeros((LANES - table.shape[0], table.shape[1]))], axis=0)


def pad_columns(table):
    return np.concatenate([table, np.zeros((table.shape[0], LANES - table.shape[1]))], axis=1)


def zeta_tables(length):
    system, source = derivative_system(length)
    table = own_rows(system, source, length)
    _, edge, _ = derivative_parts(length)
    inverse = np.linalg.inv(system)
    extent = length + 2 * WIDTH
    sums = np.zeros((length, 4))
    sums[length - WIDTH :, 0] = edge
    sums[length - 1, 1] = 1.0
    sums[:WIDTH, 2] = -edge[::-1]
    sums[0, 3] = 1.0
    own = slice(WIDTH, WIDTH + length)
    back = np.stack(
        [
            inverse[own, WIDTH],
            -1.0 / 36.0 * inverse[own, WIDTH + 1],
            inverse[own, extent - WIDTH - 1],
            1.0 / 36.0 * inverse[own, extent - WIDTH - 2],
        ]
    )
    smooth = own_rows(*filter_system(length), length)
    ends = np.concatenate([smooth[:, :WIDTH], smooth[:, WIDTH + length :]], axis=1)
    return {
        "derive": split_weights(table[:, own].T),
        "sums": split_weights(pad_columns(sums)),
        "back": split_weights(pad_rows(back)),
        "smooth": split_weights(smooth[:, own].T),
        "ends": split_weights(pad_rows(ends.T)),
    }


def twisted_solve(rights, pivots, off):
    count = len(rights)
    half = count // 2
    low = [rights[0]]
    high = [rights[count - 1]]
    for step in range(1, half):
        factor = off / pivots[step - 1]
        low.append(rights[step] - factor * low[-1])
        high.append(rights[count - 1 - step] - factor * high[-1])
    middle = pivots[half - 1]
    det = middle * middle - off * off
    first, second = low[-1], high[-1]
    answer = [None] * count
    answer[half - 1] = (middle / det) * first - (off / det) * second
    answer[half] = (middle / det) * second - (off / det) * first
    for step in range(half - 2, -1, -1):
        scale = 1.0 / pivots[step]
        factor = off / pivots[step]
        answer[step] = scale * low[step] - factor * answer[step + 1]
        answer[count - 1 - step] = scale * high[step] - factor * answer[count - 2 - step]
    return answer


def derive_line(cells, below, above):
    count = len(cells)
    pivots, _, edge = derivative_parts(count)
    near, far = 7.0 / 9.0, 1.0 / 36.0
    rights = [None] * count
    rights[0] = below[0] + edge[0] * cells[0] + edge[1] * cells[1] + edge[2] * cells[2]
    rights[1] = near * (cells[2] - cells[0]) + far * (cells[3] - below[1])
    for step in range(2, count - 2):
        rights[step] = near * (cells[step + 1] - cells[step - 1]) + far * (
            cells[step + 2] - cells[step - 2]
        )
    rights[count - 2] = near * (cells[count - 1] - cells[count - 3]) + far * (
        above[1] - cells[count - 4]
    )
    rights[count - 1] = above[0] - (
        edge[0] * cells[count - 1] + edge[1] * cells[count - 2] + edge[2] * cells[count - 3]
    )
    return twisted_solve(rights, pivots, 1.0 / 3.0)


def end_sums(cells):
    _, edge, _ = derivative_parts(16)
    total = edge[WIDTH - 1] * cells[0]
    for step in range(1, WIDTH):
        total = total + edge[WIDTH - 1 - step] * cells[step]
    return total, cells[0]


def smooth_line(cells):
    count = len(cells) - 2 * WIDTH
    coeffs = filter_coefficients()
    pivots = [1.0]
    for _ in range(count):
        pivots.append(1.0 - 0.16 / pivots[-1])
    rights = []
    for step in range(WIDTH, WIDTH + count):
        total = coeffs[0] * cells[step]
        for offset in range(1, WIDTH + 1):
            total = total + (0.5 * coeffs[offset]) * (cells[step + offset] + cells[step - offset])
        rights.append(total)
    rights[0] = rights[0] - 0.4 * cells[WIDTH - 1]
    rights[-1] = rights[-1] - 0.4 * cells[WIDTH + count]
    return twisted_solve(rights, pivots, 0.4)


def split_values(values):
    high = values.astype(jnp.bfloat16)
    low = (values - high.astype(jnp.float32)).astype(jnp.bfloat16)
    return jnp.concatenate([high, low], axis=1)


def lane_product(values, weights):
    both = jnp.dot(split_values(values), weights, preferred_element_type=jnp.float32)
    return both[:, :LANES] + both[:, LANES:]


class Grid:
    def __init__(self, nx, ny):
        self.nx, self.ny, self.rows = nx, ny, nx * ny
        self.eta_groups = ny // TILE
        self.xi_groups = nx // TILE

    def xi_tile(self, position, group):
        return pl.ds(position * self.ny + group * TILE, TILE)

    def eta_tile(self, position, group):
        return pl.ds(position + group * TILE * self.ny, TILE, stride=self.ny)


def group_rows(group):
    return pl.ds(group * TILE, TILE)


def odd(axis):
    return lax.rem(lax.axis_index(axis), 2) == 1


def send_sums(read, groups, count, flag, first_ref, second_ref, field):
    for group in range(groups):
        top = end_sums([read(count - 1 - step, group) for step in range(WIDTH)])
        low = end_sums([read(step, group) for step in range(WIDTH)])
        low = (-low[0], low[1])
        for part in range(2):
            first_ref[2 * field + part, group_rows(group), :] = jnp.where(flag, low[part], top[part])
            second_ref[2 * field + part, group_rows(group), :] = jnp.where(flag, top[part], low[part])


def take_sums(first_ref, second_ref, flag, field, group):
    below, above = [], []
    for part in range(2):
        first = first_ref[2 * field + part, group_rows(group), :]
        second = second_ref[2 * field + part, group_rows(group), :]
        below.append(jnp.where(flag, first, second))
        above.append(jnp.where(flag, second, first))
    return below, above


def pack_sums(values, weights, grid):
    sums = lane_product(values, weights)
    packed = None
    for group in range(grid.rows // TILE):
        part = sums[group * TILE : (group + 1) * TILE]
        if group:
            part = pltpu.roll(part, 4 * group, axis=1)
        packed = part if packed is None else packed + part
    return packed


def unpack_sums(below, above, grid):
    lane = lax.broadcasted_iota(jnp.int32, below.shape, 1)
    packed = jnp.where(lax.rem(lane, 4) < 2, below, above)
    parts = [packed]
    for group in range(1, grid.rows // TILE):
        parts.append(pltpu.roll(packed, LANES - 4 * group, axis=1))
    return jnp.concatenate(parts, axis=0)


def primitive_kernel(
    grid,
    u_hbm, sums_hbm,
    u_ref, sums_ref, prim_ref, eta_first, eta_second, xi_first, xi_second, zeta_ref,
    sums_sem, u_sems,
):
    chunks = u_sems.shape[0]
    step = grid.rows // chunks
    copies = []
    for index in range(chunks):
        rows = pl.ds(index * step, step)
        copy = pltpu.make_async_copy(u_hbm.at[:, rows, :], u_ref.at[:, rows, :], u_sems.at[index])
        copy.start()
        copies.append(copy)
    weights = pltpu.make_async_copy(sums_hbm, sums_ref, sums_sem)
    weights.start()
    for index in range(chunks):
        copies[index].wait()
        rows = pl.ds(index * step, step)
        inverse = 1.0 / u_ref[0, rows, :]
        work = None
        for c in range(3):
            momentum = u_ref[1 + c, rows, :]
            speed = momentum * inverse
            prim_ref[c, rows, :] = speed
            work = momentum * speed if work is None else work + momentum * speed
        pressure = 0.4 * (u_ref[4, rows, :] - 0.5 * work)
        prim_ref[3, rows, :] = pressure * inverse
    for field in range(4):
        send_sums(
            lambda position, group: prim_ref[field, grid.eta_tile(position, group), :],
            grid.xi_groups, grid.ny, odd("eta"), eta_first, eta_second, field,
        )
        send_sums(
            lambda position, group: prim_ref[field, grid.xi_tile(position, group), :],
            grid.eta_groups, grid.nx, odd("xi"), xi_first, xi_second, field,
        )
    weights.wait()
    for field in range(4):
        zeta_ref[field] = pack_sums(prim_ref[field], sums_ref[...], grid)


def fetch_kernel(count, *refs):
    sources, results, sems = refs[:count], refs[count + 1 : 2 * count + 1], refs[-1]
    copies = [
        pltpu.make_async_copy(source, result, sems.at[index])
        for index, (source, result) in enumerate(zip(sources, results))
    ]
    for copy in copies:
        copy.start()
    for copy in copies:
        copy.wait()


def slope_kernel(grid, prim_ref, eta_a, eta_b, xi_a, xi_b, derive_ref, slope_ref):
    for field in range(4):
        for group in range(grid.eta_groups):
            below, above = take_sums(xi_a, xi_b, odd("xi"), field, group)
            cells = [prim_ref[field, grid.xi_tile(i, group), :] for i in range(grid.nx)]
            for i, value in enumerate(derive_line(cells, below, above)):
                slope_ref[0, field, grid.xi_tile(i, group), :] = value
        for group in range(grid.xi_groups):
            below, above = take_sums(eta_a, eta_b, odd("eta"), field, group)
            cells = [prim_ref[field, grid.eta_tile(i, group), :] for i in range(grid.ny)]
            for i, value in enumerate(derive_line(cells, below, above)):
                slope_ref[1, field, grid.eta_tile(i, group), :] = value
        slope_ref[2, field] = lane_product(prim_ref[field], derive_ref[...])


def flux_kernel(
    grid,
    u_ref, prim_ref, metrics_ref, jacobian_ref, slope_ref, zeta_below, zeta_above, back_ref, sums_ref,
    contra_ref, eta_first, eta_second, xi_first, xi_second, zeta_ref,
    zeta_slope_ref,
):
    for field in range(4):
        halo = unpack_sums(zeta_below[field], zeta_above[field], grid)
        zeta_slope_ref[field] = slope_ref[2, field] + lane_product(halo, back_ref[...])

    step = TILE

    def body(index, carry):
        rows = pl.ds(pl.multiple_of(index * step, step), step)
        u = [u_ref[c, rows, :] for c in range(5)]
        speed = [prim_ref[c, rows, :] for c in range(3)]
        pressure = prim_ref[3, rows, :] * u[0]
        jacobian = jacobian_ref[rows, :]
        metrics = [[metrics_ref[3 * k + j, rows, :] for j in range(3)] for k in range(3)]
        physical = []
        for c in range(4):
            slopes = [slope_ref[0, c, rows, :], slope_ref[1, c, rows, :], zeta_slope_ref[c, rows, :]]
            physical.append(
                [
                    jacobian
                    * (
                        metrics[0][j] * slopes[0] + metrics[1][j] * slopes[1] + metrics[2][j] * slopes[2]
                    )
                    for j in range(3)
                ]
            )
        spread = (2.0 / 3.0 * viscosity) * (physical[0][0] + physical[1][1] + physical[2][2])
        stress = [[None] * 3 for _ in range(3)]
        for c in range(3):
            stress[c][c] = (2.0 * viscosity) * physical[c][c] - spread
            for j in range(c):
                stress[c][j] = stress[j][c] = viscosity * (physical[c][j] + physical[j][c])
        total = u[4] + pressure
        fluxes = []
        for j in range(3):
            parts = [u[1 + j]]
            for c in range(3):
                carried = u[1 + c] * speed[j] - stress[c][j]
                if c == j:
                    carried = carried + pressure
                parts.append(carried)
            worked = speed[0] * stress[0][j] + speed[1] * stress[1][j] + speed[2] * stress[2][j]
            parts.append(total * speed[j] - worked - conduction * physical[3][j])
            fluxes.append(parts)
        for k in range(3):
            for f in range(5):
                contra_ref[k, f, rows, :] = (
                    metrics[k][0] * fluxes[0][f]
                    + metrics[k][1] * fluxes[1][f]
                    + metrics[k][2] * fluxes[2][f]
                )
        return carry

    lax.fori_loop(0, grid.rows // step, body, 0)
    for field in range(5):
        send_sums(
            lambda position, group: contra_ref[1, field, grid.eta_tile(position, group), :],
            grid.xi_groups, grid.ny, odd("eta"), eta_first, eta_second, field,
        )
        send_sums(
            lambda position, group: contra_ref[0, field, grid.xi_tile(position, group), :],
            grid.eta_groups, grid.nx, odd("xi"), xi_first, xi_second, field,
        )
        zeta_ref[field] = pack_sums(contra_ref[2, field], sums_ref[...], grid)


def divergence_kernel(grid, contra_ref, eta_a, eta_b, xi_a, xi_b, derive_ref, total_ref):
    for field in range(5):
        total_ref[field] = lane_product(contra_ref[2, field], derive_ref[...])
        for group in range(grid.xi_groups):
            below, above = take_sums(eta_a, eta_b, odd("eta"), field, group)
            cells = [contra_ref[1, field, grid.eta_tile(i, group), :] for i in range(grid.ny)]
            for i, value in enumerate(derive_line(cells, below, above)):
                rows = grid.eta_tile(i, group)
                total_ref[field, rows, :] = total_ref[field, rows, :] + value
        for group in range(grid.eta_groups):
            below, above = take_sums(xi_a, xi_b, odd("xi"), field, group)
            cells = [contra_ref[0, field, grid.xi_tile(i, group), :] for i in range(grid.nx)]
            for i, value in enumerate(derive_line(cells, below, above)):
                rows = grid.xi_tile(i, group)
                total_ref[field, rows, :] = total_ref[field, rows, :] + value


def step_kernel(
    grid,
    u_ref, jacobian_ref, total_ref, zeta_below, zeta_above, back_ref,
    state_ref, eta_first, eta_second,
):
    scale = step_duration * jacobian_ref[...]
    for field in range(5):
        halo = unpack_sums(zeta_below[field], zeta_above[field], grid)
        total = total_ref[field] + lane_product(halo, back_ref[...])
        state_ref[field] = u_ref[field] - scale * total
        send_cells(
            lambda position, group: state_ref[field, grid.eta_tile(position, group), :],
            grid.xi_groups, grid.ny, odd("eta"), eta_first, eta_second, field,
        )


def send_cells(read, groups, count, flag, first_ref, second_ref, field):
    for group in range(groups):
        for step in range(WIDTH):
            low = read(step, group)
            top = read(count - 1 - step, group)
            index = WIDTH * field + step
            first_ref[index, group_rows(group), :] = jnp.where(flag, low, top)
            second_ref[index, group_rows(group), :] = jnp.where(flag, top, low)


def take_cells(first_ref, second_ref, flag, field, group):
    below, above = [], []
    for step in range(WIDTH):
        first = first_ref[WIDTH * field + step, group_rows(group), :]
        second = second_ref[WIDTH * field + step, group_rows(group), :]
        below.insert(0, jnp.where(flag, first, second))
        above.append(jnp.where(flag, second, first))
    return below, above


def eta_filter_kernel(grid, state_ref, eta_a, eta_b, result_ref, xi_first, xi_second):
    flag = odd("eta")
    for field in range(5):
        for group in range(grid.xi_groups):
            below, above = take_cells(eta_a, eta_b, flag, field, group)
            cells = [state_ref[field, grid.eta_tile(i, group), :] for i in range(grid.ny)]
            for i, value in enumerate(smooth_line(below + cells + above)):
                result_ref[field, grid.eta_tile(i, group), :] = value
        send_cells(
            lambda position, group: result_ref[field, grid.xi_tile(position, group), :],
            grid.eta_groups, grid.nx, odd("xi"), xi_first, xi_second, field,
        )


PACKED = 12


def xi_filter_kernel(grid, state_ref, xi_a, xi_b, result_ref, zeta_ref):
    flag = odd("xi")
    tiles = grid.rows // TILE
    for field in range(5):
        for group in range(grid.eta_groups):
            below, above = take_cells(xi_a, xi_b, flag, field, group)
            cells = [state_ref[field, grid.xi_tile(i, group), :] for i in range(grid.nx)]
            for i, value in enumerate(smooth_line(below + cells + above)):
                result_ref[field, grid.xi_tile(i, group), :] = value
        lane = lax.broadcasted_iota(jnp.int32, (TILE, LANES), 1)
        for start in range(0, tiles, PACKED):
            packed = None
            for slot in range(min(PACKED, tiles - start)):
                part = result_ref[field, group_rows(start + slot), :]
                part = pltpu.roll(part, WIDTH + 2 * WIDTH * slot, axis=1)
                packed = part if packed is None else jnp.where(lane >= 2 * WIDTH * slot, part, packed)
            zeta_ref[field, group_rows(start // PACKED), :] = packed


def zeta_filter_kernel(
    grid, state_ref, below_ref, above_ref, smooth_ref, ends_ref, result_hbm, result_ref, sems
):
    copies = []
    tiles = grid.rows // TILE
    lane = lax.broadcasted_iota(jnp.int32, (TILE, LANES), 1)
    for field in range(5):
        parts = []
        for start in range(0, tiles, PACKED):
            rows = group_rows(start // PACKED)
            packed = jnp.where(
                lax.rem(lane, 2 * WIDTH) < WIDTH, below_ref[field, rows, :], above_ref[field, rows, :]
            )
            for slot in range(min(PACKED, tiles - start)):
                parts.append(pltpu.roll(packed, LANES - 2 * WIDTH * slot, axis=1) if slot else packed)
        halo = jnp.concatenate(parts, axis=0)
        result_ref[field] = lane_product(state_ref[field], smooth_ref[...]) + lane_product(
            halo, ends_ref[...]
        )
        copy = pltpu.make_async_copy(result_ref.at[field], result_hbm.at[field], sems.at[field])
        copy.start()
        copies.append(copy)
    for copy in copies:
        copy.wait()


def pair_swap(value, axis, parity):
    count = lax.axis_size(axis)
    pairs = []
    for index in range(count):
        step = 1 if index % 2 == parity else -1
        pairs.append((index, (index + step) % count))
    return lax.ppermute(value, axis, pairs)


def ring_swap(value, axis):
    count = lax.axis_size(axis)
    if count == 2:
        other = lax.ppermute(value, axis, [(0, 1), (1, 0)])
        return other, other
    up = [(index, (index + 1) % count) for index in range(count)]
    down = [(index, (index - 1) % count) for index in range(count)]
    return lax.ppermute(value, axis, up), lax.ppermute(value, axis, down)


HBM = pltpu.MemorySpace.HBM


def call(kernel, outs, *operands, scratch=(), cost=1.0, far=(), far_outs=()):
    shapes = [
        out if isinstance(out, jax.ShapeDtypeStruct) else jax.ShapeDtypeStruct(out, jnp.float32)
        for out in outs
    ]
    near = pltpu.MemorySpace.VMEM
    return pl.pallas_call(
        kernel,
        out_shape=shapes,
        in_specs=[
            pl.BlockSpec(memory_space=HBM if index in far else near) for index in range(len(operands))
        ],
        out_specs=[
            pl.BlockSpec(memory_space=HBM if index in far_outs else near) for index in range(len(outs))
        ],
        scratch_shapes=scratch,
        cost_estimate=pl.CostEstimate(flops=0, transcendentals=0, bytes_accessed=int(cost * 3.6e6)),
        compiler_params=pltpu.CompilerParams(vmem_limit_bytes=20 * 2**20),
    )(*operands)


def like(value):
    return jax.ShapeDtypeStruct(value.shape, value.dtype)


def local(conserved_solution, metrics, jacobian):
    _, nx, ny, nz = conserved_solution.shape
    grid = Grid(nx, ny)
    rows = grid.rows
    u = conserved_solution.reshape(5, rows, nz)
    metrics = metrics.reshape(9, rows, nz)
    jacobian = jacobian.reshape(rows, nz)
    tables = {name: jnp.asarray(table) for name, table in zeta_tables(nz).items()}
    packs = -(-(rows // TILE) // PACKED)

    def exchange(eta_first, eta_second, xi_first, xi_second, zeta):
        eta_b = pair_swap(eta_second, "eta", 1)
        eta_a = pair_swap(eta_first, "eta", 0)
        xi_b = pair_swap(xi_second, "xi", 1)
        below, above = ring_swap(zeta, "zeta")
        xi_a = pair_swap(xi_first, "xi", 0)
        return (eta_a, eta_b, xi_a, xi_b), (below, above)

    def sums_shapes(fields):
        return [(2 * fields, nx, nz)] * 2 + [(2 * fields, ny, nz)] * 2 + [(fields, TILE, LANES)]

    chunks = 4
    u, sums, prim, *sends = call(
        functools.partial(primitive_kernel, grid),
        [like(u), like(tables["sums"]), (4, rows, nz)] + sums_shapes(4),
        u, tables["sums"],
        scratch=[pltpu.SemaphoreType.DMA, pltpu.SemaphoreType.DMA((chunks,))],
        far=(0, 1),
    )
    sides, ends = exchange(*sends)
    fetched = [metrics, jacobian] + [tables[name] for name in ("derive", "back", "smooth", "ends")]
    metrics, jacobian, derive, back, smooth, smooth_ends = call(
        functools.partial(fetch_kernel, len(fetched)),
        [like(value) for value in fetched],
        *fetched, sends[-1],
        scratch=[pltpu.SemaphoreType.DMA((len(fetched),))],
        far=tuple(range(len(fetched))),
    )
    (slopes,) = call(
        functools.partial(slope_kernel, grid), [(3, 4, rows, nz)], prim, *sides, derive,
    )
    contra, *sends = call(
        functools.partial(flux_kernel, grid),
        [(3, 5, rows, nz)] + sums_shapes(5),
        u, prim, metrics, jacobian, slopes, *ends, back, sums,
        scratch=[pltpu.VMEM((4, rows, nz), jnp.float32)],
    )
    sides, ends = exchange(*sends)
    (total,) = call(
        functools.partial(divergence_kernel, grid), [(5, rows, nz)], contra, *sides, derive,
    )
    state, eta_first, eta_second = call(
        functools.partial(step_kernel, grid),
        [(5, rows, nz)] + [(5 * WIDTH, nx, nz)] * 2,
        u, jacobian, total, *ends, back,
    )
    eta_b = pair_swap(eta_second, "eta", 1)
    eta_a = pair_swap(eta_first, "eta", 0)
    state, xi_first, xi_second = call(
        functools.partial(eta_filter_kernel, grid),
        [(5, rows, nz)] + [(5 * WIDTH, ny, nz)] * 2,
        state, eta_a, eta_b,
    )
    xi_b = pair_swap(xi_second, "xi", 1)
    xi_a = pair_swap(xi_first, "xi", 0)
    state, zeta = call(
        functools.partial(xi_filter_kernel, grid),
        [(5, rows, nz), (5, packs * TILE, LANES)],
        state, xi_a, xi_b,
    )
    below, above = ring_swap(zeta, "zeta")
    (result,) = call(
        functools.partial(zeta_filter_kernel, grid),
        [(5, rows, nz)],
        state, below, above, smooth, smooth_ends,
        scratch=[pltpu.VMEM((5, rows, nz), jnp.float32), pltpu.SemaphoreType.DMA((5,))],
        far_outs=(0,),
    )
    return result.reshape(5, nx, ny, nz)


def solution(mesh):
    in_specs = (
        P(None, "xi", "eta", "zeta"),
        P(None, None, "xi", "eta", "zeta"),
        P("xi", "eta", "zeta"),
    )
    out_specs = P(None, "xi", "eta", "zeta")
    return jax.shard_map(local, mesh=mesh, in_specs=in_specs, out_specs=out_specs, check_vma=False)
```

```python
import functools

import jax
import jax.numpy as jnp
import numpy as np
from jax import lax
from jax.experimental import pallas as pl
from jax.experimental.pallas import tpu as pltpu
from jax.sharding import PartitionSpec as P

WIDTH = 5
LANES = 128
TILE = 8

viscosity = 0.15
conduction = 0.15 * 1.4 / (0.4 * 0.72)
step_duration = 0.08


def derivative_system(length):
    extent = length + 2 * WIDTH
    system = np.eye(extent)
    source = np.zeros((extent, extent))
    for position in range(2, extent - 2):
        system[position, position - 1] = 1.0 / 3.0
        system[position, position + 1] = 1.0 / 3.0
        source[position, position + 1] = 7.0 / 9.0
        source[position, position - 1] = -7.0 / 9.0
        source[position, position + 2] = 1.0 / 36.0
        source[position, position - 2] = -1.0 / 36.0
    source[1, 2] = 0.5
    source[1, 0] = -0.5
    source[extent - 2, extent - 1] = 0.5
    source[extent - 2, extent - 3] = -0.5
    source[0, 1] = 1.0
    source[0, 0] = -1.0
    source[extent - 1, extent - 1] = 1.0
    source[extent - 1, extent - 2] = -1.0
    return system, source


def filter_coefficients():
    strength = 0.4
    return [
        (193.0 + 126.0 * strength) / 256.0,
        (105.0 + 302.0 * strength) / 256.0,
        15.0 * (2.0 * strength - 1.0) / 64.0,
        45.0 * (1.0 - 2.0 * strength) / 512.0,
        5.0 * (2.0 * strength - 1.0) / 256.0,
        (1.0 - 2.0 * strength) / 512.0,
    ]


def filter_system(length):
    strength = 0.4
    coeffs = filter_coefficients()
    extent = length + 2 * WIDTH
    system = np.eye(extent)
    source = np.eye(extent)
    for position in range(5, extent - 5):
        system[position, position - 1] = strength
        system[position, position + 1] = strength
        source[position, position] = coeffs[0]
        for offset in range(1, 6):
            source[position, position + offset] = coeffs[offset] / 2.0
            source[position, position - offset] = coeffs[offset] / 2.0
    return system, source


def own_rows(system, source, length):
    return np.linalg.solve(system, source)[WIDTH : WIDTH + length]


def derivative_parts(length):
    system, source = derivative_system(length)
    halo = np.linalg.solve(system[:WIDTH, :WIDTH], source[:WIDTH])
    row = source[WIDTH] - system[WIDTH, WIDTH - 1] * halo[WIDTH - 1]
    pivots = [1.0]
    for position in range(3, WIDTH + length):
        pivots.append(1.0 - 1.0 / 9.0 / pivots[-1])
    return pivots[WIDTH - 2 :], row[:WIDTH], row[WIDTH : WIDTH + 3]


def pad_rows(table):
    return np.concatenate([table, np.zeros((LANES - table.shape[0], table.shape[1]))], axis=0)


def pad_columns(table):
    return np.concatenate([table, np.zeros((table.shape[0], LANES - table.shape[1]))], axis=1)


def zeta_tables(length):
    system, source = derivative_system(length)
    table = own_rows(system, source, length)
    _, edge, _ = derivative_parts(length)
    inverse = np.linalg.inv(system)
    extent = length + 2 * WIDTH
    sums = np.zeros((length, 4))
    sums[length - WIDTH :, 0] = edge
    sums[length - 1, 1] = 1.0
    sums[:WIDTH, 2] = -edge[::-1]
    sums[0, 3] = 1.0
    own = slice(WIDTH, WIDTH + length)
    back = np.stack(
        [
            inverse[own, WIDTH],
            -1.0 / 36.0 * inverse[own, WIDTH + 1],
            inverse[own, extent - WIDTH - 1],
            1.0 / 36.0 * inverse[own, extent - WIDTH - 2],
        ]
    )
    smooth = own_rows(*filter_system(length), length)
    ends = np.concatenate([smooth[:, :WIDTH], smooth[:, WIDTH + length :]], axis=1)
    tables = [table[:, own].T, pad_columns(sums), pad_rows(back), smooth[:, own].T, pad_rows(ends.T)]
    return np.stack(tables).astype(np.float32)


DERIVE, SUMS, BACK, SMOOTH, ENDS = range(5)


def twisted_solve(rights, pivots, off):
    count = len(rights)
    half = count // 2
    low = [rights[0]]
    high = [rights[count - 1]]
    for step in range(1, half):
        factor = off / pivots[step - 1]
        low.append(rights[step] - factor * low[-1])
        high.append(rights[count - 1 - step] - factor * high[-1])
    middle = pivots[half - 1]
    det = middle * middle - off * off
    first, second = low[-1], high[-1]
    answer = [None] * count
    answer[half - 1] = (middle / det) * first - (off / det) * second
    answer[half] = (middle / det) * second - (off / det) * first
    for step in range(half - 2, -1, -1):
        scale = 1.0 / pivots[step]
        factor = off / pivots[step]
        answer[step] = scale * low[step] - factor * answer[step + 1]
        answer[count - 1 - step] = scale * high[step] - factor * answer[count - 2 - step]
    return answer


def derive_line(cells, below, above):
    count = len(cells)
    pivots, _, edge = derivative_parts(count)
    near, far = 7.0 / 9.0, 1.0 / 36.0
    rights = [None] * count
    rights[0] = below[0] + edge[0] * cells[0] + edge[1] * cells[1] + edge[2] * cells[2]
    rights[1] = near * (cells[2] - cells[0]) + far * (cells[3] - below[1])
    for step in range(2, count - 2):
        rights[step] = near * (cells[step + 1] - cells[step - 1]) + far * (
            cells[step + 2] - cells[step - 2]
        )
    rights[count - 2] = near * (cells[count - 1] - cells[count - 3]) + far * (
        above[1] - cells[count - 4]
    )
    rights[count - 1] = above[0] - (
        edge[0] * cells[count - 1] + edge[1] * cells[count - 2] + edge[2] * cells[count - 3]
    )
    return twisted_solve(rights, pivots, 1.0 / 3.0)


def end_sums(cells):
    _, edge, _ = derivative_parts(16)
    total = edge[WIDTH - 1] * cells[0]
    for step in range(1, WIDTH):
        total = total + edge[WIDTH - 1 - step] * cells[step]
    return total, cells[0]


def smooth_line(cells):
    count = len(cells) - 2 * WIDTH
    coeffs = filter_coefficients()
    pivots = [1.0]
    for _ in range(count):
        pivots.append(1.0 - 0.16 / pivots[-1])
    rights = []
    for step in range(WIDTH, WIDTH + count):
        total = coeffs[0] * cells[step]
        for offset in range(1, WIDTH + 1):
            total = total + (0.5 * coeffs[offset]) * (cells[step + offset] + cells[step - offset])
        rights.append(total)
    rights[0] = rights[0] - 0.4 * cells[WIDTH - 1]
    rights[-1] = rights[-1] - 0.4 * cells[WIDTH + count]
    return twisted_solve(rights, pivots, 0.4)


def split_values(values):
    high = values.astype(jnp.bfloat16)
    low = (values - high.astype(jnp.float32)).astype(jnp.bfloat16)
    return jnp.concatenate([high, low], axis=1)


def split_weights(table):
    high = table.astype(jnp.bfloat16)
    low = (table - high.astype(jnp.float32)).astype(jnp.bfloat16)
    top = jnp.concatenate([high, low], axis=1)
    return jnp.concatenate([top, jnp.concatenate([high, jnp.zeros_like(low)], axis=1)], axis=0)


def lane_product(values, weights):
    both = jnp.dot(split_values(values), weights, preferred_element_type=jnp.float32)
    return both[:, :LANES] + both[:, LANES:]


class Grid:
    def __init__(self, nx, ny):
        self.nx, self.ny, self.rows = nx, ny, nx * ny
        self.eta_groups = ny // TILE
        self.xi_groups = nx // TILE

    def xi_tile(self, position, group):
        return pl.ds(position * self.ny + group * TILE, TILE)

    def eta_tile(self, position, group):
        return pl.ds(position + group * TILE * self.ny, TILE, stride=self.ny)


def group_rows(group):
    return pl.ds(group * TILE, TILE)


def odd(axis):
    return lax.rem(lax.axis_index(axis), 2) == 1


def send_sums(read, groups, count, flag, first_ref, second_ref, field):
    for group in range(groups):
        top = end_sums([read(count - 1 - step, group) for step in range(WIDTH)])
        low = end_sums([read(step, group) for step in range(WIDTH)])
        low = (-low[0], low[1])
        for part in range(2):
            first_ref[2 * field + part, group_rows(group), :] = jnp.where(flag, low[part], top[part])
            second_ref[2 * field + part, group_rows(group), :] = jnp.where(flag, top[part], low[part])


def take_sums(first_ref, second_ref, flag, field, group):
    below, above = [], []
    for part in range(2):
        first = first_ref[2 * field + part, group_rows(group), :]
        second = second_ref[2 * field + part, group_rows(group), :]
        below.append(jnp.where(flag, first, second))
        above.append(jnp.where(flag, second, first))
    return below, above


def pack_sums(values, weights, grid):
    sums = lane_product(values, weights)
    packed = None
    for group in range(grid.rows // TILE):
        part = sums[group * TILE : (group + 1) * TILE]
        if group:
            part = pltpu.roll(part, 4 * group, axis=1)
        packed = part if packed is None else packed + part
    return packed


def unpack_sums(below, above, grid):
    lane = lax.broadcasted_iota(jnp.int32, below.shape, 1)
    packed = jnp.where(lax.rem(lane, 4) < 2, below, above)
    parts = [packed]
    for group in range(1, grid.rows // TILE):
        parts.append(pltpu.roll(packed, LANES - 4 * group, axis=1))
    return jnp.concatenate(parts, axis=0)


def primitive_kernel(
    grid,
    u_hbm, tables_hbm,
    u_ref, tables_ref, prim_ref, eta_first, eta_second, xi_first, xi_second, zeta_ref,
    tables_sem, u_sems,
):
    chunks = u_sems.shape[0]
    step = grid.rows // chunks
    copies = []
    for index in range(chunks):
        rows = pl.ds(index * step, step)
        copy = pltpu.make_async_copy(u_hbm.at[:, rows, :], u_ref.at[:, rows, :], u_sems.at[index])
        copy.start()
        copies.append(copy)
    weights = pltpu.make_async_copy(tables_hbm, tables_ref, tables_sem)
    weights.start()
    for index in range(chunks):
        copies[index].wait()
        rows = pl.ds(index * step, step)
        inverse = 1.0 / u_ref[0, rows, :]
        work = None
        for c in range(3):
            momentum = u_ref[1 + c, rows, :]
            speed = momentum * inverse
            prim_ref[c, rows, :] = speed
            work = momentum * speed if work is None else work + momentum * speed
        pressure = 0.4 * (u_ref[4, rows, :] - 0.5 * work)
        prim_ref[3, rows, :] = pressure * inverse
    for field in range(4):
        send_sums(
            lambda position, group: prim_ref[field, grid.eta_tile(position, group), :],
            grid.xi_groups, grid.ny, odd("eta"), eta_first, eta_second, field,
        )
        send_sums(
            lambda position, group: prim_ref[field, grid.xi_tile(position, group), :],
            grid.eta_groups, grid.nx, odd("xi"), xi_first, xi_second, field,
        )
    weights.wait()
    sums = split_weights(tables_ref[SUMS])
    for field in range(4):
        zeta_ref[field] = pack_sums(prim_ref[field], sums, grid)


def fetch_kernel(count, *refs):
    sources, results, sems = refs[:count], refs[count + 1 : 2 * count + 1], refs[-1]
    copies = [
        pltpu.make_async_copy(source, result, sems.at[index])
        for index, (source, result) in enumerate(zip(sources, results))
    ]
    for copy in copies:
        copy.start()
    for copy in copies:
        copy.wait()


def slope_kernel(grid, prim_ref, eta_a, eta_b, xi_a, xi_b, tables_ref, slope_ref):
    derive = split_weights(tables_ref[DERIVE])
    for field in range(4):
        for group in range(grid.eta_groups):
            below, above = take_sums(xi_a, xi_b, odd("xi"), field, group)
            cells = [prim_ref[field, grid.xi_tile(i, group), :] for i in range(grid.nx)]
            for i, value in enumerate(derive_line(cells, below, above)):
                slope_ref[0, field, grid.xi_tile(i, group), :] = value
        for group in range(grid.xi_groups):
            below, above = take_sums(eta_a, eta_b, odd("eta"), field, group)
            cells = [prim_ref[field, grid.eta_tile(i, group), :] for i in range(grid.ny)]
            for i, value in enumerate(derive_line(cells, below, above)):
                slope_ref[1, field, grid.eta_tile(i, group), :] = value
        slope_ref[2, field] = lane_product(prim_ref[field], derive)


def flux_kernel(
    grid,
    u_ref, prim_ref, metrics_ref, jacobian_ref, slope_ref, zeta_below, zeta_above, tables_ref,
    contra_ref, eta_first, eta_second, xi_first, xi_second, zeta_ref,
    zeta_slope_ref,
):
    back, sums = split_weights(tables_ref[BACK]), split_weights(tables_ref[SUMS])
    for field in range(4):
        halo = unpack_sums(zeta_below[field], zeta_above[field], grid)
        zeta_slope_ref[field] = slope_ref[2, field] + lane_product(halo, back)

    step = TILE

    def body(index, carry):
        rows = pl.ds(pl.multiple_of(index * step, step), step)
        u = [u_ref[c, rows, :] for c in range(5)]
        speed = [prim_ref[c, rows, :] for c in range(3)]
        pressure = prim_ref[3, rows, :] * u[0]
        jacobian = jacobian_ref[rows, :]
        metrics = [[metrics_ref[3 * k + j, rows, :] for j in range(3)] for k in range(3)]
        physical = []
        for c in range(4):
            slopes = [slope_ref[0, c, rows, :], slope_ref[1, c, rows, :], zeta_slope_ref[c, rows, :]]
            physical.append(
                [
                    jacobian
                    * (
                        metrics[0][j] * slopes[0] + metrics[1][j] * slopes[1] + metrics[2][j] * slopes[2]
                    )
                    for j in range(3)
                ]
            )
        spread = (2.0 / 3.0 * viscosity) * (physical[0][0] + physical[1][1] + physical[2][2])
        stress = [[None] * 3 for _ in range(3)]
        for c in range(3):
            stress[c][c] = (2.0 * viscosity) * physical[c][c] - spread
            for j in range(c):
                stress[c][j] = stress[j][c] = viscosity * (physical[c][j] + physical[j][c])
        total = u[4] + pressure
        fluxes = []
        for j in range(3):
            parts = [u[1 + j]]
            for c in range(3):
                carried = u[1 + c] * speed[j] - stress[c][j]
                if c == j:
                    carried = carried + pressure
                parts.append(carried)
            worked = speed[0] * stress[0][j] + speed[1] * stress[1][j] + speed[2] * stress[2][j]
            parts.append(total * speed[j] - worked - conduction * physical[3][j])
            fluxes.append(parts)
        for k in range(3):
            for f in range(5):
                contra_ref[k, f, rows, :] = (
                    metrics[k][0] * fluxes[0][f]
                    + metrics[k][1] * fluxes[1][f]
                    + metrics[k][2] * fluxes[2][f]
                )
        return carry

    lax.fori_loop(0, grid.rows // step, body, 0)
    for field in range(5):
        send_sums(
            lambda position, group: contra_ref[1, field, grid.eta_tile(position, group), :],
            grid.xi_groups, grid.ny, odd("eta"), eta_first, eta_second, field,
        )
        send_sums(
            lambda position, group: contra_ref[0, field, grid.xi_tile(position, group), :],
            grid.eta_groups, grid.nx, odd("xi"), xi_first, xi_second, field,
        )
        zeta_ref[field] = pack_sums(contra_ref[2, field], sums, grid)


def divergence_kernel(grid, contra_ref, eta_a, eta_b, xi_a, xi_b, tables_ref, total_ref):
    derive = split_weights(tables_ref[DERIVE])
    for field in range(5):
        total_ref[field] = lane_product(contra_ref[2, field], derive)
        for group in range(grid.xi_groups):
            below, above = take_sums(eta_a, eta_b, odd("eta"), field, group)
            cells = [contra_ref[1, field, grid.eta_tile(i, group), :] for i in range(grid.ny)]
            for i, value in enumerate(derive_line(cells, below, above)):
                rows = grid.eta_tile(i, group)
                total_ref[field, rows, :] = total_ref[field, rows, :] + value
        for group in range(grid.eta_groups):
            below, above = take_sums(xi_a, xi_b, odd("xi"), field, group)
            cells = [contra_ref[0, field, grid.xi_tile(i, group), :] for i in range(grid.nx)]
            for i, value in enumerate(derive_line(cells, below, above)):
                rows = grid.xi_tile(i, group)
                total_ref[field, rows, :] = total_ref[field, rows, :] + value


def step_kernel(
    grid,
    u_ref, jacobian_ref, total_ref, zeta_below, zeta_above, tables_ref,
    state_ref, eta_first, eta_second,
):
    back = split_weights(tables_ref[BACK])
    scale = step_duration * jacobian_ref[...]
    for field in range(5):
        halo = unpack_sums(zeta_below[field], zeta_above[field], grid)
        total = total_ref[field] + lane_product(halo, back)
        state_ref[field] = u_ref[field] - scale * total
        send_cells(
            lambda position, group: state_ref[field, grid.eta_tile(position, group), :],
            grid.xi_groups, grid.ny, odd("eta"), eta_first, eta_second, field,
        )


def send_cells(read, groups, count, flag, first_ref, second_ref, field):
    for group in range(groups):
        for step in range(WIDTH):
            low = read(step, group)
            top = read(count - 1 - step, group)
            index = WIDTH * field + step
            first_ref[index, group_rows(group), :] = jnp.where(flag, low, top)
            second_ref[index, group_rows(group), :] = jnp.where(flag, top, low)


def take_cells(first_ref, second_ref, flag, field, group):
    below, above = [], []
    for step in range(WIDTH):
        first = first_ref[WIDTH * field + step, group_rows(group), :]
        second = second_ref[WIDTH * field + step, group_rows(group), :]
        below.insert(0, jnp.where(flag, first, second))
        above.append(jnp.where(flag, second, first))
    return below, above


def eta_filter_kernel(
    grid, state_ref, eta_a, eta_b, result_ref, xi_first, xi_second, zeta_ref, edge_first, edge_second
):
    for field in range(5):
        for group in range(grid.xi_groups):
            below, above = take_cells(eta_a, eta_b, odd("eta"), field, group)
            cells = [state_ref[field, grid.eta_tile(i, group), :] for i in range(grid.ny)]
            for i, value in enumerate(smooth_line(below + cells + above)):
                result_ref[field, grid.eta_tile(i, group), :] = value
    flag = odd("xi")
    for field in range(5):
        send_cells(
            lambda position, group: result_ref[field, grid.xi_tile(position, group), :],
            grid.eta_groups, grid.nx, flag, xi_first, xi_second, field,
        )
    lane = lax.broadcasted_iota(jnp.int32, (TILE, LANES), 1)
    for position in range(grid.nx):
        packed = None
        for slot in range(5 * grid.eta_groups):
            field, group = slot // grid.eta_groups, slot % grid.eta_groups
            part = result_ref[field, grid.xi_tile(position, group), :]
            part = pltpu.roll(part, WIDTH * (2 * slot + 1), axis=1)
            packed = part if packed is None else jnp.where(lane >= 2 * WIDTH * slot, part, packed)
        zeta_ref[group_rows(position), :] = packed
    send_cells(
        lambda position, group: zeta_ref[group_rows(position), :],
        1, grid.nx, flag, edge_first, edge_second, 0,
    )


def xi_filter_kernel(grid, state_ref, xi_a, xi_b, tables_ref, result_ref):
    smooth = split_weights(tables_ref[SMOOTH])
    flag = odd("xi")
    for field in range(5):
        for group in range(grid.eta_groups):
            below, above = take_cells(xi_a, xi_b, flag, field, group)
            cells = [state_ref[field, grid.xi_tile(i, group), :] for i in range(grid.nx)]
            for i, value in enumerate(smooth_line(below + cells + above)):
                result_ref[field, grid.xi_tile(i, group), :] = value
        result_ref[field] = lane_product(result_ref[field], smooth)


def zeta_filter_kernel(
    grid,
    state_ref, below_ref, above_ref, a_below, a_above, b_below, b_above, tables_ref,
    result_hbm,
    result_ref, sems,
):
    ends = split_weights(tables_ref[ENDS])
    flag = odd("xi")
    lane = lax.broadcasted_iota(jnp.int32, (TILE, LANES), 1)
    from_below = lax.rem(lane, 2 * WIDTH) < WIDTH

    def merge(below, above, index):
        return jnp.where(from_below, below[group_rows(index), :], above[group_rows(index), :])

    low, high = [], []
    for step in range(WIDTH):
        first, second = merge(a_below, a_above, step), merge(b_below, b_above, step)
        low.insert(0, jnp.where(flag, first, second))
        high.append(jnp.where(flag, second, first))
    cells = [merge(below_ref, above_ref, position) for position in range(grid.nx)]
    cells = smooth_line(low + cells + high)
    copies = []
    for field in range(5):
        parts = []
        for packed in cells:
            for group in range(grid.eta_groups):
                slot = field * grid.eta_groups + group
                parts.append(pltpu.roll(packed, LANES - 2 * WIDTH * slot, axis=1) if slot else packed)
        halo = jnp.concatenate(parts, axis=0)
        result_ref[field] = state_ref[field] + lane_product(halo, ends)
        copy = pltpu.make_async_copy(result_ref.at[field], result_hbm.at[field], sems.at[field])
        copy.start()
        copies.append(copy)
    for copy in copies:
        copy.wait()


def pair_swap(value, axis, parity):
    count = lax.axis_size(axis)
    pairs = []
    for index in range(count):
        step = 1 if index % 2 == parity else -1
        pairs.append((index, (index + step) % count))
    return lax.ppermute(value, axis, pairs)


def diagonal_swap(value, parity):
    nx, nz = lax.axis_size("xi"), lax.axis_size("zeta")

    def send(shift):
        pairs = []
        for i in range(nx):
            partner = (i + (1 if i % 2 == parity else -1)) % nx
            for k in range(nz):
                pairs.append((i * nz + k, partner * nz + (k + shift) % nz))
        return lax.ppermute(value, ("xi", "zeta"), pairs)

    below = send(1)
    return (below, below) if nz == 2 else (below, send(-1))


def ring_swap(value, axis):
    count = lax.axis_size(axis)
    if count == 2:
        other = lax.ppermute(value, axis, [(0, 1), (1, 0)])
        return other, other
    up = [(index, (index + 1) % count) for index in range(count)]
    down = [(index, (index - 1) % count) for index in range(count)]
    return lax.ppermute(value, axis, up), lax.ppermute(value, axis, down)


HBM = pltpu.MemorySpace.HBM


def call(kernel, outs, *operands, scratch=(), cost=1.0, far=(), far_outs=()):
    shapes = [
        out if isinstance(out, jax.ShapeDtypeStruct) else jax.ShapeDtypeStruct(out, jnp.float32)
        for out in outs
    ]
    near = pltpu.MemorySpace.VMEM
    operands = [
        pltpu.with_memory_space_constraint(value, HBM) if index in far else value
        for index, value in enumerate(operands)
    ]
    return pl.pallas_call(
        kernel,
        out_shape=shapes,
        in_specs=[
            pl.BlockSpec(memory_space=HBM if index in far else near) for index in range(len(operands))
        ],
        out_specs=[
            pl.BlockSpec(memory_space=HBM if index in far_outs else near) for index in range(len(outs))
        ],
        scratch_shapes=scratch,
        cost_estimate=pl.CostEstimate(flops=0, transcendentals=0, bytes_accessed=int(cost * 3.6e6)),
        compiler_params=pltpu.CompilerParams(vmem_limit_bytes=20 * 2**20),
    )(*operands)


def like(value):
    return jax.ShapeDtypeStruct(value.shape, value.dtype)


def local(conserved_solution, metrics, jacobian):
    _, nx, ny, nz = conserved_solution.shape
    grid = Grid(nx, ny)
    rows = grid.rows
    u = conserved_solution.reshape(5, rows, nz)
    metrics = metrics.reshape(9, rows, nz)
    jacobian = jacobian.reshape(rows, nz)
    tables = jnp.asarray(zeta_tables(nz))

    def exchange(eta_first, eta_second, xi_first, xi_second, zeta):
        eta_b = pair_swap(eta_second, "eta", 1)
        eta_a = pair_swap(eta_first, "eta", 0)
        xi_b = pair_swap(xi_second, "xi", 1)
        below, above = ring_swap(zeta, "zeta")
        xi_a = pair_swap(xi_first, "xi", 0)
        return (eta_a, eta_b, xi_a, xi_b), (below, above)

    def sums_shapes(fields):
        return [(2 * fields, nx, nz)] * 2 + [(2 * fields, ny, nz)] * 2 + [(fields, TILE, LANES)]

    chunks = 4
    u, tables, prim, *sends = call(
        functools.partial(primitive_kernel, grid),
        [like(u), like(tables), (4, rows, nz)] + sums_shapes(4),
        u, tables,
        scratch=[pltpu.SemaphoreType.DMA, pltpu.SemaphoreType.DMA((chunks,))],
        far=(0, 1),
    )
    sides, ends = exchange(*sends)
    metrics, jacobian = call(
        functools.partial(fetch_kernel, 2),
        [like(metrics), like(jacobian)],
        metrics, jacobian, sends[-1],
        scratch=[pltpu.SemaphoreType.DMA((2,))],
        far=(0, 1),
    )
    (slopes,) = call(
        functools.partial(slope_kernel, grid), [(3, 4, rows, nz)], prim, *sides, tables,
    )
    contra, *sends = call(
        functools.partial(flux_kernel, grid),
        [(3, 5, rows, nz)] + sums_shapes(5),
        u, prim, metrics, jacobian, slopes, *ends, tables,
        scratch=[pltpu.VMEM((4, rows, nz), jnp.float32)],
    )
    sides, ends = exchange(*sends)
    (total,) = call(
        functools.partial(divergence_kernel, grid), [(5, rows, nz)], contra, *sides, tables,
    )
    state, eta_first, eta_second = call(
        functools.partial(step_kernel, grid),
        [(5, rows, nz)] + [(5 * WIDTH, nx, nz)] * 2,
        u, jacobian, total, *ends, tables,
    )
    eta_b = pair_swap(eta_second, "eta", 1)
    eta_a = pair_swap(eta_first, "eta", 0)
    state, xi_first, xi_second, zeta, edge_first, edge_second = call(
        functools.partial(eta_filter_kernel, grid),
        [(5, rows, nz)]
        + [(5 * WIDTH, ny, nz)] * 2
        + [(nx * TILE, LANES)]
        + [(WIDTH, TILE, LANES)] * 2,
        state, eta_a, eta_b,
    )
    xi_b = pair_swap(xi_second, "xi", 1)
    ends = ring_swap(zeta, "zeta")
    edges_b = diagonal_swap(edge_second, 1)
    edges_a = diagonal_swap(edge_first, 0)
    xi_a = pair_swap(xi_first, "xi", 0)
    (state,) = call(
        functools.partial(xi_filter_kernel, grid), [(5, rows, nz)], state, xi_a, xi_b, tables,
    )
    edges = [edge.reshape(WIDTH * TILE, LANES) for edge in (*edges_a, *edges_b)]
    (result,) = call(
        functools.partial(zeta_filter_kernel, grid),
        [(5, rows, nz)],
        state, *ends, *edges, tables,
        scratch=[pltpu.VMEM((5, rows, nz), jnp.float32), pltpu.SemaphoreType.DMA((5,))],
        far_outs=(0,),
    )
    return result.reshape(5, nx, ny, nz)


def solution(mesh):
    in_specs = (
        P(None, "xi", "eta", "zeta"),
        P(None, None, "xi", "eta", "zeta"),
        P("xi", "eta", "zeta"),
    )
    out_specs = P(None, "xi", "eta", "zeta")
    return jax.shard_map(local, mesh=mesh, in_specs=in_specs, out_specs=out_specs, check_vma=False)
```

```python
import functools

import jax
import jax.numpy as jnp
import numpy as np
from jax import lax
from jax.experimental import pallas as pl
from jax.experimental.pallas import tpu as pltpu
from jax.sharding import PartitionSpec as P

WIDTH = 5
LANES = 128
TILE = 8

viscosity = 0.15
conduction = 0.15 * 1.4 / (0.4 * 0.72)
step_duration = 0.08


def derivative_system(length):
    extent = length + 2 * WIDTH
    system = np.eye(extent)
    source = np.zeros((extent, extent))
    for position in range(2, extent - 2):
        system[position, position - 1] = 1.0 / 3.0
        system[position, position + 1] = 1.0 / 3.0
        source[position, position + 1] = 7.0 / 9.0
        source[position, position - 1] = -7.0 / 9.0
        source[position, position + 2] = 1.0 / 36.0
        source[position, position - 2] = -1.0 / 36.0
    source[1, 2] = 0.5
    source[1, 0] = -0.5
    source[extent - 2, extent - 1] = 0.5
    source[extent - 2, extent - 3] = -0.5
    source[0, 1] = 1.0
    source[0, 0] = -1.0
    source[extent - 1, extent - 1] = 1.0
    source[extent - 1, extent - 2] = -1.0
    return system, source


def filter_coefficients():
    strength = 0.4
    return [
        (193.0 + 126.0 * strength) / 256.0,
        (105.0 + 302.0 * strength) / 256.0,
        15.0 * (2.0 * strength - 1.0) / 64.0,
        45.0 * (1.0 - 2.0 * strength) / 512.0,
        5.0 * (2.0 * strength - 1.0) / 256.0,
        (1.0 - 2.0 * strength) / 512.0,
    ]


def filter_system(length):
    strength = 0.4
    coeffs = filter_coefficients()
    extent = length + 2 * WIDTH
    system = np.eye(extent)
    source = np.eye(extent)
    for position in range(5, extent - 5):
        system[position, position - 1] = strength
        system[position, position + 1] = strength
        source[position, position] = coeffs[0]
        for offset in range(1, 6):
            source[position, position + offset] = coeffs[offset] / 2.0
            source[position, position - offset] = coeffs[offset] / 2.0
    return system, source


def own_rows(system, source, length):
    return np.linalg.solve(system, source)[WIDTH : WIDTH + length]


def derivative_parts(length):
    system, source = derivative_system(length)
    halo = np.linalg.solve(system[:WIDTH, :WIDTH], source[:WIDTH])
    row = source[WIDTH] - system[WIDTH, WIDTH - 1] * halo[WIDTH - 1]
    pivots = [1.0]
    for position in range(3, WIDTH + length):
        pivots.append(1.0 - 1.0 / 9.0 / pivots[-1])
    return pivots[WIDTH - 2 :], row[:WIDTH], row[WIDTH : WIDTH + 3]


def pad_rows(table):
    return np.concatenate([table, np.zeros((LANES - table.shape[0], table.shape[1]))], axis=0)


def pad_columns(table):
    return np.concatenate([table, np.zeros((table.shape[0], LANES - table.shape[1]))], axis=1)


def zeta_tables(length):
    system, source = derivative_system(length)
    table = own_rows(system, source, length)
    _, edge, _ = derivative_parts(length)
    inverse = np.linalg.inv(system)
    extent = length + 2 * WIDTH
    sums = np.zeros((length, 4))
    sums[length - WIDTH :, 0] = edge
    sums[length - 1, 1] = 1.0
    sums[:WIDTH, 2] = -edge[::-1]
    sums[0, 3] = 1.0
    own = slice(WIDTH, WIDTH + length)
    back = np.stack(
        [
            inverse[own, WIDTH],
            -1.0 / 36.0 * inverse[own, WIDTH + 1],
            inverse[own, extent - WIDTH - 1],
            1.0 / 36.0 * inverse[own, extent - WIDTH - 2],
        ]
    )
    smooth = own_rows(*filter_system(length), length)
    ends = np.concatenate([smooth[:, :WIDTH], smooth[:, WIDTH + length :]], axis=1)
    tables = [table[:, own].T, pad_columns(sums), pad_rows(back), smooth[:, own].T, pad_rows(ends.T)]
    return np.stack(tables).astype(np.float32)


DERIVE, SUMS, BACK, SMOOTH, ENDS = range(5)


def twisted_solve(rights, pivots, off):
    count = len(rights)
    half = count // 2
    low = [rights[0]]
    high = [rights[count - 1]]
    for step in range(1, half):
        factor = off / pivots[step - 1]
        low.append(rights[step] - factor * low[-1])
        high.append(rights[count - 1 - step] - factor * high[-1])
    middle = pivots[half - 1]
    det = middle * middle - off * off
    first, second = low[-1], high[-1]
    answer = [None] * count
    answer[half - 1] = (middle / det) * first - (off / det) * second
    answer[half] = (middle / det) * second - (off / det) * first
    for step in range(half - 2, -1, -1):
        scale = 1.0 / pivots[step]
        factor = off / pivots[step]
        answer[step] = scale * low[step] - factor * answer[step + 1]
        answer[count - 1 - step] = scale * high[step] - factor * answer[count - 2 - step]
    return answer


def derive_source(cells):
    count = len(cells)
    _, _, edge = derivative_parts(count)
    near, far = 7.0 / 9.0, 1.0 / 36.0
    rights = [None] * count
    rights[0] = edge[0] * cells[0] + edge[1] * cells[1] + edge[2] * cells[2]
    rights[1] = near * (cells[2] - cells[0]) + far * cells[3]
    for step in range(2, count - 2):
        rights[step] = near * (cells[step + 1] - cells[step - 1]) + far * (
            cells[step + 2] - cells[step - 2]
        )
    rights[count - 2] = near * (cells[count - 1] - cells[count - 3]) - far * cells[count - 4]
    rights[count - 1] = -(
        edge[0] * cells[count - 1] + edge[1] * cells[count - 2] + edge[2] * cells[count - 3]
    )
    return rights


def derive_solve(rights, below, above):
    pivots, _, _ = derivative_parts(len(rights))
    rights = list(rights)
    far = 1.0 / 36.0
    rights[0] = rights[0] + below[0]
    rights[1] = rights[1] - far * below[1]
    rights[-2] = rights[-2] + far * above[1]
    rights[-1] = rights[-1] + above[0]
    return twisted_solve(rights, pivots, 1.0 / 3.0)


def end_sums(cells):
    _, edge, _ = derivative_parts(16)
    total = edge[WIDTH - 1] * cells[0]
    for step in range(1, WIDTH):
        total = total + edge[WIDTH - 1 - step] * cells[step]
    return total, cells[0]


def smooth_source(cells):
    count = len(cells)
    coeffs = filter_coefficients()
    rights = []
    for step in range(count):
        total = coeffs[0] * cells[step]
        for offset in range(1, WIDTH + 1):
            around = [cells[i] for i in (step - offset, step + offset) if 0 <= i < count]
            around = around[0] + around[1] if len(around) == 2 else around[0]
            total = total + (0.5 * coeffs[offset]) * around
        rights.append(total)
    return rights


def smooth_solve(rights, below, above):
    count = len(rights)
    coeffs = filter_coefficients()
    rights = list(rights)
    for step in range(WIDTH):
        for cell in range(WIDTH - step):
            factor = 0.5 * coeffs[step + cell + 1]
            if step == 0 and cell == 0:
                factor = factor - 0.4
            rights[step] = rights[step] + factor * below[cell]
            rights[count - 1 - step] = rights[count - 1 - step] + factor * above[cell]
    pivots = [1.0]
    for _ in range(count):
        pivots.append(1.0 - 0.16 / pivots[-1])
    return twisted_solve(rights, pivots, 0.4)


def split_values(values):
    high = values.astype(jnp.bfloat16)
    low = (values - high.astype(jnp.float32)).astype(jnp.bfloat16)
    return jnp.concatenate([high, low], axis=1)


def split_weights(table):
    high = table.astype(jnp.bfloat16)
    low = (table - high.astype(jnp.float32)).astype(jnp.bfloat16)
    top = jnp.concatenate([high, low], axis=1)
    return jnp.concatenate([top, jnp.concatenate([high, jnp.zeros_like(low)], axis=1)], axis=0)


def lane_product(values, weights):
    both = jnp.dot(split_values(values), weights, preferred_element_type=jnp.float32)
    return both[:, :LANES] + both[:, LANES:]


class Grid:
    def __init__(self, nx, ny):
        self.nx, self.ny, self.rows = nx, ny, nx * ny
        self.eta_groups = ny // TILE
        self.xi_groups = nx // TILE

    def xi_tile(self, position, group):
        return pl.ds(position * self.ny + group * TILE, TILE)

    def eta_tile(self, position, group):
        return pl.ds(position + group * TILE * self.ny, TILE, stride=self.ny)

    def eta_major(self, position, group):
        return pl.ds(position * self.nx + group * TILE, TILE)


def group_rows(group):
    return pl.ds(group * TILE, TILE)


def odd(axis):
    return lax.rem(lax.axis_index(axis), 2) == 1


def send_sums(read, groups, count, flag, first_ref, second_ref, field):
    for group in range(groups):
        top = end_sums([read(count - 1 - step, group) for step in range(WIDTH)])
        low = end_sums([read(step, group) for step in range(WIDTH)])
        low = (-low[0], low[1])
        for part in range(2):
            first_ref[2 * field + part, group_rows(group), :] = jnp.where(flag, low[part], top[part])
            second_ref[2 * field + part, group_rows(group), :] = jnp.where(flag, top[part], low[part])


def take_sums(first_ref, second_ref, flag, field, group):
    below, above = [], []
    for part in range(2):
        first = first_ref[2 * field + part, group_rows(group), :]
        second = second_ref[2 * field + part, group_rows(group), :]
        below.append(jnp.where(flag, first, second))
        above.append(jnp.where(flag, second, first))
    return below, above


def pack_sums(values, weights, grid):
    sums = lane_product(values, weights)
    packed = None
    for group in range(grid.rows // TILE):
        part = sums[group * TILE : (group + 1) * TILE]
        if group:
            part = pltpu.roll(part, 4 * group, axis=1)
        packed = part if packed is None else packed + part
    return packed


def unpack_sums(below, above, grid):
    lane = lax.broadcasted_iota(jnp.int32, below.shape, 1)
    packed = jnp.where(lax.rem(lane, 4) < 2, below, above)
    parts = [packed]
    for group in range(1, grid.rows // TILE):
        parts.append(pltpu.roll(packed, LANES - 4 * group, axis=1))
    return jnp.concatenate(parts, axis=0)


def primitive_kernel(
    grid,
    u_hbm, tables_hbm,
    u_ref, tables_ref, prim_ref, eta_first, eta_second, xi_first, xi_second, zeta_ref,
    tables_sem, u_sems,
):
    chunks = u_sems.shape[0]
    step = grid.rows // chunks
    copies = []
    for index in range(chunks):
        rows = pl.ds(index * step, step)
        for field in range(5):
            copy = pltpu.make_async_copy(
                u_hbm.at[field, rows, :], u_ref.at[field, rows, :], u_sems.at[index, field]
            )
            copy.start()
            copies.append(copy)
    weights = pltpu.make_async_copy(tables_hbm, tables_ref, tables_sem)
    weights.start()
    for index in range(chunks):
        for copy in copies[5 * index : 5 * index + 5]:
            copy.wait()
        rows = pl.ds(index * step, step)
        inverse = 1.0 / u_ref[0, rows, :]
        work = None
        for c in range(3):
            momentum = u_ref[1 + c, rows, :]
            speed = momentum * inverse
            prim_ref[c, rows, :] = speed
            work = momentum * speed if work is None else work + momentum * speed
        pressure = 0.4 * (u_ref[4, rows, :] - 0.5 * work)
        prim_ref[3, rows, :] = pressure * inverse
    for field in range(4):
        send_sums(
            lambda position, group: prim_ref[field, grid.eta_tile(position, group), :],
            grid.xi_groups, grid.ny, odd("eta"), eta_first, eta_second, field,
        )
        send_sums(
            lambda position, group: prim_ref[field, grid.xi_tile(position, group), :],
            grid.eta_groups, grid.nx, odd("xi"), xi_first, xi_second, field,
        )
    weights.wait()
    sums = split_weights(tables_ref[SUMS])
    for field in range(4):
        zeta_ref[field] = pack_sums(prim_ref[field], sums, grid)


def fetch_kernel(count, *refs):
    sources, results, sems = refs[:count], refs[count + 1 : 2 * count + 1], refs[-1]
    copies = [
        pltpu.make_async_copy(source, result, sems.at[index])
        for index, (source, result) in enumerate(zip(sources, results))
    ]
    for copy in copies:
        copy.start()
    for copy in copies:
        copy.wait()


def derive_source_kernel(grid, fields, value_ref, tables_ref, xi_ref, eta_ref, zeta_ref):
    parts = [value_ref.at[k] for k in range(3)] if len(value_ref.shape) == 4 else [value_ref] * 3
    xi_value, eta_value, zeta_value = parts
    derive = split_weights(tables_ref[DERIVE])
    for field in range(fields):
        zeta_ref[field] = lane_product(zeta_value[field], derive)
        for group in range(grid.eta_groups):
            cells = [xi_value[field, grid.xi_tile(i, group), :] for i in range(grid.nx)]
            for i, value in enumerate(derive_source(cells)):
                xi_ref[field, grid.xi_tile(i, group), :] = value
        for group in range(grid.xi_groups):
            cells = [eta_value[field, grid.eta_tile(i, group), :] for i in range(grid.ny)]
            for i, value in enumerate(derive_source(cells)):
                eta_ref[field, grid.eta_major(i, group), :] = value


def xi_derivative(grid, source_ref, xi_a, xi_b, field, group):
    below, above = take_sums(xi_a, xi_b, odd("xi"), field, group)
    rights = [source_ref[field, grid.xi_tile(i, group), :] for i in range(grid.nx)]
    return derive_solve(rights, below, above)


def eta_derivative(grid, source_ref, eta_a, eta_b, field, group):
    below, above = take_sums(eta_a, eta_b, odd("eta"), field, group)
    rights = [source_ref[field, grid.eta_major(i, group), :] for i in range(grid.ny)]
    return derive_solve(rights, below, above)


def slope_kernel(grid, xi_source, eta_source, eta_a, eta_b, xi_a, xi_b, slope_ref):
    for field in range(4):
        for group in range(grid.eta_groups):
            for i, value in enumerate(xi_derivative(grid, xi_source, xi_a, xi_b, field, group)):
                slope_ref[0, field, grid.xi_tile(i, group), :] = value
        for group in range(grid.xi_groups):
            for i, value in enumerate(eta_derivative(grid, eta_source, eta_a, eta_b, field, group)):
                slope_ref[1, field, grid.eta_tile(i, group), :] = value


def flux_kernel(
    grid,
    u_ref, prim_ref, metrics_ref, jacobian_ref, slope_ref, own_ref, zeta_below, zeta_above, tables_ref,
    contra_ref, eta_first, eta_second, xi_first, xi_second, zeta_ref,
    zeta_slope_ref,
):
    back, sums = split_weights(tables_ref[BACK]), split_weights(tables_ref[SUMS])
    for field in range(4):
        halo = unpack_sums(zeta_below[field], zeta_above[field], grid)
        zeta_slope_ref[field] = own_ref[field] + lane_product(halo, back)

    step = TILE

    def body(index, carry):
        rows = pl.ds(pl.multiple_of(index * step, step), step)
        u = [u_ref[c, rows, :] for c in range(5)]
        speed = [prim_ref[c, rows, :] for c in range(3)]
        pressure = prim_ref[3, rows, :] * u[0]
        metrics = [[metrics_ref[3 * k + j, rows, :] for j in range(3)] for k in range(3)]
        scaled = (viscosity * jacobian_ref[rows, :])
        scaled = [[scaled * metrics[k][j] for j in range(3)] for k in range(3)]
        physical = []
        for c in range(4):
            slopes = [slope_ref[0, c, rows, :], slope_ref[1, c, rows, :], zeta_slope_ref[c, rows, :]]
            physical.append(
                [
                    scaled[0][j] * slopes[0] + scaled[1][j] * slopes[1] + scaled[2][j] * slopes[2]
                    for j in range(3)
                ]
            )
        spread = (2.0 / 3.0) * (physical[0][0] + physical[1][1] + physical[2][2])
        stress = [[None] * 3 for _ in range(3)]
        momentum = [[None] * 3 for _ in range(3)]
        for c in range(3):
            stress[c][c] = (physical[c][c] + physical[c][c]) - spread
            momentum[c][c] = (u[1 + c] * speed[c] + pressure) - stress[c][c]
            for j in range(c):
                stress[c][j] = stress[j][c] = physical[c][j] + physical[j][c]
                momentum[c][j] = momentum[j][c] = u[1 + c] * speed[j] - stress[c][j]
        total = u[4] + pressure
        fluxes = []
        for j in range(3):
            worked = speed[0] * stress[0][j] + speed[1] * stress[1][j] + speed[2] * stress[2][j]
            energy = (total * speed[j] - worked) - (conduction / viscosity) * physical[3][j]
            fluxes.append([u[1 + j], momentum[0][j], momentum[1][j], momentum[2][j], energy])
        for k in range(3):
            for f in range(5):
                contra_ref[k, f, rows, :] = (
                    metrics[k][0] * fluxes[0][f]
                    + metrics[k][1] * fluxes[1][f]
                    + metrics[k][2] * fluxes[2][f]
                )
        return carry

    lax.fori_loop(0, grid.rows // step, body, 0, unroll=4)
    for field in range(5):
        send_sums(
            lambda position, group: contra_ref[1, field, grid.eta_tile(position, group), :],
            grid.xi_groups, grid.ny, odd("eta"), eta_first, eta_second, field,
        )
        send_sums(
            lambda position, group: contra_ref[0, field, grid.xi_tile(position, group), :],
            grid.eta_groups, grid.nx, odd("xi"), xi_first, xi_second, field,
        )
        zeta_ref[field] = pack_sums(contra_ref[2, field], sums, grid)


def divergence_kernel(grid, xi_source, eta_source, own_ref, eta_a, eta_b, xi_a, xi_b, total_ref):
    for field in range(5):
        for group in range(grid.xi_groups):
            for i, value in enumerate(eta_derivative(grid, eta_source, eta_a, eta_b, field, group)):
                rows = grid.eta_tile(i, group)
                total_ref[field, rows, :] = own_ref[field, rows, :] + value
        for group in range(grid.eta_groups):
            for i, value in enumerate(xi_derivative(grid, xi_source, xi_a, xi_b, field, group)):
                rows = grid.xi_tile(i, group)
                total_ref[field, rows, :] = total_ref[field, rows, :] + value


def step_kernel(
    grid,
    u_ref, jacobian_ref, total_ref, zeta_below, zeta_above, tables_ref,
    state_ref, eta_first, eta_second,
):
    back = split_weights(tables_ref[BACK])
    scale = step_duration * jacobian_ref[...]
    for field in range(5):
        halo = unpack_sums(zeta_below[field], zeta_above[field], grid)
        total = total_ref[field] + lane_product(halo, back)
        state_ref[field] = u_ref[field] - scale * total
        send_cells(
            lambda position, group: state_ref[field, grid.eta_tile(position, group), :],
            grid.xi_groups, grid.ny, odd("eta"), eta_first, eta_second, field,
        )


def send_cells(read, groups, count, flag, first_ref, second_ref, field):
    for group in range(groups):
        for step in range(WIDTH):
            low = read(step, group)
            top = read(count - 1 - step, group)
            index = WIDTH * field + step
            first_ref[index, group_rows(group), :] = jnp.where(flag, low, top)
            second_ref[index, group_rows(group), :] = jnp.where(flag, top, low)


def take_cells(first_ref, second_ref, flag, field, group):
    below, above = [], []
    for step in range(WIDTH):
        first = first_ref[WIDTH * field + step, group_rows(group), :]
        second = second_ref[WIDTH * field + step, group_rows(group), :]
        below.append(jnp.where(flag, first, second))
        above.append(jnp.where(flag, second, first))
    return below, above


def eta_source_kernel(grid, state_ref, source_ref):
    for field in range(5):
        for group in range(grid.xi_groups):
            cells = [state_ref[field, grid.eta_tile(i, group), :] for i in range(grid.ny)]
            for i, value in enumerate(smooth_source(cells)):
                source_ref[field, grid.eta_major(i, group), :] = value


def xi_source_kernel(grid, state_ref, source_ref):
    for field in range(5):
        for group in range(grid.eta_groups):
            cells = [state_ref[field, grid.xi_tile(i, group), :] for i in range(grid.nx)]
            for i, value in enumerate(smooth_source(cells)):
                source_ref[field, grid.xi_tile(i, group), :] = value


def eta_filter_kernel(
    grid, source_ref, eta_a, eta_b, result_ref, xi_first, xi_second, zeta_ref, edge_first, edge_second
):
    for field in range(5):
        for group in range(grid.xi_groups):
            below, above = take_cells(eta_a, eta_b, odd("eta"), field, group)
            rights = [source_ref[field, grid.eta_major(i, group), :] for i in range(grid.ny)]
            for i, value in enumerate(smooth_solve(rights, below, above)):
                result_ref[field, grid.eta_tile(i, group), :] = value
    flag = odd("xi")
    for field in range(5):
        send_cells(
            lambda position, group: result_ref[field, grid.xi_tile(position, group), :],
            grid.eta_groups, grid.nx, flag, xi_first, xi_second, field,
        )
    lane = lax.broadcasted_iota(jnp.int32, (TILE, LANES), 1)
    for position in range(grid.nx):
        packed = None
        for slot in range(5 * grid.eta_groups):
            field, group = slot // grid.eta_groups, slot % grid.eta_groups
            part = result_ref[field, grid.xi_tile(position, group), :]
            part = pltpu.roll(part, WIDTH * (2 * slot + 1), axis=1)
            packed = part if packed is None else jnp.where(lane >= 2 * WIDTH * slot, part, packed)
        zeta_ref[group_rows(position), :] = packed
    send_cells(
        lambda position, group: zeta_ref[group_rows(position), :],
        1, grid.nx, flag, edge_first, edge_second, 0,
    )


def xi_filter_kernel(grid, source_ref, xi_a, xi_b, tables_ref, result_ref):
    smooth = split_weights(tables_ref[SMOOTH])
    flag = odd("xi")
    for field in range(5):
        for group in range(grid.eta_groups):
            below, above = take_cells(xi_a, xi_b, flag, field, group)
            rights = [source_ref[field, grid.xi_tile(i, group), :] for i in range(grid.nx)]
            for i, value in enumerate(smooth_solve(rights, below, above)):
                result_ref[field, grid.xi_tile(i, group), :] = value
        result_ref[field] = lane_product(result_ref[field], smooth)


def zeta_filter_kernel(
    grid,
    state_ref, below_ref, above_ref, a_below, a_above, b_below, b_above, tables_ref,
    result_hbm,
    result_ref, sems,
):
    ends = split_weights(tables_ref[ENDS])
    flag = odd("xi")
    lane = lax.broadcasted_iota(jnp.int32, (TILE, LANES), 1)
    from_below = lax.rem(lane, 2 * WIDTH) < WIDTH

    def merge(below, above, index):
        return jnp.where(from_below, below[group_rows(index), :], above[group_rows(index), :])

    low, high = [], []
    for step in range(WIDTH):
        first, second = merge(a_below, a_above, step), merge(b_below, b_above, step)
        low.append(jnp.where(flag, first, second))
        high.append(jnp.where(flag, second, first))
    cells = [merge(below_ref, above_ref, position) for position in range(grid.nx)]
    cells = smooth_solve(smooth_source(cells), low, high)
    copies = []
    for field in range(5):
        parts = []
        for packed in cells:
            for group in range(grid.eta_groups):
                slot = field * grid.eta_groups + group
                parts.append(pltpu.roll(packed, LANES - 2 * WIDTH * slot, axis=1) if slot else packed)
        halo = jnp.concatenate(parts, axis=0)
        result_ref[field] = state_ref[field] + lane_product(halo, ends)
        copy = pltpu.make_async_copy(result_ref.at[field], result_hbm.at[field], sems.at[field])
        copy.start()
        copies.append(copy)
    for copy in copies:
        copy.wait()


def pair_swap(value, axis, parity):
    count = lax.axis_size(axis)
    pairs = []
    for index in range(count):
        step = 1 if index % 2 == parity else -1
        pairs.append((index, (index + step) % count))
    return lax.ppermute(value, axis, pairs)


def diagonal_swap(value, parity):
    nx, nz = lax.axis_size("xi"), lax.axis_size("zeta")

    def send(shift):
        pairs = []
        for i in range(nx):
            partner = (i + (1 if i % 2 == parity else -1)) % nx
            for k in range(nz):
                pairs.append((i * nz + k, partner * nz + (k + shift) % nz))
        return lax.ppermute(value, ("xi", "zeta"), pairs)

    below = send(1)
    return (below, below) if nz == 2 else (below, send(-1))


def ring_swap(value, axis):
    count = lax.axis_size(axis)
    if count == 2:
        other = lax.ppermute(value, axis, [(0, 1), (1, 0)])
        return other, other
    up = [(index, (index + 1) % count) for index in range(count)]
    down = [(index, (index - 1) % count) for index in range(count)]
    return lax.ppermute(value, axis, up), lax.ppermute(value, axis, down)


HBM = pltpu.MemorySpace.HBM


def call(kernel, outs, *operands, scratch=(), cost=1.0, far=(), far_outs=()):
    shapes = [
        out if isinstance(out, jax.ShapeDtypeStruct) else jax.ShapeDtypeStruct(out, jnp.float32)
        for out in outs
    ]
    near = pltpu.MemorySpace.VMEM
    operands = [
        pltpu.with_memory_space_constraint(value, HBM) if index in far else value
        for index, value in enumerate(operands)
    ]
    return pl.pallas_call(
        kernel,
        out_shape=shapes,
        in_specs=[
            pl.BlockSpec(memory_space=HBM if index in far else near) for index in range(len(operands))
        ],
        out_specs=[
            pl.BlockSpec(memory_space=HBM if index in far_outs else near) for index in range(len(outs))
        ],
        scratch_shapes=scratch,
        cost_estimate=pl.CostEstimate(flops=0, transcendentals=0, bytes_accessed=int(cost * 3.6e6)),
        compiler_params=pltpu.CompilerParams(vmem_limit_bytes=20 * 2**20),
    )(*operands)


def like(value):
    return jax.ShapeDtypeStruct(value.shape, value.dtype)


def local(conserved_solution, metrics, jacobian):
    _, nx, ny, nz = conserved_solution.shape
    grid = Grid(nx, ny)
    rows = grid.rows
    u = conserved_solution.reshape(5, rows, nz)
    metrics = metrics.reshape(9, rows, nz)
    jacobian = jacobian.reshape(rows, nz)
    tables = jnp.asarray(zeta_tables(nz))

    def exchange(eta_first, eta_second, xi_first, xi_second, zeta):
        eta_b = pair_swap(eta_second, "eta", 1)
        eta_a = pair_swap(eta_first, "eta", 0)
        xi_b = pair_swap(xi_second, "xi", 1)
        below, above = ring_swap(zeta, "zeta")
        xi_a = pair_swap(xi_first, "xi", 0)
        return (eta_a, eta_b, xi_a, xi_b), (below, above)

    def sums_shapes(fields):
        return [(2 * fields, nx, nz)] * 2 + [(2 * fields, ny, nz)] * 2 + [(fields, TILE, LANES)]

    chunks = 2
    u, tables, prim, *sends = call(
        functools.partial(primitive_kernel, grid),
        [like(u), like(tables), (4, rows, nz)] + sums_shapes(4),
        u, tables,
        scratch=[pltpu.SemaphoreType.DMA, pltpu.SemaphoreType.DMA((chunks, 5))],
        far=(0, 1),
    )
    sides, ends = exchange(*sends)
    metrics, jacobian = call(
        functools.partial(fetch_kernel, 2),
        [like(metrics), like(jacobian)],
        metrics, jacobian, sends[-1],
        scratch=[pltpu.SemaphoreType.DMA((2,))],
        far=(0, 1),
    )
    xi_source, eta_source, own = call(
        functools.partial(derive_source_kernel, grid, 4),
        [(4, rows, nz)] * 3,
        prim, tables,
    )
    (slopes,) = call(
        functools.partial(slope_kernel, grid), [(2, 4, rows, nz)], xi_source, eta_source, *sides,
    )
    contra, *sends = call(
        functools.partial(flux_kernel, grid),
        [(3, 5, rows, nz)] + sums_shapes(5),
        u, prim, metrics, jacobian, slopes, own, *ends, tables,
        scratch=[pltpu.VMEM((4, rows, nz), jnp.float32)],
    )
    sides, ends = exchange(*sends)
    xi_source, eta_source, own = call(
        functools.partial(derive_source_kernel, grid, 5), [(5, rows, nz)] * 3, contra, tables,
    )
    (total,) = call(
        functools.partial(divergence_kernel, grid),
        [(5, rows, nz)],
        xi_source, eta_source, own, *sides,
    )
    state, eta_first, eta_second = call(
        functools.partial(step_kernel, grid),
        [(5, rows, nz)] + [(5 * WIDTH, nx, nz)] * 2,
        u, jacobian, total, *ends, tables,
    )
    eta_b = pair_swap(eta_second, "eta", 1)
    eta_a = pair_swap(eta_first, "eta", 0)
    (source,) = call(functools.partial(eta_source_kernel, grid), [(5, rows, nz)], state)
    state, xi_first, xi_second, zeta, edge_first, edge_second = call(
        functools.partial(eta_filter_kernel, grid),
        [(5, rows, nz)]
        + [(5 * WIDTH, ny, nz)] * 2
        + [(nx * TILE, LANES)]
        + [(WIDTH, TILE, LANES)] * 2,
        source, eta_a, eta_b,
    )
    xi_b = pair_swap(xi_second, "xi", 1)
    ends = ring_swap(zeta, "zeta")
    edges_b = diagonal_swap(edge_second, 1)
    edges_a = diagonal_swap(edge_first, 0)
    xi_a = pair_swap(xi_first, "xi", 0)
    (source,) = call(functools.partial(xi_source_kernel, grid), [(5, rows, nz)], state)
    (state,) = call(
        functools.partial(xi_filter_kernel, grid), [(5, rows, nz)], source, xi_a, xi_b, tables,
    )
    edges = [edge.reshape(WIDTH * TILE, LANES) for edge in (*edges_a, *edges_b)]
    (result,) = call(
        functools.partial(zeta_filter_kernel, grid),
        [(5, rows, nz)],
        state, *ends, *edges, tables,
        scratch=[pltpu.VMEM((5, rows, nz), jnp.float32), pltpu.SemaphoreType.DMA((5,))],
        far_outs=(0,),
    )
    return result.reshape(5, nx, ny, nz)


def solution(mesh):
    in_specs = (
        P(None, "xi", "eta", "zeta"),
        P(None, None, "xi", "eta", "zeta"),
        P("xi", "eta", "zeta"),
    )
    out_specs = P(None, "xi", "eta", "zeta")
    return jax.shard_map(local, mesh=mesh, in_specs=in_specs, out_specs=out_specs, check_vma=False)
```

```python
import functools

import jax
import jax.numpy as jnp
import numpy as np
from jax import lax
from jax.experimental import pallas as pl
from jax.experimental.pallas import tpu as pltpu
from jax.sharding import PartitionSpec as P

WIDTH = 5
LANES = 128
TILE = 8

viscosity = 0.15
conduction = 0.15 * 1.4 / (0.4 * 0.72)
step_duration = 0.08


def derivative_system(length):
    extent = length + 2 * WIDTH
    system = np.eye(extent)
    source = np.zeros((extent, extent))
    for position in range(2, extent - 2):
        system[position, position - 1] = 1.0 / 3.0
        system[position, position + 1] = 1.0 / 3.0
        source[position, position + 1] = 7.0 / 9.0
        source[position, position - 1] = -7.0 / 9.0
        source[position, position + 2] = 1.0 / 36.0
        source[position, position - 2] = -1.0 / 36.0
    source[1, 2] = 0.5
    source[1, 0] = -0.5
    source[extent - 2, extent - 1] = 0.5
    source[extent - 2, extent - 3] = -0.5
    source[0, 1] = 1.0
    source[0, 0] = -1.0
    source[extent - 1, extent - 1] = 1.0
    source[extent - 1, extent - 2] = -1.0
    return system, source


def filter_coefficients():
    strength = 0.4
    return [
        (193.0 + 126.0 * strength) / 256.0,
        (105.0 + 302.0 * strength) / 256.0,
        15.0 * (2.0 * strength - 1.0) / 64.0,
        45.0 * (1.0 - 2.0 * strength) / 512.0,
        5.0 * (2.0 * strength - 1.0) / 256.0,
        (1.0 - 2.0 * strength) / 512.0,
    ]


def filter_system(length):
    strength = 0.4
    coeffs = filter_coefficients()
    extent = length + 2 * WIDTH
    system = np.eye(extent)
    source = np.eye(extent)
    for position in range(5, extent - 5):
        system[position, position - 1] = strength
        system[position, position + 1] = strength
        source[position, position] = coeffs[0]
        for offset in range(1, 6):
            source[position, position + offset] = coeffs[offset] / 2.0
            source[position, position - offset] = coeffs[offset] / 2.0
    return system, source


def own_rows(system, source, length):
    return np.linalg.solve(system, source)[WIDTH : WIDTH + length]


def derivative_parts(length):
    system, source = derivative_system(length)
    halo = np.linalg.solve(system[:WIDTH, :WIDTH], source[:WIDTH])
    row = source[WIDTH] - system[WIDTH, WIDTH - 1] * halo[WIDTH - 1]
    pivots = [1.0]
    for position in range(3, WIDTH + length):
        pivots.append(1.0 - 1.0 / 9.0 / pivots[-1])
    return pivots[WIDTH - 2 :], row[:WIDTH], row[WIDTH : WIDTH + 3]


def pad_rows(table):
    return np.concatenate([table, np.zeros((LANES - table.shape[0], table.shape[1]))], axis=0)


def pad_columns(table):
    return np.concatenate([table, np.zeros((table.shape[0], LANES - table.shape[1]))], axis=1)


def zeta_tables(length):
    system, source = derivative_system(length)
    table = own_rows(system, source, length)
    _, edge, _ = derivative_parts(length)
    inverse = np.linalg.inv(system)
    extent = length + 2 * WIDTH
    sums = np.zeros((length, 4))
    sums[length - WIDTH :, 0] = edge
    sums[length - 1, 1] = 1.0
    sums[:WIDTH, 2] = -edge[::-1]
    sums[0, 3] = 1.0
    own = slice(WIDTH, WIDTH + length)
    back = np.stack(
        [
            inverse[own, WIDTH],
            -1.0 / 36.0 * inverse[own, WIDTH + 1],
            inverse[own, extent - WIDTH - 1],
            1.0 / 36.0 * inverse[own, extent - WIDTH - 2],
        ]
    )
    smooth = own_rows(*filter_system(length), length)
    ends = np.concatenate([smooth[:, :WIDTH], smooth[:, WIDTH + length :]], axis=1)
    tables = [table[:, own].T, pad_columns(sums), pad_rows(back), smooth[:, own].T, pad_rows(ends.T)]
    return np.stack(tables).astype(np.float32)


DERIVE, SUMS, BACK, SMOOTH, ENDS = range(5)


def twisted_solve(rights, pivots, off):
    count = len(rights)
    half = count // 2
    low = [rights[0]]
    high = [rights[count - 1]]
    for step in range(1, half):
        factor = off / pivots[step - 1]
        low.append(rights[step] - factor * low[-1])
        high.append(rights[count - 1 - step] - factor * high[-1])
    middle = pivots[half - 1]
    det = middle * middle - off * off
    first, second = low[-1], high[-1]
    answer = [None] * count
    answer[half - 1] = (middle / det) * first - (off / det) * second
    answer[half] = (middle / det) * second - (off / det) * first
    for step in range(half - 2, -1, -1):
        scale = 1.0 / pivots[step]
        factor = off / pivots[step]
        answer[step] = scale * low[step] - factor * answer[step + 1]
        answer[count - 1 - step] = scale * high[step] - factor * answer[count - 2 - step]
    return answer


def derive_source(cells):
    count = len(cells)
    _, _, edge = derivative_parts(count)
    near, far = 7.0 / 9.0, 1.0 / 36.0
    rights = [None] * count
    rights[0] = edge[0] * cells[0] + edge[1] * cells[1] + edge[2] * cells[2]
    rights[1] = near * (cells[2] - cells[0]) + far * cells[3]
    for step in range(2, count - 2):
        rights[step] = near * (cells[step + 1] - cells[step - 1]) + far * (
            cells[step + 2] - cells[step - 2]
        )
    rights[count - 2] = near * (cells[count - 1] - cells[count - 3]) - far * cells[count - 4]
    rights[count - 1] = -(
        edge[0] * cells[count - 1] + edge[1] * cells[count - 2] + edge[2] * cells[count - 3]
    )
    return rights


def derive_solve(rights, below, above):
    pivots, _, _ = derivative_parts(len(rights))
    rights = list(rights)
    far = 1.0 / 36.0
    rights[0] = rights[0] + below[0]
    rights[1] = rights[1] - far * below[1]
    rights[-2] = rights[-2] + far * above[1]
    rights[-1] = rights[-1] + above[0]
    return twisted_solve(rights, pivots, 1.0 / 3.0)


def end_sums(cells):
    _, edge, _ = derivative_parts(16)
    total = edge[WIDTH - 1] * cells[0]
    for step in range(1, WIDTH):
        total = total + edge[WIDTH - 1 - step] * cells[step]
    return total, cells[0]


def smooth_source(cells):
    count = len(cells)
    coeffs = filter_coefficients()
    rights = []
    for step in range(count):
        total = coeffs[0] * cells[step]
        for offset in range(1, WIDTH + 1):
            around = [cells[i] for i in (step - offset, step + offset) if 0 <= i < count]
            around = around[0] + around[1] if len(around) == 2 else around[0]
            total = total + (0.5 * coeffs[offset]) * around
        rights.append(total)
    return rights


def smooth_solve(rights, below, above):
    count = len(rights)
    coeffs = filter_coefficients()
    rights = list(rights)
    for step in range(WIDTH):
        for cell in range(WIDTH - step):
            factor = 0.5 * coeffs[step + cell + 1]
            if step == 0 and cell == 0:
                factor = factor - 0.4
            rights[step] = rights[step] + factor * below[cell]
            rights[count - 1 - step] = rights[count - 1 - step] + factor * above[cell]
    pivots = [1.0]
    for _ in range(count):
        pivots.append(1.0 - 0.16 / pivots[-1])
    return twisted_solve(rights, pivots, 0.4)


def split_values(values):
    high = values.astype(jnp.bfloat16)
    low = (values - high.astype(jnp.float32)).astype(jnp.bfloat16)
    return jnp.concatenate([high, low], axis=1)


def split_weights(table):
    high = table.astype(jnp.bfloat16)
    low = (table - high.astype(jnp.float32)).astype(jnp.bfloat16)
    top = jnp.concatenate([high, low], axis=1)
    return jnp.concatenate([top, jnp.concatenate([high, jnp.zeros_like(low)], axis=1)], axis=0)


def lane_product(values, weights):
    both = jnp.dot(split_values(values), weights, preferred_element_type=jnp.float32)
    return both[:, :LANES] + both[:, LANES:]


class Grid:
    def __init__(self, nx, ny):
        self.nx, self.ny, self.rows = nx, ny, nx * ny
        self.eta_groups = ny // TILE
        self.xi_groups = nx // TILE

    def xi_tile(self, position, group):
        return pl.ds(position * self.ny + group * TILE, TILE)

    def eta_tile(self, position, group):
        return pl.ds(position + group * TILE * self.ny, TILE, stride=self.ny)

    def eta_major(self, position, group):
        return pl.ds(position * self.nx + group * TILE, TILE)


def group_rows(group):
    return pl.ds(group * TILE, TILE)


def odd(axis):
    return lax.rem(lax.axis_index(axis), 2) == 1


def send_sums(read, groups, count, flag, first_ref, second_ref, field):
    for group in range(groups):
        top = end_sums([read(count - 1 - step, group) for step in range(WIDTH)])
        low = end_sums([read(step, group) for step in range(WIDTH)])
        low = (-low[0], low[1])
        for part in range(2):
            first_ref[2 * field + part, group_rows(group), :] = jnp.where(flag, low[part], top[part])
            second_ref[2 * field + part, group_rows(group), :] = jnp.where(flag, top[part], low[part])


def take_sums(first_ref, second_ref, flag, field, group):
    below, above = [], []
    for part in range(2):
        first = first_ref[2 * field + part, group_rows(group), :]
        second = second_ref[2 * field + part, group_rows(group), :]
        below.append(jnp.where(flag, first, second))
        above.append(jnp.where(flag, second, first))
    return below, above


def pack_sums(values, weights, grid):
    sums = lane_product(values, weights)
    parts = []
    for group in range(grid.rows // TILE):
        part = sums[group * TILE : (group + 1) * TILE]
        parts.append(pltpu.roll(part, 4 * group, axis=1) if group else part)
    while len(parts) > 1:
        parts = [sum(parts[i + 1 : i + 2], parts[i]) for i in range(0, len(parts), 2)]
    return parts[0]


def unpack_sums(below, above, grid):
    lane = lax.broadcasted_iota(jnp.int32, below.shape, 1)
    packed = jnp.where(lax.rem(lane, 4) < 2, below, above)
    parts = [packed]
    for group in range(1, grid.rows // TILE):
        parts.append(pltpu.roll(packed, LANES - 4 * group, axis=1))
    return jnp.concatenate(parts, axis=0)


def primitive_kernel(
    grid,
    u_hbm, tables_hbm, metrics_hbm, jacobian_hbm,
    u_ref, tables_ref, metrics_ref, jacobian_ref,
    prim_ref, mass_ref, eta_first, eta_second, xi_first, xi_second, zeta_ref,
    u_sems, late_sems,
):
    chunks = u_sems.shape[0]
    step = grid.rows // chunks
    copies = []
    for index in range(chunks):
        rows = pl.ds(index * step, step)
        for field in range(5):
            copy = pltpu.make_async_copy(
                u_hbm.at[field, rows, :], u_ref.at[field, rows, :], u_sems.at[index, field]
            )
            copy.start()
            copies.append(copy)
    late = [
        pltpu.make_async_copy(source, result, late_sems.at[index])
        for index, (source, result) in enumerate(
            [(tables_hbm, tables_ref)]
            + [(metrics_hbm.at[k], metrics_ref.at[k]) for k in range(9)]
            + [(jacobian_hbm, jacobian_ref)]
        )
    ]
    for copy in late:
        copy.start()
    for index in range(chunks):
        for copy in copies[5 * index : 5 * index + 5]:
            copy.wait()
        rows = pl.ds(index * step, step)
        inverse = 1.0 / u_ref[0, rows, :]
        work = None
        for c in range(3):
            momentum = u_ref[1 + c, rows, :]
            speed = momentum * inverse
            prim_ref[c, rows, :] = speed
            work = momentum * speed if work is None else work + momentum * speed
        pressure = 0.4 * (u_ref[4, rows, :] - 0.5 * work)
        prim_ref[3, rows, :] = pressure * inverse

    def send(xi_value, eta_value, field):
        send_sums(
            lambda position, group: eta_value[grid.eta_tile(position, group), :],
            grid.xi_groups, grid.ny, odd("eta"), eta_first, eta_second, field,
        )
        send_sums(
            lambda position, group: xi_value[grid.xi_tile(position, group), :],
            grid.eta_groups, grid.nx, odd("xi"), xi_first, xi_second, field,
        )

    for field in range(4):
        send(prim_ref.at[field], prim_ref.at[field], field)
    for copy in late:
        copy.wait()
    for k in range(3):
        for index in range(chunks):
            rows = pl.ds(index * step, step)
            mass_ref[k, rows, :] = (
                metrics_ref[3 * k, rows, :] * u_ref[1, rows, :]
                + metrics_ref[3 * k + 1, rows, :] * u_ref[2, rows, :]
                + metrics_ref[3 * k + 2, rows, :] * u_ref[3, rows, :]
            )
    send(mass_ref.at[0], mass_ref.at[1], 4)
    sums = split_weights(tables_ref[SUMS])
    for field in range(5):
        values = prim_ref[field] if field < 4 else mass_ref[2]
        zeta_ref[field] = pack_sums(values, sums, grid)


def derive_sources(grid, xi_value, eta_value, zeta_value, derive, field, xi_ref, eta_ref, zeta_ref):
    zeta_ref[field] = lane_product(zeta_value[...], derive)
    for group in range(grid.eta_groups):
        cells = [xi_value[grid.xi_tile(i, group), :] for i in range(grid.nx)]
        for i, value in enumerate(derive_source(cells)):
            xi_ref[field, grid.xi_tile(i, group), :] = value
    for group in range(grid.xi_groups):
        cells = [eta_value[grid.eta_tile(i, group), :] for i in range(grid.ny)]
        for i, value in enumerate(derive_source(cells)):
            eta_ref[field, grid.eta_major(i, group), :] = value


def primitive_source_kernel(grid, prim_ref, mass_ref, tables_ref, *results):
    derive = split_weights(tables_ref[DERIVE])
    for field in range(4):
        derive_sources(grid, *[prim_ref.at[field]] * 3, derive, field, *results)
    derive_sources(grid, *[mass_ref.at[k] for k in range(3)], derive, 4, *results)


def contra_source_kernel(grid, contra_ref, tables_ref, *results):
    derive = split_weights(tables_ref[DERIVE])
    for field in range(4):
        derive_sources(grid, *[contra_ref.at[k, field] for k in range(3)], derive, field, *results)


def xi_derivative(grid, source_ref, xi_a, xi_b, field, group):
    below, above = take_sums(xi_a, xi_b, odd("xi"), field, group)
    rights = [source_ref[field, grid.xi_tile(i, group), :] for i in range(grid.nx)]
    return derive_solve(rights, below, above)


def eta_derivative(grid, source_ref, eta_a, eta_b, field, group):
    below, above = take_sums(eta_a, eta_b, odd("eta"), field, group)
    rights = [source_ref[field, grid.eta_major(i, group), :] for i in range(grid.ny)]
    return derive_solve(rights, below, above)


def add_derivatives(grid, xi_source, eta_source, own_ref, eta_a, eta_b, xi_a, xi_b, field, total_ref):
    for group in range(grid.xi_groups):
        for i, value in enumerate(eta_derivative(grid, eta_source, eta_a, eta_b, field, group)):
            rows = grid.eta_tile(i, group)
            total_ref[rows, :] = own_ref[field, rows, :] + value
    for group in range(grid.eta_groups):
        for i, value in enumerate(xi_derivative(grid, xi_source, xi_a, xi_b, field, group)):
            rows = grid.xi_tile(i, group)
            total_ref[rows, :] = total_ref[rows, :] + value


def slope_kernel(grid, xi_source, eta_source, own_ref, eta_a, eta_b, xi_b, xi_a, slope_ref, mass_total_ref):
    for field in range(4):
        for group in range(grid.eta_groups):
            for i, value in enumerate(xi_derivative(grid, xi_source, xi_a, xi_b, field, group)):
                slope_ref[0, field, grid.xi_tile(i, group), :] = value
        for group in range(grid.xi_groups):
            for i, value in enumerate(eta_derivative(grid, eta_source, eta_a, eta_b, field, group)):
                slope_ref[1, field, grid.eta_tile(i, group), :] = value
    add_derivatives(
        grid, xi_source, eta_source, own_ref, eta_a, eta_b, xi_a, xi_b, 4, mass_total_ref
    )


def flux_kernel(
    grid,
    u_ref, prim_ref, metrics_ref, jacobian_ref, slope_ref, own_ref, mass_total_ref,
    zeta_below, zeta_above, tables_ref,
    contra_ref, mass_ref, eta_first, eta_second, xi_first, xi_second, zeta_ref,
    zeta_slope_ref,
):
    back, sums = split_weights(tables_ref[BACK]), split_weights(tables_ref[SUMS])
    for field in range(4):
        halo = unpack_sums(zeta_below[field], zeta_above[field], grid)
        zeta_slope_ref[field] = own_ref[field] + lane_product(halo, back)
    halo = unpack_sums(zeta_below[4], zeta_above[4], grid)
    total = mass_total_ref[...] + lane_product(halo, back)
    mass_ref[...] = u_ref[0] - (step_duration * jacobian_ref[...]) * total
    send_cells(
        lambda position, group: mass_ref[grid.eta_tile(position, group), :],
        grid.xi_groups, grid.ny, odd("eta"), eta_first, eta_second, 2 * 4,
    )

    step = TILE

    def body(index, carry):
        rows = pl.ds(pl.multiple_of(index * step, step), step)
        u = [u_ref[c, rows, :] for c in range(5)]
        speed = [prim_ref[c, rows, :] for c in range(3)]
        pressure = prim_ref[3, rows, :] * u[0]
        metrics = [[metrics_ref[3 * k + j, rows, :] for j in range(3)] for k in range(3)]
        scaled = (viscosity * jacobian_ref[rows, :])
        scaled = [[scaled * metrics[k][j] for j in range(3)] for k in range(3)]
        physical = []
        for c in range(4):
            slopes = [slope_ref[0, c, rows, :], slope_ref[1, c, rows, :], zeta_slope_ref[c, rows, :]]
            physical.append(
                [
                    scaled[0][j] * slopes[0] + scaled[1][j] * slopes[1] + scaled[2][j] * slopes[2]
                    for j in range(3)
                ]
            )
        spread = (2.0 / 3.0) * (physical[0][0] + physical[1][1] + physical[2][2])
        stress = [[None] * 3 for _ in range(3)]
        momentum = [[None] * 3 for _ in range(3)]
        for c in range(3):
            stress[c][c] = (physical[c][c] + physical[c][c]) - spread
            momentum[c][c] = (u[1 + c] * speed[c] + pressure) - stress[c][c]
            for j in range(c):
                stress[c][j] = stress[j][c] = physical[c][j] + physical[j][c]
                momentum[c][j] = momentum[j][c] = u[1 + c] * speed[j] - stress[c][j]
        total = u[4] + pressure
        fluxes = []
        for j in range(3):
            worked = speed[0] * stress[0][j] + speed[1] * stress[1][j] + speed[2] * stress[2][j]
            energy = (total * speed[j] - worked) - (conduction / viscosity) * physical[3][j]
            fluxes.append([momentum[0][j], momentum[1][j], momentum[2][j], energy])
        for k in range(3):
            for f in range(4):
                contra_ref[k, f, rows, :] = (
                    metrics[k][0] * fluxes[0][f]
                    + metrics[k][1] * fluxes[1][f]
                    + metrics[k][2] * fluxes[2][f]
                )
        return carry

    lax.fori_loop(0, grid.rows // step, body, 0, unroll=4)
    for field in range(4):
        send_sums(
            lambda position, group: contra_ref[1, field, grid.eta_tile(position, group), :],
            grid.xi_groups, grid.ny, odd("eta"), eta_first, eta_second, field,
        )
        send_sums(
            lambda position, group: contra_ref[0, field, grid.xi_tile(position, group), :],
            grid.eta_groups, grid.nx, odd("xi"), xi_first, xi_second, field,
        )
        zeta_ref[field] = pack_sums(contra_ref[2, field], sums, grid)


def divergence_kernel(grid, xi_source, eta_source, own_ref, eta_a, eta_b, xi_b, xi_a, total_ref):
    for field in range(4):
        add_derivatives(
            grid, xi_source, eta_source, own_ref, eta_a, eta_b, xi_a, xi_b, field, total_ref.at[field]
        )


def step_kernel(
    grid,
    u_ref, jacobian_ref, total_ref, zeta_below, zeta_above, tables_ref,
    state_ref, eta_first, eta_second,
):
    back = split_weights(tables_ref[BACK])
    scale = step_duration * jacobian_ref[...]
    for field in range(4):
        halo = unpack_sums(zeta_below[field], zeta_above[field], grid)
        total = total_ref[field] + lane_product(halo, back)
        state_ref[field] = u_ref[1 + field] - scale * total
        send_cells(
            lambda position, group: state_ref[field, grid.eta_tile(position, group), :],
            grid.xi_groups, grid.ny, odd("eta"), eta_first, eta_second, WIDTH * field,
        )


def send_cells(read, groups, count, flag, first_ref, second_ref, base):
    for group in range(groups):
        for step in range(WIDTH):
            low = read(step, group)
            top = read(count - 1 - step, group)
            first_ref[base + step, group_rows(group), :] = jnp.where(flag, low, top)
            second_ref[base + step, group_rows(group), :] = jnp.where(flag, top, low)


def take_cells(first_ref, second_ref, flag, base, group):
    below, above = [], []
    for step in range(WIDTH):
        first = first_ref[base + step, group_rows(group), :]
        second = second_ref[base + step, group_rows(group), :]
        below.append(jnp.where(flag, first, second))
        above.append(jnp.where(flag, second, first))
    return below, above


def eta_sources(grid, state_ref, source_ref):
    for group in range(grid.xi_groups):
        cells = [state_ref[grid.eta_tile(i, group), :] for i in range(grid.ny)]
        for i, value in enumerate(smooth_source(cells)):
            source_ref[grid.eta_major(i, group), :] = value


def xi_sources(grid, state_ref, source_ref):
    for group in range(grid.eta_groups):
        cells = [state_ref[grid.xi_tile(i, group), :] for i in range(grid.nx)]
        for i, value in enumerate(smooth_source(cells)):
            source_ref[grid.xi_tile(i, group), :] = value


def eta_filter(grid, source_ref, eta_a, eta_b, base, result_ref):
    for group in range(grid.xi_groups):
        below, above = take_cells(eta_a, eta_b, odd("eta"), base, group)
        rights = [source_ref[grid.eta_major(i, group), :] for i in range(grid.ny)]
        for i, value in enumerate(smooth_solve(rights, below, above)):
            result_ref[grid.eta_tile(i, group), :] = value


def xi_filter(grid, source_ref, xi_a, xi_b, base, smooth, result_ref):
    for group in range(grid.eta_groups):
        below, above = take_cells(xi_a, xi_b, odd("xi"), base, group)
        rights = [source_ref[grid.xi_tile(i, group), :] for i in range(grid.nx)]
        for i, value in enumerate(smooth_solve(rights, below, above)):
            result_ref[grid.xi_tile(i, group), :] = value
    result_ref[...] = lane_product(result_ref[...], smooth)


def source_kernel(grid, form, state_ref, source_ref):
    for field in range(state_ref.shape[0]):
        form(grid, state_ref.at[field], source_ref.at[field])


def mass_eta_kernel(grid, source_ref, eta_a, eta_b, order_ref, result_ref, next_ref, xi_first, xi_second):
    eta_filter(grid, source_ref.at[0], eta_a, eta_b, 2 * 4, result_ref.at[0])
    send_cells(
        lambda position, group: result_ref[0, grid.xi_tile(position, group), :],
        grid.eta_groups, grid.nx, odd("xi"), xi_first, xi_second, 0,
    )
    xi_sources(grid, result_ref.at[0], next_ref.at[0])


def eta_filter_kernel(
    grid, source_ref, mass_ref, order_ref, eta_b, eta_a,
    result_ref, xi_first, xi_second, zeta_ref, edge_first, edge_second,
):
    flag = odd("xi")
    for field in range(4):
        eta_filter(grid, source_ref.at[field], eta_a, eta_b, WIDTH * field, result_ref.at[field])
        send_cells(
            lambda position, group: result_ref[field, grid.xi_tile(position, group), :],
            grid.eta_groups, grid.nx, flag, xi_first, xi_second, WIDTH * field,
        )
    lane = lax.broadcasted_iota(jnp.int32, (TILE, LANES), 1)
    for position in range(grid.nx):
        packed = None
        for slot in range(5 * grid.eta_groups):
            field, group = slot // grid.eta_groups, slot % grid.eta_groups
            rows = grid.xi_tile(position, group)
            part = result_ref[field - 1, rows, :] if field else mass_ref[0, rows, :]
            part = pltpu.roll(part, WIDTH * (2 * slot + 1), axis=1)
            packed = part if packed is None else jnp.where(lane >= 2 * WIDTH * slot, part, packed)
        zeta_ref[group_rows(position), :] = packed
    send_cells(
        lambda position, group: zeta_ref[group_rows(position), :],
        1, grid.nx, flag, edge_first, edge_second, 0,
    )


def xi_filter_kernel(grid, source_ref, xi_a, xi_b, tables_ref, result_ref):
    smooth = split_weights(tables_ref[SMOOTH])
    for field in range(source_ref.shape[0]):
        xi_filter(
            grid, source_ref.at[field], xi_a, xi_b, WIDTH * field, smooth, result_ref.at[field]
        )


def zeta_filter_kernel(
    grid,
    mass_ref, state_ref, below_ref, above_ref, a_below, a_above, b_below, b_above, tables_ref,
    result_hbm,
    result_ref, sems,
):
    ends = split_weights(tables_ref[ENDS])
    flag = odd("xi")
    lane = lax.broadcasted_iota(jnp.int32, (TILE, LANES), 1)
    from_below = lax.rem(lane, 2 * WIDTH) < WIDTH

    def merge(below, above, index):
        return jnp.where(from_below, below[group_rows(index), :], above[group_rows(index), :])

    low, high = [], []
    for step in range(WIDTH):
        first, second = merge(a_below, a_above, step), merge(b_below, b_above, step)
        low.append(jnp.where(flag, first, second))
        high.append(jnp.where(flag, second, first))
    cells = [merge(below_ref, above_ref, position) for position in range(grid.nx)]
    cells = smooth_solve(smooth_source(cells), low, high)
    copies = []
    for field in range(5):
        parts = []
        for packed in cells:
            for group in range(grid.eta_groups):
                slot = field * grid.eta_groups + group
                parts.append(pltpu.roll(packed, LANES - 2 * WIDTH * slot, axis=1) if slot else packed)
        halo = jnp.concatenate(parts, axis=0)
        own = state_ref[field - 1] if field else mass_ref[0]
        result_ref[field] = own + lane_product(halo, ends)
        copy = pltpu.make_async_copy(result_ref.at[field], result_hbm.at[field], sems.at[field])
        copy.start()
        copies.append(copy)
    for copy in copies:
        copy.wait()


def pair_swap(value, axis, parity):
    count = lax.axis_size(axis)
    pairs = []
    for index in range(count):
        step = 1 if index % 2 == parity else -1
        pairs.append((index, (index + step) % count))
    return lax.ppermute(value, axis, pairs)


def diagonal_swap(value, parity):
    nx, nz = lax.axis_size("xi"), lax.axis_size("zeta")

    def send(shift):
        pairs = []
        for i in range(nx):
            partner = (i + (1 if i % 2 == parity else -1)) % nx
            for k in range(nz):
                pairs.append((i * nz + k, partner * nz + (k + shift) % nz))
        return lax.ppermute(value, ("xi", "zeta"), pairs)

    below = send(1)
    return (below, below) if nz == 2 else (below, send(-1))


def ring_swap(value, axis):
    count = lax.axis_size(axis)
    if count == 2:
        other = lax.ppermute(value, axis, [(0, 1), (1, 0)])
        return other, other
    up = [(index, (index + 1) % count) for index in range(count)]
    down = [(index, (index - 1) % count) for index in range(count)]
    return lax.ppermute(value, axis, up), lax.ppermute(value, axis, down)


HBM = pltpu.MemorySpace.HBM


def call(kernel, outs, *operands, scratch=(), cost=1.0, far=(), far_outs=()):
    shapes = [
        out if isinstance(out, jax.ShapeDtypeStruct) else jax.ShapeDtypeStruct(out, jnp.float32)
        for out in outs
    ]
    near = pltpu.MemorySpace.VMEM
    operands = [
        pltpu.with_memory_space_constraint(value, HBM) if index in far else value
        for index, value in enumerate(operands)
    ]
    return pl.pallas_call(
        kernel,
        out_shape=shapes,
        in_specs=[
            pl.BlockSpec(memory_space=HBM if index in far else near) for index in range(len(operands))
        ],
        out_specs=[
            pl.BlockSpec(memory_space=HBM if index in far_outs else near) for index in range(len(outs))
        ],
        scratch_shapes=scratch,
        cost_estimate=pl.CostEstimate(flops=0, transcendentals=0, bytes_accessed=int(cost * 3.6e6)),
        compiler_params=pltpu.CompilerParams(vmem_limit_bytes=20 * 2**20),
    )(*operands)


def like(value):
    return jax.ShapeDtypeStruct(value.shape, value.dtype)


def local(conserved_solution, metrics, jacobian):
    _, nx, ny, nz = conserved_solution.shape
    grid = Grid(nx, ny)
    rows = grid.rows
    u = conserved_solution.reshape(5, rows, nz)
    metrics = metrics.reshape(9, rows, nz)
    jacobian = jacobian.reshape(rows, nz)
    tables = jnp.asarray(zeta_tables(nz))

    def exchange(eta_first, eta_second, xi_first, xi_second, zeta):
        eta_b = pair_swap(eta_second, "eta", 1)
        eta_a = pair_swap(eta_first, "eta", 0)
        xi_b = pair_swap(xi_second, "xi", 1)
        below, above = ring_swap(zeta, "zeta")
        xi_a = pair_swap(xi_first, "xi", 0)
        return (eta_a, eta_b, xi_b, xi_a), (below, above)

    block = (rows, nz)
    chunks = 2
    u, tables, metrics, jacobian, prim, mass, *sends = call(
        functools.partial(primitive_kernel, grid),
        [like(u), like(tables), like(metrics), like(jacobian), (4, *block), (3, *block)]
        + [(2 * 5, nx, nz)] * 2
        + [(2 * 5, ny, nz)] * 2
        + [(5, TILE, LANES)],
        u, tables, metrics, jacobian,
        scratch=[pltpu.SemaphoreType.DMA((chunks, 5)), pltpu.SemaphoreType.DMA((11,))],
        far=(0, 1, 2, 3),
    )
    sides, ends = exchange(*sends)
    xi_source, eta_source, own = call(
        functools.partial(primitive_source_kernel, grid), [(5, *block)] * 3, prim, mass, tables,
    )
    slopes, mass_total = call(
        functools.partial(slope_kernel, grid),
        [(2, 4, *block), block],
        xi_source, eta_source, own, *sides,
    )
    contra, mass, *sends = call(
        functools.partial(flux_kernel, grid),
        [(3, 4, *block), block]
        + [(2 * 4 + WIDTH, nx, nz)] * 2
        + [(2 * 4, ny, nz)] * 2
        + [(4, TILE, LANES)],
        u, prim, metrics, jacobian, slopes, own, mass_total, *ends, tables,
        scratch=[pltpu.VMEM((4, *block), jnp.float32)],
    )
    sides, ends = exchange(*sends)
    xi_source, eta_source, own = call(
        functools.partial(contra_source_kernel, grid), [(4, *block)] * 3, contra, tables,
    )
    (mass_source,) = call(
        functools.partial(source_kernel, grid, eta_sources), [(1, *block)], mass.reshape(1, *block),
    )
    (total,) = call(
        functools.partial(divergence_kernel, grid),
        [(4, *block)],
        xi_source, eta_source, own, *sides,
    )
    state, eta_first, eta_second = call(
        functools.partial(step_kernel, grid),
        [(4, *block)] + [(4 * WIDTH, nx, nz)] * 2,
        u, jacobian, total, *ends, tables,
    )
    mass, mass_source, xi_first, xi_second = call(
        functools.partial(mass_eta_kernel, grid),
        [(1, *block)] * 2 + [(WIDTH, ny, nz)] * 2,
        mass_source, sides[0], sides[1], eta_first,
    )
    eta_b = pair_swap(eta_second, "eta", 1)
    eta_a = pair_swap(eta_first, "eta", 0)
    xi_b = pair_swap(xi_second, "xi", 1)
    xi_a = pair_swap(xi_first, "xi", 0)
    (source,) = call(functools.partial(source_kernel, grid, eta_sources), [(4, *block)], state)
    (mass_part,) = call(
        functools.partial(xi_filter_kernel, grid), [(1, *block)], mass_source, xi_a, xi_b, tables,
    )
    state, xi_first, xi_second, zeta, edge_first, edge_second = call(
        functools.partial(eta_filter_kernel, grid),
        [(4, *block)]
        + [(4 * WIDTH, ny, nz)] * 2
        + [(nx * TILE, LANES)]
        + [(WIDTH, TILE, LANES)] * 2,
        source, mass, mass_part, eta_b, eta_a,
    )
    xi_b = pair_swap(xi_second, "xi", 1)
    ends = ring_swap(zeta, "zeta")
    edges_b = diagonal_swap(edge_second, 1)
    edges_a = diagonal_swap(edge_first, 0)
    xi_a = pair_swap(xi_first, "xi", 0)
    (source,) = call(functools.partial(source_kernel, grid, xi_sources), [(4, *block)], state)
    (state,) = call(
        functools.partial(xi_filter_kernel, grid), [(4, *block)], source, xi_a, xi_b, tables,
    )
    edges = [edge.reshape(WIDTH * TILE, LANES) for edge in (*edges_a, *edges_b)]
    (result,) = call(
        functools.partial(zeta_filter_kernel, grid),
        [(5, *block)],
        mass_part, state, *ends, *edges, tables,
        scratch=[pltpu.VMEM((5, *block), jnp.float32), pltpu.SemaphoreType.DMA((5,))],
        far_outs=(0,),
    )
    return result.reshape(5, nx, ny, nz)


def solution(mesh):
    in_specs = (
        P(None, "xi", "eta", "zeta"),
        P(None, None, "xi", "eta", "zeta"),
        P("xi", "eta", "zeta"),
    )
    out_specs = P(None, "xi", "eta", "zeta")
    return jax.shard_map(local, mesh=mesh, in_specs=in_specs, out_specs=out_specs, check_vma=False)
```

```python
import functools

import jax
import jax.numpy as jnp
import numpy as np
from jax import lax
from jax.experimental import pallas as pl
from jax.experimental.pallas import tpu as pltpu
from jax.sharding import PartitionSpec as P

WIDTH = 5
LANES = 128
TILE = 8

viscosity = 0.15
conduction = 0.15 * 1.4 / (0.4 * 0.72)
step_duration = 0.08


def derivative_system(length):
    extent = length + 2 * WIDTH
    system = np.eye(extent)
    source = np.zeros((extent, extent))
    for position in range(2, extent - 2):
        system[position, position - 1] = 1.0 / 3.0
        system[position, position + 1] = 1.0 / 3.0
        source[position, position + 1] = 7.0 / 9.0
        source[position, position - 1] = -7.0 / 9.0
        source[position, position + 2] = 1.0 / 36.0
        source[position, position - 2] = -1.0 / 36.0
    source[1, 2] = 0.5
    source[1, 0] = -0.5
    source[extent - 2, extent - 1] = 0.5
    source[extent - 2, extent - 3] = -0.5
    source[0, 1] = 1.0
    source[0, 0] = -1.0
    source[extent - 1, extent - 1] = 1.0
    source[extent - 1, extent - 2] = -1.0
    return system, source


def filter_coefficients():
    strength = 0.4
    return [
        (193.0 + 126.0 * strength) / 256.0,
        (105.0 + 302.0 * strength) / 256.0,
        15.0 * (2.0 * strength - 1.0) / 64.0,
        45.0 * (1.0 - 2.0 * strength) / 512.0,
        5.0 * (2.0 * strength - 1.0) / 256.0,
        (1.0 - 2.0 * strength) / 512.0,
    ]


def filter_system(length):
    strength = 0.4
    coeffs = filter_coefficients()
    extent = length + 2 * WIDTH
    system = np.eye(extent)
    source = np.eye(extent)
    for position in range(5, extent - 5):
        system[position, position - 1] = strength
        system[position, position + 1] = strength
        source[position, position] = coeffs[0]
        for offset in range(1, 6):
            source[position, position + offset] = coeffs[offset] / 2.0
            source[position, position - offset] = coeffs[offset] / 2.0
    return system, source


def own_rows(system, source, length):
    return np.linalg.solve(system, source)[WIDTH : WIDTH + length]


def derivative_parts(length):
    system, source = derivative_system(length)
    halo = np.linalg.solve(system[:WIDTH, :WIDTH], source[:WIDTH])
    row = source[WIDTH] - system[WIDTH, WIDTH - 1] * halo[WIDTH - 1]
    pivots = [1.0]
    for position in range(3, WIDTH + length):
        pivots.append(1.0 - 1.0 / 9.0 / pivots[-1])
    return pivots[WIDTH - 2 :], row[:WIDTH], row[WIDTH : WIDTH + 3]


def pad_rows(table):
    return np.concatenate([table, np.zeros((LANES - table.shape[0], table.shape[1]))], axis=0)


def pad_columns(table):
    return np.concatenate([table, np.zeros((table.shape[0], LANES - table.shape[1]))], axis=1)


def zeta_tables(length):
    system, source = derivative_system(length)
    table = own_rows(system, source, length)
    _, edge, _ = derivative_parts(length)
    inverse = np.linalg.inv(system)
    extent = length + 2 * WIDTH
    sums = np.zeros((length, 4))
    sums[length - WIDTH :, 0] = edge
    sums[length - 1, 1] = 1.0
    sums[:WIDTH, 2] = -edge[::-1]
    sums[0, 3] = 1.0
    own = slice(WIDTH, WIDTH + length)
    back = np.stack(
        [
            inverse[own, WIDTH],
            -1.0 / 36.0 * inverse[own, WIDTH + 1],
            inverse[own, extent - WIDTH - 1],
            1.0 / 36.0 * inverse[own, extent - WIDTH - 2],
        ]
    )
    smooth = own_rows(*filter_system(length), length)
    ends = np.concatenate([smooth[:, :WIDTH], smooth[:, WIDTH + length :]], axis=1)
    tables = [table[:, own].T, pad_columns(sums), pad_rows(back), smooth[:, own].T, pad_rows(ends.T)]
    return np.stack(tables).astype(np.float32)


DERIVE, SUMS, BACK, SMOOTH, ENDS = range(5)


def twisted_solve(rights, pivots, off):
    count = len(rights)
    half = count // 2
    low = [rights[0]]
    high = [rights[count - 1]]
    for step in range(1, half):
        factor = off / pivots[step - 1]
        low.append(rights[step] - factor * low[-1])
        high.append(rights[count - 1 - step] - factor * high[-1])
    middle = pivots[half - 1]
    det = middle * middle - off * off
    first, second = low[-1], high[-1]
    answer = [None] * count
    answer[half - 1] = (middle / det) * first - (off / det) * second
    answer[half] = (middle / det) * second - (off / det) * first
    for step in range(half - 2, -1, -1):
        scale = 1.0 / pivots[step]
        factor = off / pivots[step]
        answer[step] = scale * low[step] - factor * answer[step + 1]
        answer[count - 1 - step] = scale * high[step] - factor * answer[count - 2 - step]
    return answer


def derive_source(cells):
    count = len(cells)
    _, _, edge = derivative_parts(count)
    near, far = 7.0 / 9.0, 1.0 / 36.0
    rights = [None] * count
    rights[0] = edge[0] * cells[0] + edge[1] * cells[1] + edge[2] * cells[2]
    rights[1] = near * (cells[2] - cells[0]) + far * cells[3]
    for step in range(2, count - 2):
        rights[step] = near * (cells[step + 1] - cells[step - 1]) + far * (
            cells[step + 2] - cells[step - 2]
        )
    rights[count - 2] = near * (cells[count - 1] - cells[count - 3]) - far * cells[count - 4]
    rights[count - 1] = -(
        edge[0] * cells[count - 1] + edge[1] * cells[count - 2] + edge[2] * cells[count - 3]
    )
    return rights


def derive_solve(rights, below, above):
    pivots, _, _ = derivative_parts(len(rights))
    rights = list(rights)
    far = 1.0 / 36.0
    rights[0] = rights[0] + below[0]
    rights[1] = rights[1] - far * below[1]
    rights[-2] = rights[-2] + far * above[1]
    rights[-1] = rights[-1] + above[0]
    return twisted_solve(rights, pivots, 1.0 / 3.0)


def end_sums(cells):
    _, edge, _ = derivative_parts(16)
    total = edge[WIDTH - 1] * cells[0]
    for step in range(1, WIDTH):
        total = total + edge[WIDTH - 1 - step] * cells[step]
    return total, cells[0]


def smooth_source(cells):
    count = len(cells)
    coeffs = filter_coefficients()
    rights = []
    for step in range(count):
        total = coeffs[0] * cells[step]
        for offset in range(1, WIDTH + 1):
            around = [cells[i] for i in (step - offset, step + offset) if 0 <= i < count]
            around = around[0] + around[1] if len(around) == 2 else around[0]
            total = total + (0.5 * coeffs[offset]) * around
        rights.append(total)
    return rights


def smooth_solve(rights, below, above):
    count = len(rights)
    coeffs = filter_coefficients()
    rights = list(rights)
    for step in range(WIDTH):
        for cell in range(WIDTH - step):
            factor = 0.5 * coeffs[step + cell + 1]
            if step == 0 and cell == 0:
                factor = factor - 0.4
            rights[step] = rights[step] + factor * below[cell]
            rights[count - 1 - step] = rights[count - 1 - step] + factor * above[cell]
    pivots = [1.0]
    for _ in range(count):
        pivots.append(1.0 - 0.16 / pivots[-1])
    return twisted_solve(rights, pivots, 0.4)


def split_values(values):
    high = values.astype(jnp.bfloat16)
    low = (values - high.astype(jnp.float32)).astype(jnp.bfloat16)
    return jnp.concatenate([high, low], axis=1)


def split_weights(table):
    high = table.astype(jnp.bfloat16)
    low = (table - high.astype(jnp.float32)).astype(jnp.bfloat16)
    top = jnp.concatenate([high, low], axis=1)
    return jnp.concatenate([top, jnp.concatenate([high, jnp.zeros_like(low)], axis=1)], axis=0)


def lane_product(values, weights):
    both = jnp.dot(split_values(values), weights, preferred_element_type=jnp.float32)
    return both[:, :LANES] + both[:, LANES:]


class Grid:
    def __init__(self, nx, ny):
        self.nx, self.ny, self.rows = nx, ny, nx * ny
        self.eta_groups = ny // TILE
        self.xi_groups = nx // TILE

    def xi_tile(self, position, group):
        return pl.ds(position * self.ny + group * TILE, TILE)

    def eta_tile(self, position, group):
        return pl.ds(position + group * TILE * self.ny, TILE, stride=self.ny)

    def eta_major(self, position, group):
        return pl.ds(position * self.nx + group * TILE, TILE)


def group_rows(group):
    return pl.ds(group * TILE, TILE)


def odd(axis):
    return lax.rem(lax.axis_index(axis), 2) == 1


def send_sums(read, groups, count, flag, first_ref, second_ref, field):
    for group in range(groups):
        top = end_sums([read(count - 1 - step, group) for step in range(WIDTH)])
        low = end_sums([read(step, group) for step in range(WIDTH)])
        low = (-low[0], low[1])
        for part in range(2):
            first_ref[2 * field + part, group_rows(group), :] = jnp.where(flag, low[part], top[part])
            second_ref[2 * field + part, group_rows(group), :] = jnp.where(flag, top[part], low[part])


def take_sums(first_ref, second_ref, flag, field, group):
    below, above = [], []
    for part in range(2):
        first = first_ref[2 * field + part, group_rows(group), :]
        second = second_ref[2 * field + part, group_rows(group), :]
        below.append(jnp.where(flag, first, second))
        above.append(jnp.where(flag, second, first))
    return below, above


def pack_sums(values, weights, grid):
    sums = lane_product(values, weights)
    parts = []
    for group in range(grid.rows // TILE):
        part = sums[group * TILE : (group + 1) * TILE]
        parts.append(pltpu.roll(part, 4 * group, axis=1) if group else part)
    while len(parts) > 1:
        parts = [sum(parts[i + 1 : i + 2], parts[i]) for i in range(0, len(parts), 2)]
    return parts[0]


def unpack_sums(below, above, grid):
    lane = lax.broadcasted_iota(jnp.int32, below.shape, 1)
    packed = jnp.where(lax.rem(lane, 4) < 2, below, above)
    parts = [packed]
    for group in range(1, grid.rows // TILE):
        parts.append(pltpu.roll(packed, LANES - 4 * group, axis=1))
    return jnp.concatenate(parts, axis=0)


def primitive_kernel(
    grid,
    u_hbm, tables_hbm, metrics_hbm, jacobian_hbm,
    u_ref, tables_ref, metrics_ref, jacobian_ref,
    prim_ref, mass_ref, eta_first, eta_second, xi_first, xi_second, zeta_ref,
    u_sems, late_sems,
):
    chunks = u_sems.shape[0]
    step = grid.rows // chunks
    copies = []
    for index in range(chunks):
        rows = pl.ds(index * step, step)
        for field in range(5):
            copy = pltpu.make_async_copy(
                u_hbm.at[field, rows, :], u_ref.at[field, rows, :], u_sems.at[index, field]
            )
            copy.start()
            copies.append(copy)
    late = [
        pltpu.make_async_copy(source, result, late_sems.at[index])
        for index, (source, result) in enumerate(
            [(tables_hbm, tables_ref)]
            + [(metrics_hbm.at[k], metrics_ref.at[k]) for k in range(9)]
            + [(jacobian_hbm, jacobian_ref)]
        )
    ]
    for copy in late:
        copy.start()
    for index in range(chunks):
        for copy in copies[5 * index : 5 * index + 5]:
            copy.wait()
        rows = pl.ds(index * step, step)
        inverse = 1.0 / u_ref[0, rows, :]
        work = None
        for c in range(3):
            momentum = u_ref[1 + c, rows, :]
            speed = momentum * inverse
            prim_ref[c, rows, :] = speed
            work = momentum * speed if work is None else work + momentum * speed
        pressure = 0.4 * (u_ref[4, rows, :] - 0.5 * work)
        prim_ref[3, rows, :] = pressure * inverse

    def send(xi_value, eta_value, field):
        send_sums(
            lambda position, group: eta_value[grid.eta_tile(position, group), :],
            grid.xi_groups, grid.ny, odd("eta"), eta_first, eta_second, field,
        )
        send_sums(
            lambda position, group: xi_value[grid.xi_tile(position, group), :],
            grid.eta_groups, grid.nx, odd("xi"), xi_first, xi_second, field,
        )

    for field in range(4):
        send(prim_ref.at[field], prim_ref.at[field], field)
    for copy in late:
        copy.wait()
    for k in range(3):
        for index in range(chunks):
            rows = pl.ds(index * step, step)
            mass_ref[k, rows, :] = (
                metrics_ref[3 * k, rows, :] * u_ref[1, rows, :]
                + metrics_ref[3 * k + 1, rows, :] * u_ref[2, rows, :]
                + metrics_ref[3 * k + 2, rows, :] * u_ref[3, rows, :]
            )
    send(mass_ref.at[0], mass_ref.at[1], 4)
    sums = split_weights(tables_ref[SUMS])
    for field in range(5):
        values = prim_ref[field] if field < 4 else mass_ref[2]
        zeta_ref[field] = pack_sums(values, sums, grid)


def derive_sources(grid, xi_value, eta_value, zeta_value, derive, field, xi_ref, eta_ref, zeta_ref):
    zeta_ref[field] = lane_product(zeta_value[...], derive)
    for group in range(grid.eta_groups):
        cells = [xi_value[grid.xi_tile(i, group), :] for i in range(grid.nx)]
        for i, value in enumerate(derive_source(cells)):
            xi_ref[field, grid.xi_tile(i, group), :] = value
    for group in range(grid.xi_groups):
        cells = [eta_value[grid.eta_tile(i, group), :] for i in range(grid.ny)]
        for i, value in enumerate(derive_source(cells)):
            eta_ref[field, grid.eta_major(i, group), :] = value


def primitive_source_kernel(grid, prim_ref, mass_ref, tables_ref, *results):
    derive = split_weights(tables_ref[DERIVE])
    for field in range(4):
        derive_sources(grid, *[prim_ref.at[field]] * 3, derive, field, *results)
    derive_sources(grid, *[mass_ref.at[k] for k in range(3)], derive, 4, *results)


def contra_source_kernel(grid, contra_ref, tables_ref, *results):
    derive = split_weights(tables_ref[DERIVE])
    for field in range(4):
        derive_sources(grid, *[contra_ref.at[k, field] for k in range(3)], derive, field, *results)


def xi_derivative(grid, source_ref, xi_a, xi_b, field, group):
    below, above = take_sums(xi_a, xi_b, odd("xi"), field, group)
    rights = [source_ref[field, grid.xi_tile(i, group), :] for i in range(grid.nx)]
    return derive_solve(rights, below, above)


def eta_derivative(grid, source_ref, eta_a, eta_b, field, group):
    below, above = take_sums(eta_a, eta_b, odd("eta"), field, group)
    rights = [source_ref[field, grid.eta_major(i, group), :] for i in range(grid.ny)]
    return derive_solve(rights, below, above)


def add_derivatives(grid, xi_source, eta_source, own_ref, eta_a, eta_b, xi_a, xi_b, field, total_ref):
    for group in range(grid.xi_groups):
        for i, value in enumerate(eta_derivative(grid, eta_source, eta_a, eta_b, field, group)):
            rows = grid.eta_tile(i, group)
            total_ref[rows, :] = own_ref[field, rows, :] + value
    for group in range(grid.eta_groups):
        for i, value in enumerate(xi_derivative(grid, xi_source, xi_a, xi_b, field, group)):
            rows = grid.xi_tile(i, group)
            total_ref[rows, :] = total_ref[rows, :] + value


def slope_kernel(grid, xi_source, eta_source, own_ref, eta_b, eta_a, xi_b, xi_a, slope_ref, mass_total_ref):
    for field in range(4):
        for group in range(grid.eta_groups):
            for i, value in enumerate(xi_derivative(grid, xi_source, xi_a, xi_b, field, group)):
                slope_ref[0, field, grid.xi_tile(i, group), :] = value
        for group in range(grid.xi_groups):
            for i, value in enumerate(eta_derivative(grid, eta_source, eta_a, eta_b, field, group)):
                slope_ref[1, field, grid.eta_tile(i, group), :] = value
    add_derivatives(
        grid, xi_source, eta_source, own_ref, eta_a, eta_b, xi_a, xi_b, 4, mass_total_ref
    )


def flux_kernel(
    grid,
    u_ref, prim_ref, metrics_ref, jacobian_ref, slope_ref, own_ref, mass_total_ref,
    zeta_below, zeta_above, tables_ref,
    contra_ref, mass_ref, eta_first, eta_second,
    zeta_slope_ref,
):
    back = split_weights(tables_ref[BACK])
    for field in range(4):
        halo = unpack_sums(zeta_below[field], zeta_above[field], grid)
        zeta_slope_ref[field] = own_ref[field] + lane_product(halo, back)
    halo = unpack_sums(zeta_below[4], zeta_above[4], grid)
    total = mass_total_ref[...] + lane_product(halo, back)
    mass_ref[...] = u_ref[0] - (step_duration * jacobian_ref[...]) * total
    send_cells(
        lambda position, group: mass_ref[grid.eta_tile(position, group), :],
        grid.xi_groups, grid.ny, odd("eta"), eta_first, eta_second, 2 * 4,
    )

    step = TILE

    def body(index, carry):
        rows = pl.ds(pl.multiple_of(index * step, step), step)
        u = [u_ref[c, rows, :] for c in range(5)]
        speed = [prim_ref[c, rows, :] for c in range(3)]
        pressure = prim_ref[3, rows, :] * u[0]
        metrics = [[metrics_ref[3 * k + j, rows, :] for j in range(3)] for k in range(3)]
        scaled = (viscosity * jacobian_ref[rows, :])
        scaled = [[scaled * metrics[k][j] for j in range(3)] for k in range(3)]
        physical = []
        for c in range(4):
            slopes = [slope_ref[0, c, rows, :], slope_ref[1, c, rows, :], zeta_slope_ref[c, rows, :]]
            physical.append(
                [
                    scaled[0][j] * slopes[0] + scaled[1][j] * slopes[1] + scaled[2][j] * slopes[2]
                    for j in range(3)
                ]
            )
        spread = (2.0 / 3.0) * (physical[0][0] + physical[1][1] + physical[2][2])
        stress = [[None] * 3 for _ in range(3)]
        momentum = [[None] * 3 for _ in range(3)]
        for c in range(3):
            stress[c][c] = (physical[c][c] + physical[c][c]) - spread
            momentum[c][c] = (u[1 + c] * speed[c] + pressure) - stress[c][c]
            for j in range(c):
                stress[c][j] = stress[j][c] = physical[c][j] + physical[j][c]
                momentum[c][j] = momentum[j][c] = u[1 + c] * speed[j] - stress[c][j]
        total = u[4] + pressure
        fluxes = []
        for j in range(3):
            worked = speed[0] * stress[0][j] + speed[1] * stress[1][j] + speed[2] * stress[2][j]
            energy = (total * speed[j] - worked) - (conduction / viscosity) * physical[3][j]
            fluxes.append([momentum[0][j], momentum[1][j], momentum[2][j], energy])
        for k in range(3):
            for f in range(4):
                contra_ref[k, f, rows, :] = (
                    metrics[k][0] * fluxes[0][f]
                    + metrics[k][1] * fluxes[1][f]
                    + metrics[k][2] * fluxes[2][f]
                )
        return carry

    lax.fori_loop(0, grid.rows // step, body, 0, unroll=4)
    for field in range(4):
        send_sums(
            lambda position, group: contra_ref[1, field, grid.eta_tile(position, group), :],
            grid.xi_groups, grid.ny, odd("eta"), eta_first, eta_second, field,
        )


def contra_sums_kernel(grid, contra_ref, tables_ref, xi_first, xi_second, zeta_ref):
    sums = split_weights(tables_ref[SUMS])
    for field in range(4):
        send_sums(
            lambda position, group: contra_ref[0, field, grid.xi_tile(position, group), :],
            grid.eta_groups, grid.nx, odd("xi"), xi_first, xi_second, field,
        )
        zeta_ref[field] = pack_sums(contra_ref[2, field], sums, grid)


def divergence_kernel(grid, xi_source, eta_source, own_ref, eta_b, eta_a, xi_b, xi_a, total_ref):
    for field in range(4):
        add_derivatives(
            grid, xi_source, eta_source, own_ref, eta_a, eta_b, xi_a, xi_b, field, total_ref.at[field]
        )


def step_kernel(
    grid,
    u_ref, jacobian_ref, total_ref, zeta_below, zeta_above, tables_ref,
    state_ref, eta_first, eta_second,
):
    back = split_weights(tables_ref[BACK])
    scale = step_duration * jacobian_ref[...]
    for field in range(4):
        halo = unpack_sums(zeta_below[field], zeta_above[field], grid)
        total = total_ref[field] + lane_product(halo, back)
        state_ref[field] = u_ref[1 + field] - scale * total
        send_cells(
            lambda position, group: state_ref[field, grid.eta_tile(position, group), :],
            grid.xi_groups, grid.ny, odd("eta"), eta_first, eta_second, WIDTH * field,
        )


def send_cells(read, groups, count, flag, first_ref, second_ref, base):
    for group in range(groups):
        for step in range(WIDTH):
            low = read(step, group)
            top = read(count - 1 - step, group)
            first_ref[base + step, group_rows(group), :] = jnp.where(flag, low, top)
            second_ref[base + step, group_rows(group), :] = jnp.where(flag, top, low)


def take_cells(first_ref, second_ref, flag, base, group):
    below, above = [], []
    for step in range(WIDTH):
        first = first_ref[base + step, group_rows(group), :]
        second = second_ref[base + step, group_rows(group), :]
        below.append(jnp.where(flag, first, second))
        above.append(jnp.where(flag, second, first))
    return below, above


def send_faces(grid, read, flag, first_ref, second_ref, base):
    for group in range(grid.eta_groups):
        for step in range(WIDTH):
            low = read(step, group)
            top = read(grid.nx - WIDTH + step, group)
            first_ref[base + step, group_rows(group), :] = jnp.where(flag, low, top)
            second_ref[base + step, group_rows(group), :] = jnp.where(flag, top, low)


def take_faces(first_ref, second_ref, flag, base, group):
    below, above = [], []
    for step in range(WIDTH):
        low, top = base + step, base + WIDTH - 1 - step
        rows = group_rows(group)
        below.append(jnp.where(flag, first_ref[top, rows, :], second_ref[top, rows, :]))
        above.append(jnp.where(flag, second_ref[low, rows, :], first_ref[low, rows, :]))
    return below, above


def eta_sources(grid, state_ref, source_ref):
    for group in range(grid.xi_groups):
        cells = [state_ref[grid.eta_tile(i, group), :] for i in range(grid.ny)]
        for i, value in enumerate(smooth_source(cells)):
            source_ref[grid.eta_major(i, group), :] = value


def xi_sources(grid, state_ref, source_ref):
    for group in range(grid.eta_groups):
        cells = [state_ref[grid.xi_tile(i, group), :] for i in range(grid.nx)]
        for i, value in enumerate(smooth_source(cells)):
            source_ref[grid.xi_tile(i, group), :] = value


def eta_filter(grid, source_ref, eta_a, eta_b, base, result_ref):
    for group in range(grid.xi_groups):
        below, above = take_cells(eta_a, eta_b, odd("eta"), base, group)
        rights = [source_ref[grid.eta_major(i, group), :] for i in range(grid.ny)]
        for i, value in enumerate(smooth_solve(rights, below, above)):
            result_ref[grid.eta_tile(i, group), :] = value


def xi_filter(grid, source_ref, xi_a, xi_b, base, smooth, result_ref):
    for group in range(grid.eta_groups):
        below, above = take_faces(xi_a, xi_b, odd("xi"), base, group)
        rights = [source_ref[grid.xi_tile(i, group), :] for i in range(grid.nx)]
        for i, value in enumerate(smooth_solve(rights, below, above)):
            result_ref[grid.xi_tile(i, group), :] = value
    result_ref[...] = lane_product(result_ref[...], smooth)


def source_kernel(grid, form, state_ref, source_ref):
    for field in range(state_ref.shape[0]):
        form(grid, state_ref.at[field], source_ref.at[field])


def face_kernel(
    grid, state_ref, source_ref, eta_a, eta_b, result_ref, next_ref, xi_first, xi_second
):
    flag = odd("xi")
    eta_filter(grid, source_ref.at[0], eta_a, eta_b, 2 * 4, result_ref.at[0])
    for field in range(5):
        values = state_ref.at[field] if field < 4 else result_ref.at[0]
        send_faces(
            grid, lambda position, group: values[grid.xi_tile(position, group), :],
            flag, xi_first, xi_second, WIDTH * field,
        )
    xi_sources(grid, result_ref.at[0], next_ref.at[0])


PLANES = 3 * TILE


def halo_source_kernel(grid, first_ref, second_ref, first_source, second_source):
    for faces, source in ((first_ref, first_source), (second_ref, second_source)):
        for tile in range(PLANES // TILE):
            cells = [
                faces[pl.ds(tile * TILE * grid.ny + i, TILE, stride=grid.ny), :] for i in range(grid.ny)
            ]
            for i, value in enumerate(smooth_source(cells)):
                source[pl.ds(i * PLANES + tile * TILE, TILE), :] = value


def edge_kernel(grid, order_ref, eta_a, eta_b, first_ref, second_ref):
    flag = odd("xi")
    eta_flag = odd("eta")
    for side in range(2):
        for step in range(WIDTH):
            start = (side * WIDTH + step) * PLANES
            for field in range(4):
                one, other = eta_a[WIDTH * field + step], eta_b[WIDTH * field + step]
                cells = jnp.where(eta_flag, other, one) if side else jnp.where(eta_flag, one, other)
                low, top = cells[:WIDTH], cells[grid.nx - WIDTH :]
                rows = pl.ds(start + WIDTH * field, WIDTH)
                first_ref[rows, :] = jnp.where(flag, low, top)
                second_ref[rows, :] = jnp.where(flag, top, low)
            rest = pl.ds(start + 4 * WIDTH, PLANES - 4 * WIDTH)
            first_ref[rest, :] = jnp.zeros((PLANES - 4 * WIDTH, LANES), jnp.float32)
            second_ref[rest, :] = jnp.zeros((PLANES - 4 * WIDTH, LANES), jnp.float32)


def filter_halo(grid, source_ref, edge_ref, result_ref):
    for tile in range(PLANES // TILE):
        ends = [
            [edge_ref[pl.ds((side * WIDTH + i) * PLANES + tile * TILE, TILE), :] for i in range(WIDTH)]
            for side in range(2)
        ]
        rights = [source_ref[pl.ds(i * PLANES + tile * TILE, TILE), :] for i in range(grid.ny)]
        for i, value in enumerate(smooth_solve(rights, *ends)):
            result_ref[pl.ds(tile * TILE * grid.ny + i, TILE, stride=grid.ny), :] = value


def eta_filter_kernel(
    grid, source_ref, mass_ref, eta_b, eta_a,
    result_ref, zeta_ref, edge_first, edge_second,
):
    flag = odd("xi")
    for field in range(4):
        eta_filter(grid, source_ref.at[field], eta_a, eta_b, WIDTH * field, result_ref.at[field])
    lane = lax.broadcasted_iota(jnp.int32, (TILE, LANES), 1)
    for position in range(grid.nx):
        packed = None
        for slot in range(5 * grid.eta_groups):
            field, group = slot // grid.eta_groups, slot % grid.eta_groups
            rows = grid.xi_tile(position, group)
            part = result_ref[field - 1, rows, :] if field else mass_ref[0, rows, :]
            part = pltpu.roll(part, WIDTH * (2 * slot + 1), axis=1)
            packed = part if packed is None else jnp.where(lane >= 2 * WIDTH * slot, part, packed)
        zeta_ref[group_rows(position), :] = packed
    send_cells(
        lambda position, group: zeta_ref[group_rows(position), :],
        1, grid.nx, flag, edge_first, edge_second, 0,
    )


def mass_xi_kernel(grid, source_ref, xi_a, xi_b, tables_ref, result_ref):
    smooth = split_weights(tables_ref[SMOOTH])
    xi_filter(grid, source_ref.at[0], xi_a, xi_b, WIDTH * 4, smooth, result_ref.at[0])


def xi_filter_kernel(
    grid, source_ref, first_source, second_source, edge_b, edge_a, tables_ref, result_ref,
    first_ref, second_ref,
):
    smooth = split_weights(tables_ref[SMOOTH])
    filter_halo(grid, first_source, edge_a, first_ref)
    filter_halo(grid, second_source, edge_b, second_ref)

    class Layers:
        def __init__(self, ref):
            self.ref = ref

        def __getitem__(self, index):
            layer, rows, _ = index
            return self.ref[pl.ds(layer * grid.ny + rows.start, rows.size), :]

    for field in range(4):
        xi_filter(
            grid, source_ref.at[field], Layers(first_ref), Layers(second_ref), WIDTH * field, smooth,
            result_ref.at[field],
        )


def zeta_filter_kernel(
    grid,
    mass_ref, state_ref, b_below, b_above, below_ref, above_ref, a_below, a_above, tables_ref,
    result_hbm,
    result_ref, sems,
):
    ends = split_weights(tables_ref[ENDS])
    flag = odd("xi")
    lane = lax.broadcasted_iota(jnp.int32, (TILE, LANES), 1)
    from_below = lax.rem(lane, 2 * WIDTH) < WIDTH

    def merge(below, above, index):
        return jnp.where(from_below, below[group_rows(index), :], above[group_rows(index), :])

    low, high = [], []
    for step in range(WIDTH):
        first, second = merge(a_below, a_above, step), merge(b_below, b_above, step)
        low.append(jnp.where(flag, first, second))
        high.append(jnp.where(flag, second, first))
    cells = [merge(below_ref, above_ref, position) for position in range(grid.nx)]
    cells = smooth_solve(smooth_source(cells), low, high)
    copies = []
    for field in range(5):
        parts = []
        for packed in cells:
            for group in range(grid.eta_groups):
                slot = field * grid.eta_groups + group
                parts.append(pltpu.roll(packed, LANES - 2 * WIDTH * slot, axis=1) if slot else packed)
        halo = jnp.concatenate(parts, axis=0)
        own = state_ref[field - 1] if field else mass_ref[0]
        result_ref[field] = own + lane_product(halo, ends)
        copy = pltpu.make_async_copy(result_ref.at[field], result_hbm.at[field], sems.at[field])
        copy.start()
        copies.append(copy)
    for copy in copies:
        copy.wait()


def pair_swap(value, axis, parity):
    count = lax.axis_size(axis)
    pairs = []
    for index in range(count):
        step = 1 if index % 2 == parity else -1
        pairs.append((index, (index + step) % count))
    return lax.ppermute(value, axis, pairs)


def diagonal_swap(value, parity):
    nx, nz = lax.axis_size("xi"), lax.axis_size("zeta")

    def send(shift):
        pairs = []
        for i in range(nx):
            partner = (i + (1 if i % 2 == parity else -1)) % nx
            for k in range(nz):
                pairs.append((i * nz + k, partner * nz + (k + shift) % nz))
        return lax.ppermute(value, ("xi", "zeta"), pairs)

    below = send(1)
    return (below, below) if nz == 2 else (below, send(-1))


def ring_swap(value, axis):
    count = lax.axis_size(axis)
    if count == 2:
        other = lax.ppermute(value, axis, [(0, 1), (1, 0)])
        return other, other
    up = [(index, (index + 1) % count) for index in range(count)]
    down = [(index, (index - 1) % count) for index in range(count)]
    return lax.ppermute(value, axis, up), lax.ppermute(value, axis, down)


HBM = pltpu.MemorySpace.HBM


def call(kernel, outs, *operands, scratch=(), cost=1.0, far=(), far_outs=()):
    shapes = [
        out if isinstance(out, jax.ShapeDtypeStruct) else jax.ShapeDtypeStruct(out, jnp.float32)
        for out in outs
    ]
    near = pltpu.MemorySpace.VMEM
    operands = [
        pltpu.with_memory_space_constraint(value, HBM) if index in far else value
        for index, value in enumerate(operands)
    ]
    return pl.pallas_call(
        kernel,
        out_shape=shapes,
        in_specs=[
            pl.BlockSpec(memory_space=HBM if index in far else near) for index in range(len(operands))
        ],
        out_specs=[
            pl.BlockSpec(memory_space=HBM if index in far_outs else near) for index in range(len(outs))
        ],
        scratch_shapes=scratch,
        cost_estimate=pl.CostEstimate(flops=0, transcendentals=0, bytes_accessed=int(cost * 3.6e6)),
        compiler_params=pltpu.CompilerParams(vmem_limit_bytes=20 * 2**20),
    )(*operands)


def like(value):
    return jax.ShapeDtypeStruct(value.shape, value.dtype)


def local(conserved_solution, metrics, jacobian):
    _, nx, ny, nz = conserved_solution.shape
    grid = Grid(nx, ny)
    rows = grid.rows
    u = conserved_solution.reshape(5, rows, nz)
    metrics = metrics.reshape(9, rows, nz)
    jacobian = jacobian.reshape(rows, nz)
    tables = jnp.asarray(zeta_tables(nz))

    def exchange(eta_first, eta_second, xi_first, xi_second, zeta):
        eta_b = pair_swap(eta_second, "eta", 1)
        eta_a = pair_swap(eta_first, "eta", 0)
        xi_b = pair_swap(xi_second, "xi", 1)
        below, above = ring_swap(zeta, "zeta")
        xi_a = pair_swap(xi_first, "xi", 0)
        return (eta_b, eta_a, xi_b, xi_a), (below, above)

    block = (rows, nz)
    chunks = 2
    u, tables, metrics, jacobian, prim, mass, *sends = call(
        functools.partial(primitive_kernel, grid),
        [like(u), like(tables), like(metrics), like(jacobian), (4, *block), (3, *block)]
        + [(2 * 5, nx, nz)] * 2
        + [(2 * 5, ny, nz)] * 2
        + [(5, TILE, LANES)],
        u, tables, metrics, jacobian,
        scratch=[pltpu.SemaphoreType.DMA((chunks, 5)), pltpu.SemaphoreType.DMA((11,))],
        far=(0, 1, 2, 3),
    )
    sides, ends = exchange(*sends)
    xi_source, eta_source, own = call(
        functools.partial(primitive_source_kernel, grid), [(5, *block)] * 3, prim, mass, tables,
    )
    slopes, mass_total = call(
        functools.partial(slope_kernel, grid),
        [(2, 4, *block), block],
        xi_source, eta_source, own, *sides,
    )
    contra, mass, *eta_sends = call(
        functools.partial(flux_kernel, grid),
        [(3, 4, *block), block] + [(2 * 4 + WIDTH, nx, nz)] * 2,
        u, prim, metrics, jacobian, slopes, own, mass_total, *ends, tables,
        scratch=[pltpu.VMEM((4, *block), jnp.float32)],
    )
    sends = call(
        functools.partial(contra_sums_kernel, grid),
        [(2 * 4, ny, nz)] * 2 + [(4, TILE, LANES)],
        contra, tables,
    )
    sides, ends = exchange(*eta_sends, *sends)
    xi_source, eta_source, own = call(
        functools.partial(contra_source_kernel, grid), [(4, *block)] * 3, contra, tables,
    )
    (mass_source,) = call(
        functools.partial(source_kernel, grid, eta_sources), [(1, *block)], mass.reshape(1, *block),
    )
    (total,) = call(
        functools.partial(divergence_kernel, grid),
        [(4, *block)],
        xi_source, eta_source, own, *sides,
    )
    state, eta_first, eta_second = call(
        functools.partial(step_kernel, grid),
        [(4, *block)] + [(4 * WIDTH, nx, nz)] * 2,
        u, jacobian, total, *ends, tables,
    )
    eta_b = pair_swap(eta_second, "eta", 1)
    eta_a = pair_swap(eta_first, "eta", 0)
    mass, mass_source, xi_first, xi_second = call(
        functools.partial(face_kernel, grid),
        [(1, *block)] * 2 + [(5 * WIDTH, ny, nz)] * 2,
        state, mass_source, sides[1], sides[0],
    )
    xi_b = pair_swap(xi_second, "xi", 1)
    xi_a = pair_swap(xi_first, "xi", 0)
    (source,) = call(functools.partial(source_kernel, grid, eta_sources), [(4, *block)], state)
    (mass_part,) = call(
        functools.partial(mass_xi_kernel, grid), [(1, *block)], mass_source, xi_a, xi_b, tables,
    )
    layers = 5 * WIDTH * ny
    halo_first, halo_second = call(
        functools.partial(halo_source_kernel, grid),
        [(ny * PLANES, nz)] * 2,
        xi_a.reshape(layers, nz), xi_b.reshape(layers, nz),
    )
    edge_first, edge_second = call(
        functools.partial(edge_kernel, grid), [(2 * WIDTH * PLANES, nz)] * 2, source, eta_a, eta_b,
    )
    edge_b = pair_swap(edge_second, "xi", 1)
    edge_a = pair_swap(edge_first, "xi", 0)
    state, zeta, corner_first, corner_second = call(
        functools.partial(eta_filter_kernel, grid),
        [(4, *block), (nx * TILE, LANES)] + [(WIDTH, TILE, LANES)] * 2,
        source, mass, eta_b, eta_a,
    )
    ends = ring_swap(zeta, "zeta")
    edges_b = diagonal_swap(corner_second, 1)
    edges_a = diagonal_swap(corner_first, 0)
    (source,) = call(functools.partial(source_kernel, grid, xi_sources), [(4, *block)], state)
    (state,) = call(
        functools.partial(xi_filter_kernel, grid),
        [(4, *block)],
        source, halo_first, halo_second, edge_b, edge_a, tables,
        scratch=[pltpu.VMEM((PLANES * ny, nz), jnp.float32)] * 2,
    )
    edges = [edge.reshape(WIDTH * TILE, LANES) for edge in (*edges_a, *edges_b)]
    (result,) = call(
        functools.partial(zeta_filter_kernel, grid),
        [(5, *block)],
        mass_part, state, *edges[2:], *ends, *edges[:2], tables,
        scratch=[pltpu.VMEM((5, *block), jnp.float32), pltpu.SemaphoreType.DMA((5,))],
        far_outs=(0,),
    )
    return result.reshape(5, nx, ny, nz)


def solution(mesh):
    in_specs = (
        P(None, "xi", "eta", "zeta"),
        P(None, None, "xi", "eta", "zeta"),
        P("xi", "eta", "zeta"),
    )
    out_specs = P(None, "xi", "eta", "zeta")
    return jax.shard_map(local, mesh=mesh, in_specs=in_specs, out_specs=out_specs, check_vma=False)
```

```python
import functools

import jax
import jax.numpy as jnp
import numpy as np
from jax import lax
from jax.experimental import pallas as pl
from jax.experimental.pallas import tpu as pltpu
from jax.sharding import PartitionSpec as P

WIDTH = 5
LANES = 128
TILE = 8

viscosity = 0.15
conduction = 0.15 * 1.4 / (0.4 * 0.72)
step_duration = 0.08


def derivative_system(length):
    extent = length + 2 * WIDTH
    system = np.eye(extent)
    source = np.zeros((extent, extent))
    for position in range(2, extent - 2):
        system[position, position - 1] = 1.0 / 3.0
        system[position, position + 1] = 1.0 / 3.0
        source[position, position + 1] = 7.0 / 9.0
        source[position, position - 1] = -7.0 / 9.0
        source[position, position + 2] = 1.0 / 36.0
        source[position, position - 2] = -1.0 / 36.0
    source[1, 2] = 0.5
    source[1, 0] = -0.5
    source[extent - 2, extent - 1] = 0.5
    source[extent - 2, extent - 3] = -0.5
    source[0, 1] = 1.0
    source[0, 0] = -1.0
    source[extent - 1, extent - 1] = 1.0
    source[extent - 1, extent - 2] = -1.0
    return system, source


def filter_coefficients():
    strength = 0.4
    return [
        (193.0 + 126.0 * strength) / 256.0,
        (105.0 + 302.0 * strength) / 256.0,
        15.0 * (2.0 * strength - 1.0) / 64.0,
        45.0 * (1.0 - 2.0 * strength) / 512.0,
        5.0 * (2.0 * strength - 1.0) / 256.0,
        (1.0 - 2.0 * strength) / 512.0,
    ]


def filter_system(length):
    strength = 0.4
    coeffs = filter_coefficients()
    extent = length + 2 * WIDTH
    system = np.eye(extent)
    source = np.eye(extent)
    for position in range(5, extent - 5):
        system[position, position - 1] = strength
        system[position, position + 1] = strength
        source[position, position] = coeffs[0]
        for offset in range(1, 6):
            source[position, position + offset] = coeffs[offset] / 2.0
            source[position, position - offset] = coeffs[offset] / 2.0
    return system, source


def own_rows(system, source, length):
    return np.linalg.solve(system, source)[WIDTH : WIDTH + length]


def derivative_parts(length):
    system, source = derivative_system(length)
    halo = np.linalg.solve(system[:WIDTH, :WIDTH], source[:WIDTH])
    row = source[WIDTH] - system[WIDTH, WIDTH - 1] * halo[WIDTH - 1]
    pivots = [1.0]
    for position in range(3, WIDTH + length):
        pivots.append(1.0 - 1.0 / 9.0 / pivots[-1])
    return pivots[WIDTH - 2 :], row[:WIDTH], row[WIDTH : WIDTH + 3]


def pad_rows(table):
    return np.concatenate([table, np.zeros((LANES - table.shape[0], table.shape[1]))], axis=0)


def pad_columns(table):
    return np.concatenate([table, np.zeros((table.shape[0], LANES - table.shape[1]))], axis=1)


def zeta_tables(length):
    system, source = derivative_system(length)
    table = own_rows(system, source, length)
    _, edge, _ = derivative_parts(length)
    inverse = np.linalg.inv(system)
    extent = length + 2 * WIDTH
    sums = np.zeros((length, 4))
    sums[length - WIDTH :, 0] = edge
    sums[length - 1, 1] = 1.0
    sums[:WIDTH, 2] = -edge[::-1]
    sums[0, 3] = 1.0
    own = slice(WIDTH, WIDTH + length)
    back = np.stack(
        [
            inverse[own, WIDTH],
            -1.0 / 36.0 * inverse[own, WIDTH + 1],
            inverse[own, extent - WIDTH - 1],
            1.0 / 36.0 * inverse[own, extent - WIDTH - 2],
        ]
    )
    smooth = own_rows(*filter_system(length), length)
    ends = np.concatenate([smooth[:, :WIDTH], smooth[:, WIDTH + length :]], axis=1)
    tables = [table[:, own].T, pad_columns(sums), pad_rows(back), smooth[:, own].T, pad_rows(ends.T)]
    return tables.pop(1).astype(np.float32), np.stack(tables).astype(np.float32)


DERIVE, BACK, SMOOTH, ENDS = range(4)


def twisted_solve(rights, pivots, off):
    count = len(rights)
    half = count // 2
    low = [rights[0]]
    high = [rights[count - 1]]
    for step in range(1, half):
        factor = off / pivots[step - 1]
        low.append(rights[step] - factor * low[-1])
        high.append(rights[count - 1 - step] - factor * high[-1])
    middle = pivots[half - 1]
    det = middle * middle - off * off
    first, second = low[-1], high[-1]
    answer = [None] * count
    answer[half - 1] = (middle / det) * first - (off / det) * second
    answer[half] = (middle / det) * second - (off / det) * first
    for step in range(half - 2, -1, -1):
        scale = 1.0 / pivots[step]
        factor = off / pivots[step]
        answer[step] = scale * low[step] - factor * answer[step + 1]
        answer[count - 1 - step] = scale * high[step] - factor * answer[count - 2 - step]
    return answer


def derive_source(cells):
    count = len(cells)
    _, _, edge = derivative_parts(count)
    near, far = 7.0 / 9.0, 1.0 / 36.0
    rights = [None] * count
    rights[0] = edge[0] * cells[0] + edge[1] * cells[1] + edge[2] * cells[2]
    rights[1] = near * (cells[2] - cells[0]) + far * cells[3]
    for step in range(2, count - 2):
        rights[step] = near * (cells[step + 1] - cells[step - 1]) + far * (
            cells[step + 2] - cells[step - 2]
        )
    rights[count - 2] = near * (cells[count - 1] - cells[count - 3]) - far * cells[count - 4]
    rights[count - 1] = -(
        edge[0] * cells[count - 1] + edge[1] * cells[count - 2] + edge[2] * cells[count - 3]
    )
    return rights


def derive_solve(rights, below, above):
    pivots, _, _ = derivative_parts(len(rights))
    rights = list(rights)
    far = 1.0 / 36.0
    rights[0] = rights[0] + below[0]
    rights[1] = rights[1] - far * below[1]
    rights[-2] = rights[-2] + far * above[1]
    rights[-1] = rights[-1] + above[0]
    return twisted_solve(rights, pivots, 1.0 / 3.0)


def end_sums(cells):
    _, edge, _ = derivative_parts(16)
    total = edge[WIDTH - 1] * cells[0]
    for step in range(1, WIDTH):
        total = total + edge[WIDTH - 1 - step] * cells[step]
    return total, cells[0]


def smooth_source(cells):
    count = len(cells)
    coeffs = filter_coefficients()
    rights = []
    for step in range(count):
        total = coeffs[0] * cells[step]
        for offset in range(1, WIDTH + 1):
            around = [cells[i] for i in (step - offset, step + offset) if 0 <= i < count]
            around = around[0] + around[1] if len(around) == 2 else around[0]
            total = total + (0.5 * coeffs[offset]) * around
        rights.append(total)
    return rights


def smooth_solve(rights, below, above):
    count = len(rights)
    coeffs = filter_coefficients()
    rights = list(rights)
    for step in range(WIDTH):
        for cell in range(WIDTH - step):
            factor = 0.5 * coeffs[step + cell + 1]
            if step == 0 and cell == 0:
                factor = factor - 0.4
            rights[step] = rights[step] + factor * below[cell]
            rights[count - 1 - step] = rights[count - 1 - step] + factor * above[cell]
    pivots = [1.0]
    for _ in range(count):
        pivots.append(1.0 - 0.16 / pivots[-1])
    return twisted_solve(rights, pivots, 0.4)


def split_values(values):
    high = values.astype(jnp.bfloat16)
    low = (values - high.astype(jnp.float32)).astype(jnp.bfloat16)
    return jnp.concatenate([high, low], axis=1)


def split_weights(table):
    high = table.astype(jnp.bfloat16)
    low = (table - high.astype(jnp.float32)).astype(jnp.bfloat16)
    top = jnp.concatenate([high, low], axis=1)
    return jnp.concatenate([top, jnp.concatenate([high, jnp.zeros_like(low)], axis=1)], axis=0)


def lane_product(values, weights):
    both = jnp.dot(split_values(values), weights, preferred_element_type=jnp.float32)
    return both[:, :LANES] + both[:, LANES:]


class Grid:
    def __init__(self, nx, ny):
        self.nx, self.ny, self.rows = nx, ny, nx * ny
        self.eta_groups = ny // TILE
        self.xi_groups = nx // TILE

    def xi_tile(self, position, group):
        return pl.ds(position * self.ny + group * TILE, TILE)

    def eta_tile(self, position, group):
        return pl.ds(position + group * TILE * self.ny, TILE, stride=self.ny)

    def eta_major(self, position, group):
        return pl.ds(position * self.nx + group * TILE, TILE)


def group_rows(group):
    return pl.ds(group * TILE, TILE)


def odd(axis):
    return lax.rem(lax.axis_index(axis), 2) == 1


def send_sums(read, groups, count, flag, first_ref, second_ref, field):
    for group in range(groups):
        top = end_sums([read(count - 1 - step, group) for step in range(WIDTH)])
        low = end_sums([read(step, group) for step in range(WIDTH)])
        low = (-low[0], low[1])
        for part in range(2):
            first_ref[2 * field + part, group_rows(group), :] = jnp.where(flag, low[part], top[part])
            second_ref[2 * field + part, group_rows(group), :] = jnp.where(flag, top[part], low[part])


def take_sums(first_ref, second_ref, flag, field, group):
    below, above = [], []
    for part in range(2):
        first = first_ref[2 * field + part, group_rows(group), :]
        second = second_ref[2 * field + part, group_rows(group), :]
        below.append(jnp.where(flag, first, second))
        above.append(jnp.where(flag, second, first))
    return below, above


def pack_sums(values, weights, grid):
    sums = lane_product(values, weights)
    parts = []
    for group in range(grid.rows // TILE):
        part = sums[group * TILE : (group + 1) * TILE]
        parts.append(pltpu.roll(part, 4 * group, axis=1) if group else part)
    while len(parts) > 1:
        parts = [sum(parts[i + 1 : i + 2], parts[i]) for i in range(0, len(parts), 2)]
    return parts[0]


def unpack_sums(below, above, grid):
    lane = lax.broadcasted_iota(jnp.int32, below.shape, 1)
    packed = jnp.where(lax.rem(lane, 4) < 2, below, above)
    parts = [packed]
    for group in range(1, grid.rows // TILE):
        parts.append(pltpu.roll(packed, LANES - 4 * group, axis=1))
    return jnp.concatenate(parts, axis=0)


def primitive_kernel(
    grid,
    u_hbm, sums_hbm, metrics_hbm,
    u_ref, sums_ref, metrics_ref,
    prim_ref, mass_ref, eta_first, eta_second, xi_first, xi_second, zeta_ref,
    u_sems, late_sems,
):
    chunks = u_sems.shape[0]
    step = grid.rows // chunks
    weights = pltpu.make_async_copy(sums_hbm, sums_ref, late_sems.at[0])
    weights.start()
    copies = []
    for index in range(chunks):
        rows = pl.ds(index * step, step)
        copy = pltpu.make_async_copy(u_hbm.at[:, rows, :], u_ref.at[:, rows, :], u_sems.at[index])
        copy.start()
        copies.append(copy)
    late = [
        pltpu.make_async_copy(source, result, late_sems.at[index])
        for index, (source, result) in enumerate(
            [(sums_hbm, sums_ref)] + [(metrics_hbm, metrics_ref)]
        )
    ]
    for copy in late[1:]:
        copy.start()
    for index in range(chunks):
        copies[index].wait()
        rows = pl.ds(index * step, step)
        inverse = 1.0 / u_ref[0, rows, :]
        work = None
        for c in range(3):
            momentum = u_ref[1 + c, rows, :]
            speed = momentum * inverse
            prim_ref[c, rows, :] = speed
            work = momentum * speed if work is None else work + momentum * speed
        pressure = 0.4 * (u_ref[4, rows, :] - 0.5 * work)
        prim_ref[3, rows, :] = pressure * inverse

    def send(xi_value, eta_value, field):
        send_sums(
            lambda position, group: eta_value[grid.eta_tile(position, group), :],
            grid.xi_groups, grid.ny, odd("eta"), eta_first, eta_second, field,
        )
        send_sums(
            lambda position, group: xi_value[grid.xi_tile(position, group), :],
            grid.eta_groups, grid.nx, odd("xi"), xi_first, xi_second, field,
        )

    for field in range(4):
        send(prim_ref.at[field], prim_ref.at[field], field)
    weights.wait()
    sums = split_weights(sums_ref[...])
    for field in range(4):
        zeta_ref[field] = pack_sums(prim_ref[field], sums, grid)
    for copy in late[1:]:
        copy.wait()
    for k in range(3):
        for index in range(chunks):
            rows = pl.ds(index * step, step)
            mass_ref[k, rows, :] = (
                metrics_ref[3 * k, rows, :] * u_ref[1, rows, :]
                + metrics_ref[3 * k + 1, rows, :] * u_ref[2, rows, :]
                + metrics_ref[3 * k + 2, rows, :] * u_ref[3, rows, :]
            )
    send(mass_ref.at[0], mass_ref.at[1], 4)
    zeta_ref[4] = pack_sums(mass_ref[2], sums, grid)


def fetch_kernel(count, *refs):
    sources, results, sems = refs[:count], refs[count + 1 : 2 * count + 1], refs[-1]
    copies = [
        pltpu.make_async_copy(source, result, sems.at[index])
        for index, (source, result) in enumerate(zip(sources, results))
    ]
    for copy in copies:
        copy.start()
    for copy in copies:
        copy.wait()


def derive_sources(grid, xi_value, eta_value, zeta_value, derive, field, xi_ref, eta_ref, zeta_ref):
    zeta_ref[field] = lane_product(zeta_value[...], derive)
    for group in range(grid.eta_groups):
        cells = [xi_value[grid.xi_tile(i, group), :] for i in range(grid.nx)]
        for i, value in enumerate(derive_source(cells)):
            xi_ref[field, grid.xi_tile(i, group), :] = value
    for group in range(grid.xi_groups):
        cells = [eta_value[grid.eta_tile(i, group), :] for i in range(grid.ny)]
        for i, value in enumerate(derive_source(cells)):
            eta_ref[field, grid.eta_major(i, group), :] = value


def primitive_source_kernel(grid, prim_ref, mass_ref, tables_ref, *results):
    derive = split_weights(tables_ref[DERIVE])
    for field in range(4):
        derive_sources(grid, *[prim_ref.at[field]] * 3, derive, field, *results)
    derive_sources(grid, *[mass_ref.at[k] for k in range(3)], derive, 4, *results)


def contra_source_kernel(grid, contra_ref, tables_ref, *results):
    derive = split_weights(tables_ref[DERIVE])
    for field in range(4):
        derive_sources(grid, *[contra_ref.at[k, field] for k in range(3)], derive, field, *results)


def xi_derivative(grid, source_ref, xi_a, xi_b, field, group):
    below, above = take_sums(xi_a, xi_b, odd("xi"), field, group)
    rights = [source_ref[field, grid.xi_tile(i, group), :] for i in range(grid.nx)]
    return derive_solve(rights, below, above)


def eta_derivative(grid, source_ref, eta_a, eta_b, field, group):
    below, above = take_sums(eta_a, eta_b, odd("eta"), field, group)
    rights = [source_ref[field, grid.eta_major(i, group), :] for i in range(grid.ny)]
    return derive_solve(rights, below, above)


def add_derivatives(grid, xi_source, eta_source, own_ref, eta_a, eta_b, xi_a, xi_b, field, total_ref):
    for group in range(grid.xi_groups):
        for i, value in enumerate(eta_derivative(grid, eta_source, eta_a, eta_b, field, group)):
            rows = grid.eta_tile(i, group)
            total_ref[rows, :] = own_ref[field, rows, :] + value
    for group in range(grid.eta_groups):
        for i, value in enumerate(xi_derivative(grid, xi_source, xi_a, xi_b, field, group)):
            rows = grid.xi_tile(i, group)
            total_ref[rows, :] = total_ref[rows, :] + value


def slope_kernel(grid, xi_source, eta_source, own_ref, eta_a, eta_b, xi_b, xi_a, slope_ref, mass_total_ref):
    for field in range(4):
        for group in range(grid.eta_groups):
            for i, value in enumerate(xi_derivative(grid, xi_source, xi_a, xi_b, field, group)):
                slope_ref[0, field, grid.xi_tile(i, group), :] = value
        for group in range(grid.xi_groups):
            for i, value in enumerate(eta_derivative(grid, eta_source, eta_a, eta_b, field, group)):
                slope_ref[1, field, grid.eta_tile(i, group), :] = value
    add_derivatives(
        grid, xi_source, eta_source, own_ref, eta_a, eta_b, xi_a, xi_b, 4, mass_total_ref
    )


def flux_kernel(
    grid,
    u_ref, prim_ref, metrics_ref, jacobian_ref, slope_ref, own_ref, mass_total_ref,
    zeta_below, zeta_above, tables_ref,
    contra_ref, mass_ref, eta_first, eta_second,
    zeta_slope_ref,
):
    back = split_weights(tables_ref[BACK])
    for field in range(4):
        halo = unpack_sums(zeta_below[field], zeta_above[field], grid)
        zeta_slope_ref[field] = own_ref[field] + lane_product(halo, back)
    halo = unpack_sums(zeta_below[4], zeta_above[4], grid)
    total = mass_total_ref[...] + lane_product(halo, back)
    mass_ref[...] = u_ref[0] - (step_duration * jacobian_ref[...]) * total
    send_cells(
        lambda position, group: mass_ref[grid.eta_tile(position, group), :],
        grid.xi_groups, grid.ny, odd("eta"), eta_first, eta_second, 2 * 4,
    )

    step = TILE

    def body(index, carry):
        rows = pl.ds(pl.multiple_of(index * step, step), step)
        u = [u_ref[c, rows, :] for c in range(5)]
        speed = [prim_ref[c, rows, :] for c in range(3)]
        pressure = prim_ref[3, rows, :] * u[0]
        metrics = [[metrics_ref[3 * k + j, rows, :] for j in range(3)] for k in range(3)]
        scaled = (viscosity * jacobian_ref[rows, :])
        scaled = [[scaled * metrics[k][j] for j in range(3)] for k in range(3)]
        physical = []
        for c in range(4):
            slopes = [slope_ref[0, c, rows, :], slope_ref[1, c, rows, :], zeta_slope_ref[c, rows, :]]
            physical.append(
                [
                    scaled[0][j] * slopes[0] + scaled[1][j] * slopes[1] + scaled[2][j] * slopes[2]
                    for j in range(3)
                ]
            )
        spread = (2.0 / 3.0) * (physical[0][0] + physical[1][1] + physical[2][2])
        stress = [[None] * 3 for _ in range(3)]
        momentum = [[None] * 3 for _ in range(3)]
        for c in range(3):
            stress[c][c] = (physical[c][c] + physical[c][c]) - spread
            momentum[c][c] = (u[1 + c] * speed[c] + pressure) - stress[c][c]
            for j in range(c):
                stress[c][j] = stress[j][c] = physical[c][j] + physical[j][c]
                momentum[c][j] = momentum[j][c] = u[1 + c] * speed[j] - stress[c][j]
        total = u[4] + pressure
        fluxes = []
        for j in range(3):
            worked = speed[0] * stress[0][j] + speed[1] * stress[1][j] + speed[2] * stress[2][j]
            energy = (total * speed[j] - worked) - (conduction / viscosity) * physical[3][j]
            fluxes.append([momentum[0][j], momentum[1][j], momentum[2][j], energy])
        for k in range(3):
            for f in range(4):
                contra_ref[k, f, rows, :] = (
                    metrics[k][0] * fluxes[0][f]
                    + metrics[k][1] * fluxes[1][f]
                    + metrics[k][2] * fluxes[2][f]
                )
        return carry

    lax.fori_loop(0, grid.rows // step, body, 0, unroll=4)
    for field in range(4):
        send_sums(
            lambda position, group: contra_ref[1, field, grid.eta_tile(position, group), :],
            grid.xi_groups, grid.ny, odd("eta"), eta_first, eta_second, field,
        )


def contra_sums_kernel(grid, contra_ref, sums_ref, xi_first, xi_second, zeta_ref):
    sums = split_weights(sums_ref[...])
    for field in range(4):
        send_sums(
            lambda position, group: contra_ref[0, field, grid.xi_tile(position, group), :],
            grid.eta_groups, grid.nx, odd("xi"), xi_first, xi_second, field,
        )
        zeta_ref[field] = pack_sums(contra_ref[2, field], sums, grid)


def divergence_kernel(grid, xi_source, eta_source, own_ref, eta_a, eta_b, xi_b, xi_a, total_ref):
    for field in range(4):
        add_derivatives(
            grid, xi_source, eta_source, own_ref, eta_a, eta_b, xi_a, xi_b, field, total_ref.at[field]
        )


def step_kernel(
    grid,
    u_ref, jacobian_ref, total_ref, zeta_below, zeta_above, tables_ref,
    state_ref, eta_first, eta_second,
):
    back = split_weights(tables_ref[BACK])
    scale = step_duration * jacobian_ref[...]
    for field in range(4):
        halo = unpack_sums(zeta_below[field], zeta_above[field], grid)
        total = total_ref[field] + lane_product(halo, back)
        state_ref[field] = u_ref[1 + field] - scale * total
        send_cells(
            lambda position, group: state_ref[field, grid.eta_tile(position, group), :],
            grid.xi_groups, grid.ny, odd("eta"), eta_first, eta_second, WIDTH * field,
        )


def send_cells(read, groups, count, flag, first_ref, second_ref, base):
    for group in range(groups):
        for step in range(WIDTH):
            low = read(step, group)
            top = read(count - 1 - step, group)
            first_ref[base + step, group_rows(group), :] = jnp.where(flag, low, top)
            second_ref[base + step, group_rows(group), :] = jnp.where(flag, top, low)


def take_cells(first_ref, second_ref, flag, base, group):
    below, above = [], []
    for step in range(WIDTH):
        first = first_ref[base + step, group_rows(group), :]
        second = second_ref[base + step, group_rows(group), :]
        below.append(jnp.where(flag, first, second))
        above.append(jnp.where(flag, second, first))
    return below, above


def send_faces(grid, read, flag, first_ref, second_ref, base):
    for group in range(grid.eta_groups):
        for step in range(WIDTH):
            low = read(step, group)
            top = read(grid.nx - WIDTH + step, group)
            first_ref[base + step, group_rows(group), :] = jnp.where(flag, low, top)
            second_ref[base + step, group_rows(group), :] = jnp.where(flag, top, low)


def take_faces(first_ref, second_ref, flag, base, group):
    below, above = [], []
    for step in range(WIDTH):
        low, top = base + step, base + WIDTH - 1 - step
        rows = group_rows(group)
        below.append(jnp.where(flag, first_ref[top, rows, :], second_ref[top, rows, :]))
        above.append(jnp.where(flag, second_ref[low, rows, :], first_ref[low, rows, :]))
    return below, above


def eta_sources(grid, state_ref, source_ref):
    for group in range(grid.xi_groups):
        cells = [state_ref[grid.eta_tile(i, group), :] for i in range(grid.ny)]
        for i, value in enumerate(smooth_source(cells)):
            source_ref[grid.eta_major(i, group), :] = value


def xi_sources(grid, state_ref, source_ref):
    for group in range(grid.eta_groups):
        cells = [state_ref[grid.xi_tile(i, group), :] for i in range(grid.nx)]
        for i, value in enumerate(smooth_source(cells)):
            source_ref[grid.xi_tile(i, group), :] = value


def eta_filter(grid, source_ref, eta_a, eta_b, base, result_ref):
    for group in range(grid.xi_groups):
        below, above = take_cells(eta_a, eta_b, odd("eta"), base, group)
        rights = [source_ref[grid.eta_major(i, group), :] for i in range(grid.ny)]
        for i, value in enumerate(smooth_solve(rights, below, above)):
            result_ref[grid.eta_tile(i, group), :] = value


def xi_filter(grid, source_ref, xi_a, xi_b, base, smooth, result_ref):
    for group in range(grid.eta_groups):
        below, above = take_faces(xi_a, xi_b, odd("xi"), base, group)
        rights = [source_ref[grid.xi_tile(i, group), :] for i in range(grid.nx)]
        for i, value in enumerate(smooth_solve(rights, below, above)):
            result_ref[grid.xi_tile(i, group), :] = value
    result_ref[...] = lane_product(result_ref[...], smooth)


def source_kernel(grid, form, state_ref, source_ref):
    for field in range(state_ref.shape[0]):
        form(grid, state_ref.at[field], source_ref.at[field])


def face_kernel(
    grid, state_ref, source_ref, eta_a, eta_b, result_ref, next_ref, xi_first, xi_second
):
    flag = odd("xi")
    eta_filter(grid, source_ref.at[0], eta_a, eta_b, 2 * 4, result_ref.at[0])
    for field in range(5):
        values = state_ref.at[field] if field < 4 else result_ref.at[0]
        send_faces(
            grid, lambda position, group: values[grid.xi_tile(position, group), :],
            flag, xi_first, xi_second, WIDTH * field,
        )
    xi_sources(grid, result_ref.at[0], next_ref.at[0])


PLANES = 3 * TILE


def halo_source_kernel(grid, first_ref, second_ref, first_source, second_source):
    for faces, source in ((first_ref, first_source), (second_ref, second_source)):
        for tile in range(PLANES // TILE):
            cells = [
                faces[pl.ds(tile * TILE * grid.ny + i, TILE, stride=grid.ny), :] for i in range(grid.ny)
            ]
            for i, value in enumerate(smooth_source(cells)):
                source[pl.ds(i * PLANES + tile * TILE, TILE), :] = value


def edge_kernel(grid, order_ref, eta_b, eta_a, first_ref, second_ref):
    flag = odd("xi")
    eta_flag = odd("eta")
    for side in range(2):
        for step in range(WIDTH):
            start = (side * WIDTH + step) * PLANES
            for field in range(4):
                one, other = eta_a[WIDTH * field + step], eta_b[WIDTH * field + step]
                cells = jnp.where(eta_flag, other, one) if side else jnp.where(eta_flag, one, other)
                low, top = cells[:WIDTH], cells[grid.nx - WIDTH :]
                rows = pl.ds(start + WIDTH * field, WIDTH)
                first_ref[rows, :] = jnp.where(flag, low, top)
                second_ref[rows, :] = jnp.where(flag, top, low)
            rest = pl.ds(start + 4 * WIDTH, PLANES - 4 * WIDTH)
            first_ref[rest, :] = jnp.zeros((PLANES - 4 * WIDTH, LANES), jnp.float32)
            second_ref[rest, :] = jnp.zeros((PLANES - 4 * WIDTH, LANES), jnp.float32)


def filter_halo(grid, source_ref, edge_ref, result_ref):
    for tile in range(PLANES // TILE):
        ends = [
            [edge_ref[pl.ds((side * WIDTH + i) * PLANES + tile * TILE, TILE), :] for i in range(WIDTH)]
            for side in range(2)
        ]
        rights = [source_ref[pl.ds(i * PLANES + tile * TILE, TILE), :] for i in range(grid.ny)]
        for i, value in enumerate(smooth_solve(rights, *ends)):
            result_ref[pl.ds(tile * TILE * grid.ny + i, TILE, stride=grid.ny), :] = value


def eta_filter_kernel(
    grid, source_ref, mass_ref, eta_a, eta_b,
    result_ref, zeta_ref, edge_first, edge_second,
):
    flag = odd("xi")
    for field in range(4):
        eta_filter(grid, source_ref.at[field], eta_a, eta_b, WIDTH * field, result_ref.at[field])
    lane = lax.broadcasted_iota(jnp.int32, (TILE, LANES), 1)
    for position in range(grid.nx):
        packed = None
        for slot in range(5 * grid.eta_groups):
            field, group = slot // grid.eta_groups, slot % grid.eta_groups
            rows = grid.xi_tile(position, group)
            part = result_ref[field - 1, rows, :] if field else mass_ref[0, rows, :]
            part = pltpu.roll(part, WIDTH * (2 * slot + 1), axis=1)
            packed = part if packed is None else jnp.where(lane >= 2 * WIDTH * slot, part, packed)
        zeta_ref[group_rows(position), :] = packed
    send_cells(
        lambda position, group: zeta_ref[group_rows(position), :],
        1, grid.nx, flag, edge_first, edge_second, 0,
    )


def mass_xi_kernel(grid, source_ref, xi_a, xi_b, tables_ref, result_ref):
    smooth = split_weights(tables_ref[SMOOTH])
    xi_filter(grid, source_ref.at[0], xi_a, xi_b, WIDTH * 4, smooth, result_ref.at[0])


def xi_filter_kernel(
    grid, source_ref, first_source, second_source, edge_b, edge_a, tables_ref, result_ref,
    first_ref, second_ref,
):
    smooth = split_weights(tables_ref[SMOOTH])
    filter_halo(grid, first_source, edge_a, first_ref)
    filter_halo(grid, second_source, edge_b, second_ref)

    class Layers:
        def __init__(self, ref):
            self.ref = ref

        def __getitem__(self, index):
            layer, rows, _ = index
            return self.ref[pl.ds(layer * grid.ny + rows.start, rows.size), :]

    for field in range(4):
        xi_filter(
            grid, source_ref.at[field], Layers(first_ref), Layers(second_ref), WIDTH * field, smooth,
            result_ref.at[field],
        )


def zeta_filter_kernel(
    grid,
    mass_ref, state_ref, b_below, b_above, below_ref, above_ref, a_below, a_above, tables_ref,
    result_hbm,
    result_ref, sems,
):
    ends = split_weights(tables_ref[ENDS])
    flag = odd("xi")
    lane = lax.broadcasted_iota(jnp.int32, (TILE, LANES), 1)
    from_below = lax.rem(lane, 2 * WIDTH) < WIDTH

    def merge(below, above, index):
        return jnp.where(from_below, below[group_rows(index), :], above[group_rows(index), :])

    low, high = [], []
    for step in range(WIDTH):
        first, second = merge(a_below, a_above, step), merge(b_below, b_above, step)
        low.append(jnp.where(flag, first, second))
        high.append(jnp.where(flag, second, first))
    cells = [merge(below_ref, above_ref, position) for position in range(grid.nx)]
    cells = smooth_solve(smooth_source(cells), low, high)
    copies = []
    for field in range(5):
        parts = []
        for packed in cells:
            for group in range(grid.eta_groups):
                slot = field * grid.eta_groups + group
                parts.append(pltpu.roll(packed, LANES - 2 * WIDTH * slot, axis=1) if slot else packed)
        halo = jnp.concatenate(parts, axis=0)
        own = state_ref[field - 1] if field else mass_ref[0]
        result_ref[field] = own + lane_product(halo, ends)
        copy = pltpu.make_async_copy(result_ref.at[field], result_hbm.at[field], sems.at[field])
        copy.start()
        copies.append(copy)
    for copy in copies:
        copy.wait()


def pair_swap(value, axis, parity):
    count = lax.axis_size(axis)
    pairs = []
    for index in range(count):
        step = 1 if index % 2 == parity else -1
        pairs.append((index, (index + step) % count))
    return lax.ppermute(value, axis, pairs)


def diagonal_swap(value, parity):
    nx, nz = lax.axis_size("xi"), lax.axis_size("zeta")

    def send(shift):
        pairs = []
        for i in range(nx):
            partner = (i + (1 if i % 2 == parity else -1)) % nx
            for k in range(nz):
                pairs.append((i * nz + k, partner * nz + (k + shift) % nz))
        return lax.ppermute(value, ("xi", "zeta"), pairs)

    below = send(1)
    return (below, below) if nz == 2 else (below, send(-1))


def ring_swap(value, axis):
    count = lax.axis_size(axis)
    if count == 2:
        other = lax.ppermute(value, axis, [(0, 1), (1, 0)])
        return other, other
    up = [(index, (index + 1) % count) for index in range(count)]
    down = [(index, (index - 1) % count) for index in range(count)]
    return lax.ppermute(value, axis, up), lax.ppermute(value, axis, down)


HBM = pltpu.MemorySpace.HBM


def call(kernel, outs, *operands, scratch=(), cost=1.0, far=(), far_outs=()):
    shapes = [
        out if isinstance(out, jax.ShapeDtypeStruct) else jax.ShapeDtypeStruct(out, jnp.float32)
        for out in outs
    ]
    near = pltpu.MemorySpace.VMEM
    operands = [
        pltpu.with_memory_space_constraint(value, HBM) if index in far else value
        for index, value in enumerate(operands)
    ]
    return pl.pallas_call(
        kernel,
        out_shape=shapes,
        in_specs=[
            pl.BlockSpec(memory_space=HBM if index in far else near) for index in range(len(operands))
        ],
        out_specs=[
            pl.BlockSpec(memory_space=HBM if index in far_outs else near) for index in range(len(outs))
        ],
        scratch_shapes=scratch,
        cost_estimate=pl.CostEstimate(flops=0, transcendentals=0, bytes_accessed=int(cost * 3.6e6)),
        compiler_params=pltpu.CompilerParams(vmem_limit_bytes=20 * 2**20),
    )(*operands)


def like(value):
    return jax.ShapeDtypeStruct(value.shape, value.dtype)


def local(conserved_solution, metrics, jacobian):
    _, nx, ny, nz = conserved_solution.shape
    grid = Grid(nx, ny)
    rows = grid.rows
    u = conserved_solution.reshape(5, rows, nz)
    metrics = metrics.reshape(9, rows, nz)
    jacobian = jacobian.reshape(rows, nz)
    sums, tables = (jnp.asarray(table) for table in zeta_tables(nz))

    def exchange(eta_first, eta_second, xi_first, xi_second, zeta):
        eta_b = pair_swap(eta_second, "eta", 1)
        eta_a = pair_swap(eta_first, "eta", 0)
        xi_b = pair_swap(xi_second, "xi", 1)
        below, above = ring_swap(zeta, "zeta")
        xi_a = pair_swap(xi_first, "xi", 0)
        return (eta_a, eta_b, xi_b, xi_a), (below, above)

    block = (rows, nz)
    chunks = 2
    u, sums, metrics, prim, mass, *sends = call(
        functools.partial(primitive_kernel, grid),
        [like(u), like(sums), like(metrics), (4, *block), (3, *block)]
        + [(2 * 5, nx, nz)] * 2
        + [(2 * 5, ny, nz)] * 2
        + [(5, TILE, LANES)],
        u, sums, metrics,
        scratch=[pltpu.SemaphoreType.DMA((chunks,)), pltpu.SemaphoreType.DMA((10,))],
        far=(0, 1, 2),
    )
    tables, jacobian = call(
        functools.partial(fetch_kernel, 2),
        [like(tables), like(jacobian)],
        tables, jacobian, sends[-1],
        scratch=[pltpu.SemaphoreType.DMA((2,))],
        far=(0, 1),
    )
    sides, ends = exchange(*sends)
    xi_source, eta_source, own = call(
        functools.partial(primitive_source_kernel, grid), [(5, *block)] * 3, prim, mass, tables,
    )
    slopes, mass_total = call(
        functools.partial(slope_kernel, grid),
        [(2, 4, *block), block],
        xi_source, eta_source, own, *sides,
    )
    contra, mass, *eta_sends = call(
        functools.partial(flux_kernel, grid),
        [(3, 4, *block), block] + [(2 * 4 + WIDTH, nx, nz)] * 2,
        u, prim, metrics, jacobian, slopes, own, mass_total, *ends, tables,
        scratch=[pltpu.VMEM((4, *block), jnp.float32)],
    )
    sends = call(
        functools.partial(contra_sums_kernel, grid),
        [(2 * 4, ny, nz)] * 2 + [(4, TILE, LANES)],
        contra, sums,
    )
    sides, ends = exchange(*eta_sends, *sends)
    xi_source, eta_source, own = call(
        functools.partial(contra_source_kernel, grid), [(4, *block)] * 3, contra, tables,
    )
    (mass_source,) = call(
        functools.partial(source_kernel, grid, eta_sources), [(1, *block)], mass.reshape(1, *block),
    )
    (total,) = call(
        functools.partial(divergence_kernel, grid),
        [(4, *block)],
        xi_source, eta_source, own, *sides,
    )
    state, eta_first, eta_second = call(
        functools.partial(step_kernel, grid),
        [(4, *block)] + [(4 * WIDTH, nx, nz)] * 2,
        u, jacobian, total, *ends, tables,
    )
    eta_b = pair_swap(eta_second, "eta", 1)
    eta_a = pair_swap(eta_first, "eta", 0)
    mass, mass_source, xi_first, xi_second = call(
        functools.partial(face_kernel, grid),
        [(1, *block)] * 2 + [(5 * WIDTH, ny, nz)] * 2,
        state, mass_source, sides[0], sides[1],
    )
    xi_b = pair_swap(xi_second, "xi", 1)
    xi_a = pair_swap(xi_first, "xi", 0)
    (source,) = call(functools.partial(source_kernel, grid, eta_sources), [(4, *block)], state)
    (mass_part,) = call(
        functools.partial(mass_xi_kernel, grid), [(1, *block)], mass_source, xi_a, xi_b, tables,
    )
    layers = 5 * WIDTH * ny
    halo_first, halo_second = call(
        functools.partial(halo_source_kernel, grid),
        [(ny * PLANES, nz)] * 2,
        xi_a.reshape(layers, nz), xi_b.reshape(layers, nz),
    )
    edge_first, edge_second = call(
        functools.partial(edge_kernel, grid), [(2 * WIDTH * PLANES, nz)] * 2, source, eta_b, eta_a,
    )
    edge_b = pair_swap(edge_second, "xi", 1)
    edge_a = pair_swap(edge_first, "xi", 0)
    state, zeta, corner_first, corner_second = call(
        functools.partial(eta_filter_kernel, grid),
        [(4, *block), (nx * TILE, LANES)] + [(WIDTH, TILE, LANES)] * 2,
        source, mass, eta_a, eta_b,
    )
    ends = ring_swap(zeta, "zeta")
    edges_b = diagonal_swap(corner_second, 1)
    edges_a = diagonal_swap(corner_first, 0)
    (source,) = call(functools.partial(source_kernel, grid, xi_sources), [(4, *block)], state)
    (state,) = call(
        functools.partial(xi_filter_kernel, grid),
        [(4, *block)],
        source, halo_first, halo_second, edge_b, edge_a, tables,
        scratch=[pltpu.VMEM((PLANES * ny, nz), jnp.float32)] * 2,
    )
    edges = [edge.reshape(WIDTH * TILE, LANES) for edge in (*edges_a, *edges_b)]
    (result,) = call(
        functools.partial(zeta_filter_kernel, grid),
        [(5, *block)],
        mass_part, state, *edges[2:], *ends, *edges[:2], tables,
        scratch=[pltpu.VMEM((5, *block), jnp.float32), pltpu.SemaphoreType.DMA((5,))],
        far_outs=(0,),
    )
    return result.reshape(5, nx, ny, nz)


def solution(mesh):
    in_specs = (
        P(None, "xi", "eta", "zeta"),
        P(None, None, "xi", "eta", "zeta"),
        P("xi", "eta", "zeta"),
    )
    out_specs = P(None, "xi", "eta", "zeta")
    return jax.shard_map(local, mesh=mesh, in_specs=in_specs, out_specs=out_specs, check_vma=False)
```

```python
import functools

import jax
import jax.numpy as jnp
import numpy as np
from jax import lax
from jax.experimental import pallas as pl
from jax.experimental.pallas import tpu as pltpu
from jax.sharding import PartitionSpec as P

WIDTH = 5
LANES = 128
TILE = 8

viscosity = 0.15
conduction = 0.15 * 1.4 / (0.4 * 0.72)
step_duration = 0.08


def derivative_system(length):
    extent = length + 2 * WIDTH
    system = np.eye(extent)
    source = np.zeros((extent, extent))
    for position in range(2, extent - 2):
        system[position, position - 1] = 1.0 / 3.0
        system[position, position + 1] = 1.0 / 3.0
        source[position, position + 1] = 7.0 / 9.0
        source[position, position - 1] = -7.0 / 9.0
        source[position, position + 2] = 1.0 / 36.0
        source[position, position - 2] = -1.0 / 36.0
    source[1, 2] = 0.5
    source[1, 0] = -0.5
    source[extent - 2, extent - 1] = 0.5
    source[extent - 2, extent - 3] = -0.5
    source[0, 1] = 1.0
    source[0, 0] = -1.0
    source[extent - 1, extent - 1] = 1.0
    source[extent - 1, extent - 2] = -1.0
    return system, source


def filter_coefficients():
    strength = 0.4
    return [
        (193.0 + 126.0 * strength) / 256.0,
        (105.0 + 302.0 * strength) / 256.0,
        15.0 * (2.0 * strength - 1.0) / 64.0,
        45.0 * (1.0 - 2.0 * strength) / 512.0,
        5.0 * (2.0 * strength - 1.0) / 256.0,
        (1.0 - 2.0 * strength) / 512.0,
    ]


def filter_system(length):
    strength = 0.4
    coeffs = filter_coefficients()
    extent = length + 2 * WIDTH
    system = np.eye(extent)
    source = np.eye(extent)
    for position in range(5, extent - 5):
        system[position, position - 1] = strength
        system[position, position + 1] = strength
        source[position, position] = coeffs[0]
        for offset in range(1, 6):
            source[position, position + offset] = coeffs[offset] / 2.0
            source[position, position - offset] = coeffs[offset] / 2.0
    return system, source


def own_rows(system, source, length):
    return np.linalg.solve(system, source)[WIDTH : WIDTH + length]


def derivative_parts(length):
    system, source = derivative_system(length)
    halo = np.linalg.solve(system[:WIDTH, :WIDTH], source[:WIDTH])
    row = source[WIDTH] - system[WIDTH, WIDTH - 1] * halo[WIDTH - 1]
    pivots = [1.0]
    for position in range(3, WIDTH + length):
        pivots.append(1.0 - 1.0 / 9.0 / pivots[-1])
    return pivots[WIDTH - 2 :], row[:WIDTH], row[WIDTH : WIDTH + 3]


def pad_rows(table):
    return np.concatenate([table, np.zeros((LANES - table.shape[0], table.shape[1]))], axis=0)


def pad_columns(table):
    return np.concatenate([table, np.zeros((table.shape[0], LANES - table.shape[1]))], axis=1)


def zeta_tables(length):
    system, source = derivative_system(length)
    table = own_rows(system, source, length)
    _, edge, _ = derivative_parts(length)
    inverse = np.linalg.inv(system)
    extent = length + 2 * WIDTH
    sums = np.zeros((length, 4))
    sums[length - WIDTH :, 0] = edge
    sums[length - 1, 1] = 1.0
    sums[:WIDTH, 2] = -edge[::-1]
    sums[0, 3] = 1.0
    own = slice(WIDTH, WIDTH + length)
    back = np.stack(
        [
            inverse[own, WIDTH],
            -1.0 / 36.0 * inverse[own, WIDTH + 1],
            inverse[own, extent - WIDTH - 1],
            1.0 / 36.0 * inverse[own, extent - WIDTH - 2],
        ]
    )
    smooth = own_rows(*filter_system(length), length)
    ends = np.concatenate([smooth[:, :WIDTH], smooth[:, WIDTH + length :]], axis=1)
    tables = [table[:, own].T, pad_columns(sums), pad_rows(back), smooth[:, own].T, pad_rows(ends.T)]
    return tables.pop(1).astype(np.float32), np.stack(tables).astype(np.float32)


DERIVE, BACK, SMOOTH, ENDS = range(4)


def twisted_solve(rights, pivots, off):
    count = len(rights)
    half = count // 2
    low = [rights[0]]
    high = [rights[count - 1]]
    for step in range(1, half):
        factor = off / pivots[step - 1]
        low.append(rights[step] - factor * low[-1])
        high.append(rights[count - 1 - step] - factor * high[-1])
    middle = pivots[half - 1]
    det = middle * middle - off * off
    first, second = low[-1], high[-1]
    answer = [None] * count
    answer[half - 1] = (middle / det) * first - (off / det) * second
    answer[half] = (middle / det) * second - (off / det) * first
    for step in range(half - 2, -1, -1):
        scale = 1.0 / pivots[step]
        factor = off / pivots[step]
        answer[step] = scale * low[step] - factor * answer[step + 1]
        answer[count - 1 - step] = scale * high[step] - factor * answer[count - 2 - step]
    return answer


def derive_source(cells):
    count = len(cells)
    _, _, edge = derivative_parts(count)
    near, far = 7.0 / 9.0, 1.0 / 36.0
    rights = [None] * count
    rights[0] = edge[0] * cells[0] + edge[1] * cells[1] + edge[2] * cells[2]
    rights[1] = near * (cells[2] - cells[0]) + far * cells[3]
    for step in range(2, count - 2):
        rights[step] = near * (cells[step + 1] - cells[step - 1]) + far * (
            cells[step + 2] - cells[step - 2]
        )
    rights[count - 2] = near * (cells[count - 1] - cells[count - 3]) - far * cells[count - 4]
    rights[count - 1] = -(
        edge[0] * cells[count - 1] + edge[1] * cells[count - 2] + edge[2] * cells[count - 3]
    )
    return rights


def derive_solve(rights, below, above):
    pivots, _, _ = derivative_parts(len(rights))
    rights = list(rights)
    far = 1.0 / 36.0
    rights[0] = rights[0] + below[0]
    rights[1] = rights[1] - far * below[1]
    rights[-2] = rights[-2] + far * above[1]
    rights[-1] = rights[-1] + above[0]
    return twisted_solve(rights, pivots, 1.0 / 3.0)


def end_sums(cells):
    _, edge, _ = derivative_parts(16)
    total = edge[WIDTH - 1] * cells[0]
    for step in range(1, WIDTH):
        total = total + edge[WIDTH - 1 - step] * cells[step]
    return total, cells[0]


def smooth_source(cells):
    count = len(cells)
    coeffs = filter_coefficients()
    rights = []
    for step in range(count):
        total = coeffs[0] * cells[step]
        for offset in range(1, WIDTH + 1):
            around = [cells[i] for i in (step - offset, step + offset) if 0 <= i < count]
            around = around[0] + around[1] if len(around) == 2 else around[0]
            total = total + (0.5 * coeffs[offset]) * around
        rights.append(total)
    return rights


def smooth_solve(rights, below, above):
    count = len(rights)
    coeffs = filter_coefficients()
    rights = list(rights)
    for step in range(WIDTH):
        for cell in range(WIDTH - step):
            factor = 0.5 * coeffs[step + cell + 1]
            if step == 0 and cell == 0:
                factor = factor - 0.4
            rights[step] = rights[step] + factor * below[cell]
            rights[count - 1 - step] = rights[count - 1 - step] + factor * above[cell]
    pivots = [1.0]
    for _ in range(count):
        pivots.append(1.0 - 0.16 / pivots[-1])
    return twisted_solve(rights, pivots, 0.4)


def split_values(values):
    high = values.astype(jnp.bfloat16)
    low = (values - high.astype(jnp.float32)).astype(jnp.bfloat16)
    return jnp.concatenate([high, low], axis=1)


def split_weights(table):
    high = table.astype(jnp.bfloat16)
    low = (table - high.astype(jnp.float32)).astype(jnp.bfloat16)
    top = jnp.concatenate([high, low], axis=1)
    return jnp.concatenate([top, jnp.concatenate([high, jnp.zeros_like(low)], axis=1)], axis=0)


def lane_product(values, weights):
    both = jnp.dot(split_values(values), weights, preferred_element_type=jnp.float32)
    return both[:, :LANES] + both[:, LANES:]


class Grid:
    def __init__(self, nx, ny):
        self.nx, self.ny, self.rows = nx, ny, nx * ny
        self.eta_groups = ny // TILE
        self.xi_groups = nx // TILE

    def xi_tile(self, position, group):
        return pl.ds(position * self.ny + group * TILE, TILE)

    def eta_tile(self, position, group):
        return pl.ds(position + group * TILE * self.ny, TILE, stride=self.ny)

    def eta_major(self, position, group):
        return pl.ds(position * self.nx + group * TILE, TILE)


def group_rows(group):
    return pl.ds(group * TILE, TILE)


def odd(axis):
    return lax.rem(lax.axis_index(axis), 2) == 1


def send_sums(read, groups, count, flag, first_ref, second_ref, field):
    for group in range(groups):
        top = end_sums([read(count - 1 - step, group) for step in range(WIDTH)])
        low = end_sums([read(step, group) for step in range(WIDTH)])
        low = (-low[0], low[1])
        for part in range(2):
            first_ref[2 * field + part, group_rows(group), :] = jnp.where(flag, low[part], top[part])
            second_ref[2 * field + part, group_rows(group), :] = jnp.where(flag, top[part], low[part])


def take_sums(first_ref, second_ref, flag, field, group):
    below, above = [], []
    for part in range(2):
        first = first_ref[2 * field + part, group_rows(group), :]
        second = second_ref[2 * field + part, group_rows(group), :]
        below.append(jnp.where(flag, first, second))
        above.append(jnp.where(flag, second, first))
    return below, above


def pack_sums(values, weights, grid):
    sums = lane_product(values, weights)
    parts = []
    for group in range(grid.rows // TILE):
        part = sums[group * TILE : (group + 1) * TILE]
        parts.append(pltpu.roll(part, 4 * group, axis=1) if group else part)
    while len(parts) > 1:
        parts = [sum(parts[i + 1 : i + 2], parts[i]) for i in range(0, len(parts), 2)]
    return parts[0]


def unpack_sums(below, above, grid):
    lane = lax.broadcasted_iota(jnp.int32, below.shape, 1)
    packed = jnp.where(lax.rem(lane, 4) < 2, below, above)
    parts = [packed]
    for group in range(1, grid.rows // TILE):
        parts.append(pltpu.roll(packed, LANES - 4 * group, axis=1))
    return jnp.concatenate(parts, axis=0)


def primitive_kernel(
    grid,
    u_hbm, sums_hbm, metrics_hbm,
    u_ref, sums_ref, metrics_ref,
    prim_ref, mass_ref, eta_first, eta_second, xi_first, xi_second, zeta_ref,
    u_sems, late_sems,
):
    chunks = u_sems.shape[0]
    step = grid.rows // chunks
    weights = pltpu.make_async_copy(sums_hbm, sums_ref, late_sems.at[0])
    weights.start()
    copies = []
    for index in range(chunks):
        rows = pl.ds(index * step, step)
        copy = pltpu.make_async_copy(u_hbm.at[:, rows, :], u_ref.at[:, rows, :], u_sems.at[index])
        copy.start()
        copies.append(copy)
    late = [
        pltpu.make_async_copy(source, result, late_sems.at[index])
        for index, (source, result) in enumerate(
            [(sums_hbm, sums_ref)] + [(metrics_hbm, metrics_ref)]
        )
    ]
    for copy in late[1:]:
        copy.start()
    for index in range(chunks):
        copies[index].wait()
        rows = pl.ds(index * step, step)
        inverse = 1.0 / u_ref[0, rows, :]
        work = None
        for c in range(3):
            momentum = u_ref[1 + c, rows, :]
            speed = momentum * inverse
            prim_ref[c, rows, :] = speed
            work = momentum * speed if work is None else work + momentum * speed
        pressure = 0.4 * (u_ref[4, rows, :] - 0.5 * work)
        prim_ref[3, rows, :] = pressure * inverse

    def send(xi_value, eta_value, field):
        send_sums(
            lambda position, group: eta_value[grid.eta_tile(position, group), :],
            grid.xi_groups, grid.ny, odd("eta"), eta_first, eta_second, field,
        )
        send_sums(
            lambda position, group: xi_value[grid.xi_tile(position, group), :],
            grid.eta_groups, grid.nx, odd("xi"), xi_first, xi_second, field,
        )

    for field in range(4):
        send(prim_ref.at[field], prim_ref.at[field], field)
    weights.wait()
    sums = split_weights(sums_ref[...])
    for field in range(4):
        zeta_ref[field] = pack_sums(prim_ref[field], sums, grid)
    for copy in late[1:]:
        copy.wait()
    for k in range(3):
        for index in range(chunks):
            rows = pl.ds(index * step, step)
            mass_ref[k, rows, :] = (
                metrics_ref[3 * k, rows, :] * u_ref[1, rows, :]
                + metrics_ref[3 * k + 1, rows, :] * u_ref[2, rows, :]
                + metrics_ref[3 * k + 2, rows, :] * u_ref[3, rows, :]
            )
    send(mass_ref.at[0], mass_ref.at[1], 4)
    zeta_ref[4] = pack_sums(mass_ref[2], sums, grid)


def fetch_kernel(count, *refs):
    sources, results, sems = refs[:count], refs[count + 1 : 2 * count + 1], refs[-1]
    copies = [
        pltpu.make_async_copy(source, result, sems.at[index])
        for index, (source, result) in enumerate(zip(sources, results))
    ]
    for copy in copies:
        copy.start()
    for copy in copies:
        copy.wait()


def derive_sources(grid, xi_value, eta_value, zeta_value, derive, field, xi_ref, eta_ref, zeta_ref):
    zeta_ref[field] = lane_product(zeta_value[...], derive)
    for group in range(grid.eta_groups):
        cells = [xi_value[grid.xi_tile(i, group), :] for i in range(grid.nx)]
        for i, value in enumerate(derive_source(cells)):
            xi_ref[field, grid.xi_tile(i, group), :] = value
    for group in range(grid.xi_groups):
        cells = [eta_value[grid.eta_tile(i, group), :] for i in range(grid.ny)]
        for i, value in enumerate(derive_source(cells)):
            eta_ref[field, grid.eta_major(i, group), :] = value


def primitive_source_kernel(grid, prim_ref, mass_ref, tables_ref, *results):
    derive = split_weights(tables_ref[DERIVE])
    for field in range(4):
        derive_sources(grid, *[prim_ref.at[field]] * 3, derive, field, *results)
    derive_sources(grid, *[mass_ref.at[k] for k in range(3)], derive, 4, *results)


def contra_source_kernel(grid, contra_ref, tables_ref, *results):
    derive = split_weights(tables_ref[DERIVE])
    for field in range(4):
        derive_sources(grid, *[contra_ref.at[k, field] for k in range(3)], derive, field, *results)


def xi_derivative(grid, source_ref, xi_a, xi_b, field, group):
    below, above = take_sums(xi_a, xi_b, odd("xi"), field, group)
    rights = [source_ref[field, grid.xi_tile(i, group), :] for i in range(grid.nx)]
    return derive_solve(rights, below, above)


def eta_derivative(grid, source_ref, eta_a, eta_b, field, group):
    below, above = take_sums(eta_a, eta_b, odd("eta"), field, group)
    rights = [source_ref[field, grid.eta_major(i, group), :] for i in range(grid.ny)]
    return derive_solve(rights, below, above)


def eta_slope_kernel(grid, source_ref, own_ref, eta_a, eta_b, slope_ref, mass_total_ref):
    for field in range(5):
        for group in range(grid.xi_groups):
            for i, value in enumerate(eta_derivative(grid, source_ref, eta_a, eta_b, field, group)):
                rows = grid.eta_tile(i, group)
                if field < 4:
                    slope_ref[field, rows, :] = value
                else:
                    mass_total_ref[rows, :] = own_ref[4, rows, :] + value


def zeta_slope_kernel(grid, own_ref, part_ref, below_ref, above_ref, tables_ref, slope_ref, mass_total_ref):
    back = split_weights(tables_ref[BACK])
    for field in range(5):
        beyond = lane_product(unpack_sums(below_ref[field], above_ref[field], grid), back)
        if field < 4:
            slope_ref[field] = own_ref[field] + beyond
        else:
            mass_total_ref[...] = part_ref[...] + beyond


def xi_slope_kernel(grid, source_ref, part_ref, xi_b, xi_a, slope_ref, mass_total_ref):
    for field in range(5):
        for group in range(grid.eta_groups):
            for i, value in enumerate(xi_derivative(grid, source_ref, xi_a, xi_b, field, group)):
                rows = grid.xi_tile(i, group)
                if field < 4:
                    slope_ref[field, rows, :] = value
                else:
                    mass_total_ref[rows, :] = part_ref[rows, :] + value


def flux_kernel(
    grid,
    u_ref, prim_ref, metrics_ref, jacobian_ref, xi_slope_ref, eta_slope_ref, zeta_slope_ref, mass_total_ref,
    contra_ref, mass_ref, eta_first, eta_second,
):
    mass_ref[...] = u_ref[0] - (step_duration * jacobian_ref[...]) * mass_total_ref[...]
    send_cells(
        lambda position, group: mass_ref[grid.eta_tile(position, group), :],
        grid.xi_groups, grid.ny, odd("eta"), eta_first, eta_second, 2 * 4,
    )

    step = TILE

    def body(index, carry):
        rows = pl.ds(pl.multiple_of(index * step, step), step)
        u = [u_ref[c, rows, :] for c in range(5)]
        speed = [prim_ref[c, rows, :] for c in range(3)]
        pressure = prim_ref[3, rows, :] * u[0]
        metrics = [[metrics_ref[3 * k + j, rows, :] for j in range(3)] for k in range(3)]
        scaled = (viscosity * jacobian_ref[rows, :])
        scaled = [[scaled * metrics[k][j] for j in range(3)] for k in range(3)]
        physical = []
        for c in range(4):
            slopes = [ref[c, rows, :] for ref in (xi_slope_ref, eta_slope_ref, zeta_slope_ref)]
            physical.append(
                [
                    scaled[0][j] * slopes[0] + scaled[1][j] * slopes[1] + scaled[2][j] * slopes[2]
                    for j in range(3)
                ]
            )
        spread = (2.0 / 3.0) * (physical[0][0] + physical[1][1] + physical[2][2])
        stress = [[None] * 3 for _ in range(3)]
        momentum = [[None] * 3 for _ in range(3)]
        for c in range(3):
            stress[c][c] = (physical[c][c] + physical[c][c]) - spread
            momentum[c][c] = (u[1 + c] * speed[c] + pressure) - stress[c][c]
            for j in range(c):
                stress[c][j] = stress[j][c] = physical[c][j] + physical[j][c]
                momentum[c][j] = momentum[j][c] = u[1 + c] * speed[j] - stress[c][j]
        total = u[4] + pressure
        fluxes = []
        for j in range(3):
            worked = speed[0] * stress[0][j] + speed[1] * stress[1][j] + speed[2] * stress[2][j]
            energy = (total * speed[j] - worked) - (conduction / viscosity) * physical[3][j]
            fluxes.append([momentum[0][j], momentum[1][j], momentum[2][j], energy])
        for k in range(3):
            for f in range(4):
                contra_ref[k, f, rows, :] = (
                    metrics[k][0] * fluxes[0][f]
                    + metrics[k][1] * fluxes[1][f]
                    + metrics[k][2] * fluxes[2][f]
                )
        return carry

    lax.fori_loop(0, grid.rows // step, body, 0, unroll=4)
    for field in range(4):
        send_sums(
            lambda position, group: contra_ref[1, field, grid.eta_tile(position, group), :],
            grid.xi_groups, grid.ny, odd("eta"), eta_first, eta_second, field,
        )


def contra_sums_kernel(grid, contra_ref, sums_ref, xi_first, xi_second, zeta_ref):
    sums = split_weights(sums_ref[...])
    for field in range(4):
        send_sums(
            lambda position, group: contra_ref[0, field, grid.xi_tile(position, group), :],
            grid.eta_groups, grid.nx, odd("xi"), xi_first, xi_second, field,
        )
        zeta_ref[field] = pack_sums(contra_ref[2, field], sums, grid)


def xi_divergence_kernel(grid, source_ref, own_ref, xi_b, xi_a, total_ref):
    for field in range(4):
        for group in range(grid.eta_groups):
            for i, value in enumerate(xi_derivative(grid, source_ref, xi_a, xi_b, field, group)):
                rows = grid.xi_tile(i, group)
                total_ref[field, rows, :] = own_ref[field, rows, :] + value


def zeta_divergence_kernel(grid, part_ref, below_ref, above_ref, tables_ref, total_ref):
    back = split_weights(tables_ref[BACK])
    for field in range(4):
        beyond = lane_product(unpack_sums(below_ref[field], above_ref[field], grid), back)
        total_ref[field] = part_ref[field] + beyond


def step_kernel(
    grid, u_ref, jacobian_ref, source_ref, total_ref, eta_a, eta_b, state_ref, eta_first, eta_second
):
    scale = step_duration * jacobian_ref[...]
    for field in range(4):
        for group in range(grid.xi_groups):
            for i, value in enumerate(eta_derivative(grid, source_ref, eta_a, eta_b, field, group)):
                state_ref[field, grid.eta_tile(i, group), :] = value
        total = total_ref[field] + state_ref[field]
        state_ref[field] = u_ref[1 + field] - scale * total
        send_cells(
            lambda position, group: state_ref[field, grid.eta_tile(position, group), :],
            grid.xi_groups, grid.ny, odd("eta"), eta_first, eta_second, WIDTH * field,
        )


def send_cells(read, groups, count, flag, first_ref, second_ref, base):
    for group in range(groups):
        for step in range(WIDTH):
            low = read(step, group)
            top = read(count - 1 - step, group)
            first_ref[base + step, group_rows(group), :] = jnp.where(flag, low, top)
            second_ref[base + step, group_rows(group), :] = jnp.where(flag, top, low)


def take_cells(first_ref, second_ref, flag, base, group):
    below, above = [], []
    for step in range(WIDTH):
        first = first_ref[base + step, group_rows(group), :]
        second = second_ref[base + step, group_rows(group), :]
        below.append(jnp.where(flag, first, second))
        above.append(jnp.where(flag, second, first))
    return below, above


def send_faces(grid, read, flag, first_ref, second_ref, base):
    for group in range(grid.eta_groups):
        for step in range(WIDTH):
            low = read(step, group)
            top = read(grid.nx - WIDTH + step, group)
            first_ref[base + step, group_rows(group), :] = jnp.where(flag, low, top)
            second_ref[base + step, group_rows(group), :] = jnp.where(flag, top, low)


def take_faces(first_ref, second_ref, flag, base, group):
    below, above = [], []
    for step in range(WIDTH):
        low, top = base + step, base + WIDTH - 1 - step
        rows = group_rows(group)
        below.append(jnp.where(flag, first_ref[top, rows, :], second_ref[top, rows, :]))
        above.append(jnp.where(flag, second_ref[low, rows, :], first_ref[low, rows, :]))
    return below, above


def eta_sources(grid, state_ref, source_ref):
    for group in range(grid.xi_groups):
        cells = [state_ref[grid.eta_tile(i, group), :] for i in range(grid.ny)]
        for i, value in enumerate(smooth_source(cells)):
            source_ref[grid.eta_major(i, group), :] = value


def xi_sources(grid, state_ref, source_ref):
    for group in range(grid.eta_groups):
        cells = [state_ref[grid.xi_tile(i, group), :] for i in range(grid.nx)]
        for i, value in enumerate(smooth_source(cells)):
            source_ref[grid.xi_tile(i, group), :] = value


def eta_filter(grid, source_ref, eta_a, eta_b, base, result_ref):
    for group in range(grid.xi_groups):
        below, above = take_cells(eta_a, eta_b, odd("eta"), base, group)
        rights = [source_ref[grid.eta_major(i, group), :] for i in range(grid.ny)]
        for i, value in enumerate(smooth_solve(rights, below, above)):
            result_ref[grid.eta_tile(i, group), :] = value


def xi_filter(grid, source_ref, xi_a, xi_b, base, smooth, result_ref):
    for group in range(grid.eta_groups):
        below, above = take_faces(xi_a, xi_b, odd("xi"), base, group)
        rights = [source_ref[grid.xi_tile(i, group), :] for i in range(grid.nx)]
        for i, value in enumerate(smooth_solve(rights, below, above)):
            result_ref[grid.xi_tile(i, group), :] = value
    result_ref[...] = lane_product(result_ref[...], smooth)


def source_kernel(grid, form, state_ref, source_ref):
    for field in range(state_ref.shape[0]):
        form(grid, state_ref.at[field], source_ref.at[field])


def face_kernel(
    grid, state_ref, source_ref, eta_a, eta_b, result_ref, next_ref, xi_first, xi_second
):
    flag = odd("xi")
    eta_filter(grid, source_ref.at[0], eta_a, eta_b, 2 * 4, result_ref.at[0])
    for field in range(5):
        values = state_ref.at[field] if field < 4 else result_ref.at[0]
        send_faces(
            grid, lambda position, group: values[grid.xi_tile(position, group), :],
            flag, xi_first, xi_second, WIDTH * field,
        )
    xi_sources(grid, result_ref.at[0], next_ref.at[0])


PLANES = 3 * TILE


def halo_source_kernel(grid, first_ref, second_ref, first_source, second_source):
    for faces, source in ((first_ref, first_source), (second_ref, second_source)):
        for tile in range(PLANES // TILE):
            cells = [
                faces[pl.ds(tile * TILE * grid.ny + i, TILE, stride=grid.ny), :] for i in range(grid.ny)
            ]
            for i, value in enumerate(smooth_source(cells)):
                source[pl.ds(i * PLANES + tile * TILE, TILE), :] = value


def edge_kernel(grid, order_ref, eta_b, eta_a, first_ref, second_ref):
    flag = odd("xi")
    eta_flag = odd("eta")
    for side in range(2):
        for step in range(WIDTH):
            start = (side * WIDTH + step) * PLANES
            for field in range(4):
                one, other = eta_a[WIDTH * field + step], eta_b[WIDTH * field + step]
                cells = jnp.where(eta_flag, other, one) if side else jnp.where(eta_flag, one, other)
                low, top = cells[:WIDTH], cells[grid.nx - WIDTH :]
                rows = pl.ds(start + WIDTH * field, WIDTH)
                first_ref[rows, :] = jnp.where(flag, low, top)
                second_ref[rows, :] = jnp.where(flag, top, low)
            rest = pl.ds(start + 4 * WIDTH, PLANES - 4 * WIDTH)
            first_ref[rest, :] = jnp.zeros((PLANES - 4 * WIDTH, LANES), jnp.float32)
            second_ref[rest, :] = jnp.zeros((PLANES - 4 * WIDTH, LANES), jnp.float32)


def filter_halo(grid, source_ref, edge_ref, result_ref):
    for tile in range(PLANES // TILE):
        ends = [
            [edge_ref[pl.ds((side * WIDTH + i) * PLANES + tile * TILE, TILE), :] for i in range(WIDTH)]
            for side in range(2)
        ]
        rights = [source_ref[pl.ds(i * PLANES + tile * TILE, TILE), :] for i in range(grid.ny)]
        for i, value in enumerate(smooth_solve(rights, *ends)):
            result_ref[pl.ds(tile * TILE * grid.ny + i, TILE, stride=grid.ny), :] = value


def eta_filter_kernel(
    grid, source_ref, mass_ref, eta_a, eta_b,
    result_ref, zeta_ref, edge_first, edge_second,
):
    flag = odd("xi")
    for field in range(4):
        eta_filter(grid, source_ref.at[field], eta_a, eta_b, WIDTH * field, result_ref.at[field])
    lane = lax.broadcasted_iota(jnp.int32, (TILE, LANES), 1)
    for position in range(grid.nx):
        packed = None
        for slot in range(5 * grid.eta_groups):
            field, group = slot // grid.eta_groups, slot % grid.eta_groups
            rows = grid.xi_tile(position, group)
            part = result_ref[field - 1, rows, :] if field else mass_ref[0, rows, :]
            part = pltpu.roll(part, WIDTH * (2 * slot + 1), axis=1)
            packed = part if packed is None else jnp.where(lane >= 2 * WIDTH * slot, part, packed)
        zeta_ref[group_rows(position), :] = packed
    send_cells(
        lambda position, group: zeta_ref[group_rows(position), :],
        1, grid.nx, flag, edge_first, edge_second, 0,
    )


def mass_xi_kernel(grid, source_ref, xi_a, xi_b, tables_ref, result_ref):
    smooth = split_weights(tables_ref[SMOOTH])
    xi_filter(grid, source_ref.at[0], xi_a, xi_b, WIDTH * 4, smooth, result_ref.at[0])


def xi_filter_kernel(
    grid, source_ref, first_source, second_source, edge_b, edge_a, tables_ref, result_ref,
    first_ref, second_ref,
):
    smooth = split_weights(tables_ref[SMOOTH])
    filter_halo(grid, first_source, edge_a, first_ref)
    filter_halo(grid, second_source, edge_b, second_ref)

    class Layers:
        def __init__(self, ref):
            self.ref = ref

        def __getitem__(self, index):
            layer, rows, _ = index
            return self.ref[pl.ds(layer * grid.ny + rows.start, rows.size), :]

    for field in range(4):
        xi_filter(
            grid, source_ref.at[field], Layers(first_ref), Layers(second_ref), WIDTH * field, smooth,
            result_ref.at[field],
        )


def zeta_filter_kernel(
    grid,
    mass_ref, state_ref, b_below, b_above, below_ref, above_ref, a_below, a_above, tables_ref,
    result_hbm,
    result_ref, sems,
):
    ends = split_weights(tables_ref[ENDS])
    flag = odd("xi")
    lane = lax.broadcasted_iota(jnp.int32, (TILE, LANES), 1)
    from_below = lax.rem(lane, 2 * WIDTH) < WIDTH

    def merge(below, above, index):
        return jnp.where(from_below, below[group_rows(index), :], above[group_rows(index), :])

    low, high = [], []
    for step in range(WIDTH):
        first, second = merge(a_below, a_above, step), merge(b_below, b_above, step)
        low.append(jnp.where(flag, first, second))
        high.append(jnp.where(flag, second, first))
    cells = [merge(below_ref, above_ref, position) for position in range(grid.nx)]
    cells = smooth_solve(smooth_source(cells), low, high)
    copies = []
    for field in range(5):
        parts = []
        for packed in cells:
            for group in range(grid.eta_groups):
                slot = field * grid.eta_groups + group
                parts.append(pltpu.roll(packed, LANES - 2 * WIDTH * slot, axis=1) if slot else packed)
        halo = jnp.concatenate(parts, axis=0)
        own = state_ref[field - 1] if field else mass_ref[0]
        result_ref[field] = own + lane_product(halo, ends)
        copy = pltpu.make_async_copy(result_ref.at[field], result_hbm.at[field], sems.at[field])
        copy.start()
        copies.append(copy)
    for copy in copies:
        copy.wait()


def pair_swap(value, axis, parity):
    count = lax.axis_size(axis)
    pairs = []
    for index in range(count):
        step = 1 if index % 2 == parity else -1
        pairs.append((index, (index + step) % count))
    return lax.ppermute(value, axis, pairs)


def diagonal_swap(value, parity):
    nx, nz = lax.axis_size("xi"), lax.axis_size("zeta")

    def send(shift):
        pairs = []
        for i in range(nx):
            partner = (i + (1 if i % 2 == parity else -1)) % nx
            for k in range(nz):
                pairs.append((i * nz + k, partner * nz + (k + shift) % nz))
        return lax.ppermute(value, ("xi", "zeta"), pairs)

    below = send(1)
    return (below, below) if nz == 2 else (below, send(-1))


def ring_swap(value, axis):
    count = lax.axis_size(axis)
    if count == 2:
        other = lax.ppermute(value, axis, [(0, 1), (1, 0)])
        return other, other
    up = [(index, (index + 1) % count) for index in range(count)]
    down = [(index, (index - 1) % count) for index in range(count)]
    return lax.ppermute(value, axis, up), lax.ppermute(value, axis, down)


HBM = pltpu.MemorySpace.HBM


def call(kernel, outs, *operands, scratch=(), cost=1.0, far=(), far_outs=()):
    shapes = [
        out if isinstance(out, jax.ShapeDtypeStruct) else jax.ShapeDtypeStruct(out, jnp.float32)
        for out in outs
    ]
    near = pltpu.MemorySpace.VMEM
    operands = [
        pltpu.with_memory_space_constraint(value, HBM) if index in far else value
        for index, value in enumerate(operands)
    ]
    return pl.pallas_call(
        kernel,
        out_shape=shapes,
        in_specs=[
            pl.BlockSpec(memory_space=HBM if index in far else near) for index in range(len(operands))
        ],
        out_specs=[
            pl.BlockSpec(memory_space=HBM if index in far_outs else near) for index in range(len(outs))
        ],
        scratch_shapes=scratch,
        cost_estimate=pl.CostEstimate(flops=0, transcendentals=0, bytes_accessed=int(cost * 3.6e6)),
        compiler_params=pltpu.CompilerParams(vmem_limit_bytes=20 * 2**20),
    )(*operands)


def like(value):
    return jax.ShapeDtypeStruct(value.shape, value.dtype)


def local(conserved_solution, metrics, jacobian):
    _, nx, ny, nz = conserved_solution.shape
    grid = Grid(nx, ny)
    rows = grid.rows
    u = conserved_solution.reshape(5, rows, nz)
    metrics = metrics.reshape(9, rows, nz)
    jacobian = jacobian.reshape(rows, nz)
    sums, tables = (jnp.asarray(table) for table in zeta_tables(nz))

    def exchange(eta_first, eta_second, xi_first, xi_second, zeta):
        eta_b = pair_swap(eta_second, "eta", 1)
        eta_a = pair_swap(eta_first, "eta", 0)
        xi_b = pair_swap(xi_second, "xi", 1)
        below, above = ring_swap(zeta, "zeta")
        xi_a = pair_swap(xi_first, "xi", 0)
        return (eta_a, eta_b), (xi_b, xi_a), (below, above)

    block = (rows, nz)
    chunks = 2
    u, sums, metrics, prim, mass, *sends = call(
        functools.partial(primitive_kernel, grid),
        [like(u), like(sums), like(metrics), (4, *block), (3, *block)]
        + [(2 * 5, nx, nz)] * 2
        + [(2 * 5, ny, nz)] * 2
        + [(5, TILE, LANES)],
        u, sums, metrics,
        scratch=[pltpu.SemaphoreType.DMA((chunks,)), pltpu.SemaphoreType.DMA((10,))],
        far=(0, 1, 2),
    )
    tables, jacobian = call(
        functools.partial(fetch_kernel, 2),
        [like(tables), like(jacobian)],
        tables, jacobian, sends[-1],
        scratch=[pltpu.SemaphoreType.DMA((2,))],
        far=(0, 1),
    )
    eta_sides, xi_sides, ends = exchange(*sends)
    xi_source, eta_source, own = call(
        functools.partial(primitive_source_kernel, grid), [(5, *block)] * 3, prim, mass, tables,
    )
    eta_slope, mass_total = call(
        functools.partial(eta_slope_kernel, grid), [(4, *block), block], eta_source, own, *eta_sides,
    )
    xi_slope, mass_total = call(
        functools.partial(xi_slope_kernel, grid),
        [(4, *block), block],
        xi_source, mass_total, *xi_sides,
    )
    zeta_slope, mass_total = call(
        functools.partial(zeta_slope_kernel, grid),
        [(4, *block), block],
        own, mass_total, *ends, tables,
    )
    contra, mass, *eta_sends = call(
        functools.partial(flux_kernel, grid),
        [(3, 4, *block), block] + [(2 * 4 + WIDTH, nx, nz)] * 2,
        u, prim, metrics, jacobian, xi_slope, eta_slope, zeta_slope, mass_total,
    )
    sends = call(
        functools.partial(contra_sums_kernel, grid),
        [(2 * 4, ny, nz)] * 2 + [(4, TILE, LANES)],
        contra, sums,
    )
    eta_sides, xi_sides, ends = exchange(*eta_sends, *sends)
    xi_source, eta_source, own = call(
        functools.partial(contra_source_kernel, grid), [(4, *block)] * 3, contra, tables,
    )
    (mass_source,) = call(
        functools.partial(source_kernel, grid, eta_sources), [(1, *block)], mass.reshape(1, *block),
    )
    (total,) = call(
        functools.partial(xi_divergence_kernel, grid), [(4, *block)], xi_source, own, *xi_sides,
    )
    (total,) = call(
        functools.partial(zeta_divergence_kernel, grid), [(4, *block)], total, *ends, tables,
    )
    state, eta_first, eta_second = call(
        functools.partial(step_kernel, grid),
        [(4, *block)] + [(4 * WIDTH, nx, nz)] * 2,
        u, jacobian, eta_source, total, *eta_sides,
    )
    eta_b = pair_swap(eta_second, "eta", 1)
    eta_a = pair_swap(eta_first, "eta", 0)
    mass, mass_source, xi_first, xi_second = call(
        functools.partial(face_kernel, grid),
        [(1, *block)] * 2 + [(5 * WIDTH, ny, nz)] * 2,
        state, mass_source, *eta_sides,
    )
    xi_b = pair_swap(xi_second, "xi", 1)
    xi_a = pair_swap(xi_first, "xi", 0)
    (source,) = call(functools.partial(source_kernel, grid, eta_sources), [(4, *block)], state)
    (mass_part,) = call(
        functools.partial(mass_xi_kernel, grid), [(1, *block)], mass_source, xi_a, xi_b, tables,
    )
    layers = 5 * WIDTH * ny
    halo_first, halo_second = call(
        functools.partial(halo_source_kernel, grid),
        [(ny * PLANES, nz)] * 2,
        xi_a.reshape(layers, nz), xi_b.reshape(layers, nz),
    )
    edge_first, edge_second = call(
        functools.partial(edge_kernel, grid), [(2 * WIDTH * PLANES, nz)] * 2, source, eta_b, eta_a,
    )
    edge_b = pair_swap(edge_second, "xi", 1)
    edge_a = pair_swap(edge_first, "xi", 0)
    state, zeta, corner_first, corner_second = call(
        functools.partial(eta_filter_kernel, grid),
        [(4, *block), (nx * TILE, LANES)] + [(WIDTH, TILE, LANES)] * 2,
        source, mass, eta_a, eta_b,
    )
    ends = ring_swap(zeta, "zeta")
    edges_b = diagonal_swap(corner_second, 1)
    edges_a = diagonal_swap(corner_first, 0)
    (source,) = call(functools.partial(source_kernel, grid, xi_sources), [(4, *block)], state)
    (state,) = call(
        functools.partial(xi_filter_kernel, grid),
        [(4, *block)],
        source, halo_first, halo_second, edge_b, edge_a, tables,
        scratch=[pltpu.VMEM((PLANES * ny, nz), jnp.float32)] * 2,
    )
    edges = [edge.reshape(WIDTH * TILE, LANES) for edge in (*edges_a, *edges_b)]
    (result,) = call(
        functools.partial(zeta_filter_kernel, grid),
        [(5, *block)],
        mass_part, state, *edges[2:], *ends, *edges[:2], tables,
        scratch=[pltpu.VMEM((5, *block), jnp.float32), pltpu.SemaphoreType.DMA((5,))],
        far_outs=(0,),
    )
    return result.reshape(5, nx, ny, nz)


def solution(mesh):
    in_specs = (
        P(None, "xi", "eta", "zeta"),
        P(None, None, "xi", "eta", "zeta"),
        P("xi", "eta", "zeta"),
    )
    out_specs = P(None, "xi", "eta", "zeta")
    return jax.shard_map(local, mesh=mesh, in_specs=in_specs, out_specs=out_specs, check_vma=False)
```

```python
import functools

import jax
import jax.numpy as jnp
import numpy as np
from jax import lax
from jax.experimental import pallas as pl
from jax.experimental.pallas import tpu as pltpu
from jax.sharding import PartitionSpec as P

WIDTH = 5
LANES = 128
TILE = 8

viscosity = 0.15
conduction = 0.15 * 1.4 / (0.4 * 0.72)
step_duration = 0.08


def derivative_system(length):
    extent = length + 2 * WIDTH
    system = np.eye(extent)
    source = np.zeros((extent, extent))
    for position in range(2, extent - 2):
        system[position, position - 1] = 1.0 / 3.0
        system[position, position + 1] = 1.0 / 3.0
        source[position, position + 1] = 7.0 / 9.0
        source[position, position - 1] = -7.0 / 9.0
        source[position, position + 2] = 1.0 / 36.0
        source[position, position - 2] = -1.0 / 36.0
    source[1, 2] = 0.5
    source[1, 0] = -0.5
    source[extent - 2, extent - 1] = 0.5
    source[extent - 2, extent - 3] = -0.5
    source[0, 1] = 1.0
    source[0, 0] = -1.0
    source[extent - 1, extent - 1] = 1.0
    source[extent - 1, extent - 2] = -1.0
    return system, source


def filter_coefficients():
    strength = 0.4
    return [
        (193.0 + 126.0 * strength) / 256.0,
        (105.0 + 302.0 * strength) / 256.0,
        15.0 * (2.0 * strength - 1.0) / 64.0,
        45.0 * (1.0 - 2.0 * strength) / 512.0,
        5.0 * (2.0 * strength - 1.0) / 256.0,
        (1.0 - 2.0 * strength) / 512.0,
    ]


def filter_system(length):
    strength = 0.4
    coeffs = filter_coefficients()
    extent = length + 2 * WIDTH
    system = np.eye(extent)
    source = np.eye(extent)
    for position in range(5, extent - 5):
        system[position, position - 1] = strength
        system[position, position + 1] = strength
        source[position, position] = coeffs[0]
        for offset in range(1, 6):
            source[position, position + offset] = coeffs[offset] / 2.0
            source[position, position - offset] = coeffs[offset] / 2.0
    return system, source


def own_rows(system, source, length):
    return np.linalg.solve(system, source)[WIDTH : WIDTH + length]


def derivative_parts(length):
    system, source = derivative_system(length)
    halo = np.linalg.solve(system[:WIDTH, :WIDTH], source[:WIDTH])
    row = source[WIDTH] - system[WIDTH, WIDTH - 1] * halo[WIDTH - 1]
    pivots = [1.0]
    for position in range(3, WIDTH + length):
        pivots.append(1.0 - 1.0 / 9.0 / pivots[-1])
    return pivots[WIDTH - 2 :], row[:WIDTH], row[WIDTH : WIDTH + 3]


def pad_rows(table):
    return np.concatenate([table, np.zeros((LANES - table.shape[0], table.shape[1]))], axis=0)


def pad_columns(table):
    return np.concatenate([table, np.zeros((table.shape[0], LANES - table.shape[1]))], axis=1)


def zeta_tables(length):
    system, source = derivative_system(length)
    table = own_rows(system, source, length)
    _, edge, _ = derivative_parts(length)
    inverse = np.linalg.inv(system)
    extent = length + 2 * WIDTH
    sums = np.zeros((length, 4))
    sums[length - WIDTH :, 0] = edge
    sums[length - 1, 1] = 1.0
    sums[:WIDTH, 2] = -edge[::-1]
    sums[0, 3] = 1.0
    own = slice(WIDTH, WIDTH + length)
    back = np.stack(
        [
            inverse[own, WIDTH],
            -1.0 / 36.0 * inverse[own, WIDTH + 1],
            inverse[own, extent - WIDTH - 1],
            1.0 / 36.0 * inverse[own, extent - WIDTH - 2],
        ]
    )
    smooth = own_rows(*filter_system(length), length)
    ends = np.concatenate([smooth[:, :WIDTH], smooth[:, WIDTH + length :]], axis=1)
    tables = [table[:, own].T, pad_columns(sums), pad_rows(back), smooth[:, own].T, pad_rows(ends.T)]
    return tables.pop(1).astype(np.float32), np.stack(tables).astype(np.float32)


DERIVE, BACK, SMOOTH, ENDS = range(4)


def twisted_solve(rights, pivots, off):
    count = len(rights)
    half = count // 2
    low = [rights[0]]
    high = [rights[count - 1]]
    for step in range(1, half):
        factor = off / pivots[step - 1]
        low.append(rights[step] - factor * low[-1])
        high.append(rights[count - 1 - step] - factor * high[-1])
    middle = pivots[half - 1]
    det = middle * middle - off * off
    first, second = low[-1], high[-1]
    answer = [None] * count
    answer[half - 1] = (middle / det) * first - (off / det) * second
    answer[half] = (middle / det) * second - (off / det) * first
    for step in range(half - 2, -1, -1):
        scale = 1.0 / pivots[step]
        factor = off / pivots[step]
        answer[step] = scale * low[step] - factor * answer[step + 1]
        answer[count - 1 - step] = scale * high[step] - factor * answer[count - 2 - step]
    return answer


def derive_source(cells):
    count = len(cells)
    _, _, edge = derivative_parts(count)
    near, far = 7.0 / 9.0, 1.0 / 36.0
    rights = [None] * count
    rights[0] = edge[0] * cells[0] + edge[1] * cells[1] + edge[2] * cells[2]
    rights[1] = near * (cells[2] - cells[0]) + far * cells[3]
    for step in range(2, count - 2):
        rights[step] = near * (cells[step + 1] - cells[step - 1]) + far * (
            cells[step + 2] - cells[step - 2]
        )
    rights[count - 2] = near * (cells[count - 1] - cells[count - 3]) - far * cells[count - 4]
    rights[count - 1] = -(
        edge[0] * cells[count - 1] + edge[1] * cells[count - 2] + edge[2] * cells[count - 3]
    )
    return rights


def derive_solve(rights, below, above):
    pivots, _, _ = derivative_parts(len(rights))
    rights = list(rights)
    far = 1.0 / 36.0
    rights[0] = rights[0] + below[0]
    rights[1] = rights[1] - far * below[1]
    rights[-2] = rights[-2] + far * above[1]
    rights[-1] = rights[-1] + above[0]
    return twisted_solve(rights, pivots, 1.0 / 3.0)


def end_sums(cells):
    _, edge, _ = derivative_parts(16)
    total = edge[WIDTH - 1] * cells[0]
    for step in range(1, WIDTH):
        total = total + edge[WIDTH - 1 - step] * cells[step]
    return total, cells[0]


def smooth_source(cells):
    count = len(cells)
    coeffs = filter_coefficients()
    rights = []
    for step in range(count):
        total = coeffs[0] * cells[step]
        for offset in range(1, WIDTH + 1):
            around = [cells[i] for i in (step - offset, step + offset) if 0 <= i < count]
            around = around[0] + around[1] if len(around) == 2 else around[0]
            total = total + (0.5 * coeffs[offset]) * around
        rights.append(total)
    return rights


def smooth_solve(rights, below, above):
    count = len(rights)
    coeffs = filter_coefficients()
    rights = list(rights)
    for step in range(WIDTH):
        for cell in range(WIDTH - step):
            factor = 0.5 * coeffs[step + cell + 1]
            if step == 0 and cell == 0:
                factor = factor - 0.4
            rights[step] = rights[step] + factor * below[cell]
            rights[count - 1 - step] = rights[count - 1 - step] + factor * above[cell]
    pivots = [1.0]
    for _ in range(count):
        pivots.append(1.0 - 0.16 / pivots[-1])
    return twisted_solve(rights, pivots, 0.4)


def split_values(values):
    high = values.astype(jnp.bfloat16)
    low = (values - high.astype(jnp.float32)).astype(jnp.bfloat16)
    return jnp.concatenate([high, low], axis=1)


def split_weights(table):
    high = table.astype(jnp.bfloat16)
    low = (table - high.astype(jnp.float32)).astype(jnp.bfloat16)
    top = jnp.concatenate([high, low], axis=1)
    return jnp.concatenate([top, jnp.concatenate([high, jnp.zeros_like(low)], axis=1)], axis=0)


def lane_product(values, weights):
    both = jnp.dot(split_values(values), weights, preferred_element_type=jnp.float32)
    return both[:, :LANES] + both[:, LANES:]


class Grid:
    def __init__(self, nx, ny):
        self.nx, self.ny, self.rows = nx, ny, nx * ny
        self.eta_groups = ny // TILE
        self.xi_groups = nx // TILE

    def xi_tile(self, position, group):
        return pl.ds(position * self.ny + group * TILE, TILE)

    def eta_tile(self, position, group):
        return pl.ds(position + group * TILE * self.ny, TILE, stride=self.ny)

    def eta_major(self, position, group):
        return pl.ds(position * self.nx + group * TILE, TILE)


def group_rows(group):
    return pl.ds(group * TILE, TILE)


def odd(axis):
    return lax.rem(lax.axis_index(axis), 2) == 1


def send_sums(read, groups, count, flag, first_ref, second_ref, field):
    for group in range(groups):
        top = end_sums([read(count - 1 - step, group) for step in range(WIDTH)])
        low = end_sums([read(step, group) for step in range(WIDTH)])
        low = (-low[0], low[1])
        for part in range(2):
            first_ref[2 * field + part, group_rows(group), :] = jnp.where(flag, low[part], top[part])
            second_ref[2 * field + part, group_rows(group), :] = jnp.where(flag, top[part], low[part])


def take_sums(first_ref, second_ref, flag, field, group):
    below, above = [], []
    for part in range(2):
        first = first_ref[2 * field + part, group_rows(group), :]
        second = second_ref[2 * field + part, group_rows(group), :]
        below.append(jnp.where(flag, first, second))
        above.append(jnp.where(flag, second, first))
    return below, above


def pack_sums(values, weights, grid):
    sums = lane_product(values, weights)
    parts = []
    for group in range(grid.rows // TILE):
        part = sums[group * TILE : (group + 1) * TILE]
        parts.append(pltpu.roll(part, 4 * group, axis=1) if group else part)
    while len(parts) > 1:
        parts = [sum(parts[i + 1 : i + 2], parts[i]) for i in range(0, len(parts), 2)]
    return parts[0]


def unpack_sums(below, above, grid):
    lane = lax.broadcasted_iota(jnp.int32, below.shape, 1)
    packed = jnp.where(lax.rem(lane, 4) < 2, below, above)
    parts = [packed]
    for group in range(1, grid.rows // TILE):
        parts.append(pltpu.roll(packed, LANES - 4 * group, axis=1))
    return jnp.concatenate(parts, axis=0)


def primitive_kernel(
    grid,
    u_hbm, sums_hbm, metrics_hbm,
    u_ref, sums_ref, metrics_ref,
    prim_ref, mass_ref, eta_first, eta_second, xi_first, xi_second, zeta_ref,
    u_sems, late_sems,
):
    chunks = u_sems.shape[0]
    step = grid.rows // chunks
    weights = pltpu.make_async_copy(sums_hbm, sums_ref, late_sems.at[0])
    weights.start()
    copies = []
    for index in range(chunks):
        rows = pl.ds(index * step, step)
        copy = pltpu.make_async_copy(u_hbm.at[:, rows, :], u_ref.at[:, rows, :], u_sems.at[index])
        copy.start()
        copies.append(copy)
    late = [
        pltpu.make_async_copy(source, result, late_sems.at[index])
        for index, (source, result) in enumerate(
            [(sums_hbm, sums_ref)] + [(metrics_hbm, metrics_ref)]
        )
    ]
    for copy in late[1:]:
        copy.start()
    for index in range(chunks):
        copies[index].wait()
        rows = pl.ds(index * step, step)
        inverse = 1.0 / u_ref[0, rows, :]
        work = None
        for c in range(3):
            momentum = u_ref[1 + c, rows, :]
            speed = momentum * inverse
            prim_ref[c, rows, :] = speed
            work = momentum * speed if work is None else work + momentum * speed
        pressure = 0.4 * (u_ref[4, rows, :] - 0.5 * work)
        prim_ref[3, rows, :] = pressure * inverse

    def send(xi_value, eta_value, field):
        send_sums(
            lambda position, group: eta_value[grid.eta_tile(position, group), :],
            grid.xi_groups, grid.ny, odd("eta"), eta_first, eta_second, field,
        )
        send_sums(
            lambda position, group: xi_value[grid.xi_tile(position, group), :],
            grid.eta_groups, grid.nx, odd("xi"), xi_first, xi_second, field,
        )

    for field in range(4):
        send(prim_ref.at[field], prim_ref.at[field], field)
    weights.wait()
    sums = split_weights(sums_ref[...])
    for field in range(4):
        zeta_ref[field] = pack_sums(prim_ref[field], sums, grid)
    for copy in late[1:]:
        copy.wait()
    for k in range(3):
        for index in range(chunks):
            rows = pl.ds(index * step, step)
            mass_ref[k, rows, :] = (
                metrics_ref[3 * k, rows, :] * u_ref[1, rows, :]
                + metrics_ref[3 * k + 1, rows, :] * u_ref[2, rows, :]
                + metrics_ref[3 * k + 2, rows, :] * u_ref[3, rows, :]
            )
    send(mass_ref.at[0], mass_ref.at[1], 4)
    zeta_ref[4] = pack_sums(mass_ref[2], sums, grid)


def fetch_kernel(count, *refs):
    sources, results, sems = refs[:count], refs[count + 1 : 2 * count + 1], refs[-1]
    copies = [
        pltpu.make_async_copy(source, result, sems.at[index])
        for index, (source, result) in enumerate(zip(sources, results))
    ]
    for copy in copies:
        copy.start()
    for copy in copies:
        copy.wait()


def derive_sources(grid, xi_value, eta_value, zeta_value, derive, field, xi_ref, eta_ref, zeta_ref):
    zeta_ref[field] = lane_product(zeta_value[...], derive)
    for group in range(grid.eta_groups):
        cells = [xi_value[grid.xi_tile(i, group), :] for i in range(grid.nx)]
        for i, value in enumerate(derive_source(cells)):
            xi_ref[field, grid.xi_tile(i, group), :] = value
    for group in range(grid.xi_groups):
        cells = [eta_value[grid.eta_tile(i, group), :] for i in range(grid.ny)]
        for i, value in enumerate(derive_source(cells)):
            eta_ref[field, grid.eta_major(i, group), :] = value


def primitive_source_kernel(grid, prim_ref, mass_ref, tables_ref, *results):
    derive = split_weights(tables_ref[DERIVE])
    for field in range(4):
        derive_sources(grid, *[prim_ref.at[field]] * 3, derive, field, *results)
    derive_sources(grid, *[mass_ref.at[k] for k in range(3)], derive, 4, *results)


def contra_source_kernel(grid, contra_ref, tables_ref, *results):
    derive = split_weights(tables_ref[DERIVE])
    for field in range(4):
        derive_sources(grid, *[contra_ref.at[k, field] for k in range(3)], derive, field, *results)


def xi_derivative(grid, source_ref, xi_a, xi_b, field, group):
    below, above = take_sums(xi_a, xi_b, odd("xi"), field, group)
    rights = [source_ref[field, grid.xi_tile(i, group), :] for i in range(grid.nx)]
    return derive_solve(rights, below, above)


def eta_derivative(grid, source_ref, eta_a, eta_b, field, group):
    below, above = take_sums(eta_a, eta_b, odd("eta"), field, group)
    rights = [source_ref[field, grid.eta_major(i, group), :] for i in range(grid.ny)]
    return derive_solve(rights, below, above)


def add_derivatives(grid, xi_source, eta_source, own_ref, eta_a, eta_b, xi_a, xi_b, field, total_ref):
    for group in range(grid.xi_groups):
        for i, value in enumerate(eta_derivative(grid, eta_source, eta_a, eta_b, field, group)):
            rows = grid.eta_tile(i, group)
            total_ref[rows, :] = own_ref[field, rows, :] + value
    for group in range(grid.eta_groups):
        for i, value in enumerate(xi_derivative(grid, xi_source, xi_a, xi_b, field, group)):
            rows = grid.xi_tile(i, group)
            total_ref[rows, :] = total_ref[rows, :] + value


def slope_kernel(grid, xi_source, eta_source, own_ref, eta_a, eta_b, xi_b, xi_a, slope_ref, mass_total_ref):
    for field in range(4):
        for group in range(grid.eta_groups):
            for i, value in enumerate(xi_derivative(grid, xi_source, xi_a, xi_b, field, group)):
                slope_ref[0, field, grid.xi_tile(i, group), :] = value
        for group in range(grid.xi_groups):
            for i, value in enumerate(eta_derivative(grid, eta_source, eta_a, eta_b, field, group)):
                slope_ref[1, field, grid.eta_tile(i, group), :] = value
    add_derivatives(
        grid, xi_source, eta_source, own_ref, eta_a, eta_b, xi_a, xi_b, 4, mass_total_ref
    )


def flux_kernel(
    grid,
    u_ref, prim_ref, metrics_ref, jacobian_ref, slope_ref, own_ref, mass_total_ref,
    zeta_below, zeta_above, tables_ref,
    contra_ref, mass_ref, eta_first, eta_second,
    zeta_slope_ref,
):
    back = split_weights(tables_ref[BACK])
    for field in range(4):
        halo = unpack_sums(zeta_below[field], zeta_above[field], grid)
        zeta_slope_ref[field] = own_ref[field] + lane_product(halo, back)
    halo = unpack_sums(zeta_below[4], zeta_above[4], grid)
    total = mass_total_ref[...] + lane_product(halo, back)
    mass_ref[...] = u_ref[0] - (step_duration * jacobian_ref[...]) * total
    send_cells(
        lambda position, group: mass_ref[grid.eta_tile(position, group), :],
        grid.xi_groups, grid.ny, odd("eta"), eta_first, eta_second, 2 * 4,
    )

    step = TILE

    def body(index, carry):
        rows = pl.ds(pl.multiple_of(index * step, step), step)
        u = [u_ref[c, rows, :] for c in range(5)]
        speed = [prim_ref[c, rows, :] for c in range(3)]
        pressure = prim_ref[3, rows, :] * u[0]
        metrics = [[metrics_ref[3 * k + j, rows, :] for j in range(3)] for k in range(3)]
        scaled = (viscosity * jacobian_ref[rows, :])
        scaled = [[scaled * metrics[k][j] for j in range(3)] for k in range(3)]
        physical = []
        for c in range(4):
            slopes = [slope_ref[0, c, rows, :], slope_ref[1, c, rows, :], zeta_slope_ref[c, rows, :]]
            physical.append(
                [
                    scaled[0][j] * slopes[0] + scaled[1][j] * slopes[1] + scaled[2][j] * slopes[2]
                    for j in range(3)
                ]
            )
        spread = (2.0 / 3.0) * (physical[0][0] + physical[1][1] + physical[2][2])
        stress = [[None] * 3 for _ in range(3)]
        momentum = [[None] * 3 for _ in range(3)]
        for c in range(3):
            stress[c][c] = (physical[c][c] + physical[c][c]) - spread
            momentum[c][c] = (u[1 + c] * speed[c] + pressure) - stress[c][c]
            for j in range(c):
                stress[c][j] = stress[j][c] = physical[c][j] + physical[j][c]
                momentum[c][j] = momentum[j][c] = u[1 + c] * speed[j] - stress[c][j]
        total = u[4] + pressure
        fluxes = []
        for j in range(3):
            worked = speed[0] * stress[0][j] + speed[1] * stress[1][j] + speed[2] * stress[2][j]
            energy = (total * speed[j] - worked) - (conduction / viscosity) * physical[3][j]
            fluxes.append([momentum[0][j], momentum[1][j], momentum[2][j], energy])
        for k in range(3):
            for f in range(4):
                contra_ref[k, f, rows, :] = (
                    metrics[k][0] * fluxes[0][f]
                    + metrics[k][1] * fluxes[1][f]
                    + metrics[k][2] * fluxes[2][f]
                )
        return carry

    lax.fori_loop(0, grid.rows // step, body, 0, unroll=4)
    for field in range(4):
        send_sums(
            lambda position, group: contra_ref[1, field, grid.eta_tile(position, group), :],
            grid.xi_groups, grid.ny, odd("eta"), eta_first, eta_second, field,
        )


def contra_sums_kernel(grid, contra_ref, sums_ref, xi_first, xi_second, zeta_ref):
    sums = split_weights(sums_ref[...])
    for field in range(4):
        send_sums(
            lambda position, group: contra_ref[0, field, grid.xi_tile(position, group), :],
            grid.eta_groups, grid.nx, odd("xi"), xi_first, xi_second, field,
        )
        zeta_ref[field] = pack_sums(contra_ref[2, field], sums, grid)


def divergence_kernel(grid, xi_source, eta_source, own_ref, eta_a, eta_b, xi_b, xi_a, total_ref):
    for field in range(4):
        add_derivatives(
            grid, xi_source, eta_source, own_ref, eta_a, eta_b, xi_a, xi_b, field, total_ref.at[field]
        )


def step_kernel(
    grid,
    u_ref, jacobian_ref, total_ref, zeta_below, zeta_above, tables_ref,
    state_ref, eta_first, eta_second,
):
    back = split_weights(tables_ref[BACK])
    scale = step_duration * jacobian_ref[...]
    for field in range(4):
        halo = unpack_sums(zeta_below[field], zeta_above[field], grid)
        total = total_ref[field] + lane_product(halo, back)
        state_ref[field] = u_ref[1 + field] - scale * total
        send_cells(
            lambda position, group: state_ref[field, grid.eta_tile(position, group), :],
            grid.xi_groups, grid.ny, odd("eta"), eta_first, eta_second, WIDTH * field,
        )


def send_cells(read, groups, count, flag, first_ref, second_ref, base):
    for group in range(groups):
        for step in range(WIDTH):
            low = read(step, group)
            top = read(count - 1 - step, group)
            first_ref[base + step, group_rows(group), :] = jnp.where(flag, low, top)
            second_ref[base + step, group_rows(group), :] = jnp.where(flag, top, low)


def take_cells(first_ref, second_ref, flag, base, group):
    below, above = [], []
    for step in range(WIDTH):
        first = first_ref[base + step, group_rows(group), :]
        second = second_ref[base + step, group_rows(group), :]
        below.append(jnp.where(flag, first, second))
        above.append(jnp.where(flag, second, first))
    return below, above


def send_faces(grid, read, flag, first_ref, second_ref, base):
    for group in range(grid.eta_groups):
        for step in range(WIDTH):
            low = read(step, group)
            top = read(grid.nx - WIDTH + step, group)
            first_ref[base + step, group_rows(group), :] = jnp.where(flag, low, top)
            second_ref[base + step, group_rows(group), :] = jnp.where(flag, top, low)


def take_faces(first_ref, second_ref, flag, base, group):
    below, above = [], []
    for step in range(WIDTH):
        low, top = base + step, base + WIDTH - 1 - step
        rows = group_rows(group)
        below.append(jnp.where(flag, first_ref[top, rows, :], second_ref[top, rows, :]))
        above.append(jnp.where(flag, second_ref[low, rows, :], first_ref[low, rows, :]))
    return below, above


def eta_sources(grid, state_ref, source_ref):
    for group in range(grid.xi_groups):
        cells = [state_ref[grid.eta_tile(i, group), :] for i in range(grid.ny)]
        for i, value in enumerate(smooth_source(cells)):
            source_ref[grid.eta_major(i, group), :] = value


def xi_sources(grid, state_ref, source_ref):
    for group in range(grid.eta_groups):
        cells = [state_ref[grid.xi_tile(i, group), :] for i in range(grid.nx)]
        for i, value in enumerate(smooth_source(cells)):
            source_ref[grid.xi_tile(i, group), :] = value


def eta_filter(grid, source_ref, eta_a, eta_b, base, result_ref):
    for group in range(grid.xi_groups):
        below, above = take_cells(eta_a, eta_b, odd("eta"), base, group)
        rights = [source_ref[grid.eta_major(i, group), :] for i in range(grid.ny)]
        for i, value in enumerate(smooth_solve(rights, below, above)):
            result_ref[grid.eta_tile(i, group), :] = value


def xi_filter(grid, source_ref, xi_a, xi_b, base, smooth, result_ref):
    for group in range(grid.eta_groups):
        below, above = take_faces(xi_a, xi_b, odd("xi"), base, group)
        rights = [source_ref[grid.xi_tile(i, group), :] for i in range(grid.nx)]
        for i, value in enumerate(smooth_solve(rights, below, above)):
            result_ref[grid.xi_tile(i, group), :] = value
    result_ref[...] = lane_product(result_ref[...], smooth)


def source_kernel(grid, form, state_ref, source_ref):
    for field in range(state_ref.shape[0]):
        form(grid, state_ref.at[field], source_ref.at[field])


def face_kernel(
    grid, state_ref, source_ref, eta_a, eta_b, result_ref, next_ref, xi_first, xi_second
):
    flag = odd("xi")
    eta_filter(grid, source_ref.at[0], eta_a, eta_b, 2 * 4, result_ref.at[0])
    for field in range(5):
        values = state_ref.at[field] if field < 4 else result_ref.at[0]
        send_faces(
            grid, lambda position, group: values[grid.xi_tile(position, group), :],
            flag, xi_first, xi_second, WIDTH * field,
        )
    xi_sources(grid, result_ref.at[0], next_ref.at[0])


PLANES = 3 * TILE


def halo_source_kernel(grid, first_ref, second_ref, first_source, second_source):
    for faces, source in ((first_ref, first_source), (second_ref, second_source)):
        for tile in range(PLANES // TILE):
            cells = [
                faces[pl.ds(tile * TILE * grid.ny + i, TILE, stride=grid.ny), :] for i in range(grid.ny)
            ]
            for i, value in enumerate(smooth_source(cells)):
                source[pl.ds(i * PLANES + tile * TILE, TILE), :] = value


def edge_kernel(grid, order_ref, eta_b, eta_a, first_ref, second_ref):
    flag = odd("xi")
    eta_flag = odd("eta")
    for side in range(2):
        for step in range(WIDTH):
            start = (side * WIDTH + step) * PLANES
            for field in range(4):
                one, other = eta_a[WIDTH * field + step], eta_b[WIDTH * field + step]
                cells = jnp.where(eta_flag, other, one) if side else jnp.where(eta_flag, one, other)
                low, top = cells[:WIDTH], cells[grid.nx - WIDTH :]
                rows = pl.ds(start + WIDTH * field, WIDTH)
                first_ref[rows, :] = jnp.where(flag, low, top)
                second_ref[rows, :] = jnp.where(flag, top, low)
            rest = pl.ds(start + 4 * WIDTH, PLANES - 4 * WIDTH)
            first_ref[rest, :] = jnp.zeros((PLANES - 4 * WIDTH, LANES), jnp.float32)
            second_ref[rest, :] = jnp.zeros((PLANES - 4 * WIDTH, LANES), jnp.float32)


def filter_halo(grid, source_ref, edge_ref, result_ref):
    for tile in range(PLANES // TILE):
        ends = [
            [edge_ref[pl.ds((side * WIDTH + i) * PLANES + tile * TILE, TILE), :] for i in range(WIDTH)]
            for side in range(2)
        ]
        rights = [source_ref[pl.ds(i * PLANES + tile * TILE, TILE), :] for i in range(grid.ny)]
        for i, value in enumerate(smooth_solve(rights, *ends)):
            result_ref[pl.ds(tile * TILE * grid.ny + i, TILE, stride=grid.ny), :] = value


def eta_filter_kernel(
    grid, source_ref, mass_ref, eta_a, eta_b,
    result_ref, zeta_ref, edge_first, edge_second,
):
    flag = odd("xi")
    for field in range(4):
        eta_filter(grid, source_ref.at[field], eta_a, eta_b, WIDTH * field, result_ref.at[field])
    lane = lax.broadcasted_iota(jnp.int32, (TILE, LANES), 1)
    for position in range(grid.nx):
        packed = None
        for slot in range(5 * grid.eta_groups):
            field, group = slot // grid.eta_groups, slot % grid.eta_groups
            rows = grid.xi_tile(position, group)
            part = result_ref[field - 1, rows, :] if field else mass_ref[0, rows, :]
            part = pltpu.roll(part, WIDTH * (2 * slot + 1), axis=1)
            packed = part if packed is None else jnp.where(lane >= 2 * WIDTH * slot, part, packed)
        zeta_ref[group_rows(position), :] = packed
    send_cells(
        lambda position, group: zeta_ref[group_rows(position), :],
        1, grid.nx, flag, edge_first, edge_second, 0,
    )


def mass_xi_kernel(grid, source_ref, xi_a, xi_b, tables_ref, order_ref, result_ref):
    smooth = split_weights(tables_ref[SMOOTH])
    xi_filter(grid, source_ref.at[0], xi_a, xi_b, WIDTH * 4, smooth, result_ref.at[0])


def xi_filter_kernel(
    grid, source_ref, first_source, second_source, edge_b, edge_a, tables_ref, result_ref,
    first_ref, second_ref,
):
    smooth = split_weights(tables_ref[SMOOTH])
    filter_halo(grid, first_source, edge_a, first_ref)
    filter_halo(grid, second_source, edge_b, second_ref)

    class Layers:
        def __init__(self, ref):
            self.ref = ref

        def __getitem__(self, index):
            layer, rows, _ = index
            return self.ref[pl.ds(layer * grid.ny + rows.start, rows.size), :]

    for field in range(4):
        xi_filter(
            grid, source_ref.at[field], Layers(first_ref), Layers(second_ref), WIDTH * field, smooth,
            result_ref.at[field],
        )


def zeta_filter_kernel(
    grid,
    mass_ref, state_ref, b_below, b_above, below_ref, above_ref, a_below, a_above, tables_ref,
    result_hbm,
    result_ref, sems,
):
    ends = split_weights(tables_ref[ENDS])
    flag = odd("xi")
    lane = lax.broadcasted_iota(jnp.int32, (TILE, LANES), 1)
    from_below = lax.rem(lane, 2 * WIDTH) < WIDTH

    def merge(below, above, index):
        return jnp.where(from_below, below[group_rows(index), :], above[group_rows(index), :])

    low, high = [], []
    for step in range(WIDTH):
        first, second = merge(a_below, a_above, step), merge(b_below, b_above, step)
        low.append(jnp.where(flag, first, second))
        high.append(jnp.where(flag, second, first))
    cells = [merge(below_ref, above_ref, position) for position in range(grid.nx)]
    cells = smooth_solve(smooth_source(cells), low, high)
    copies = []
    for field in range(5):
        parts = []
        for packed in cells:
            for group in range(grid.eta_groups):
                slot = field * grid.eta_groups + group
                parts.append(pltpu.roll(packed, LANES - 2 * WIDTH * slot, axis=1) if slot else packed)
        halo = jnp.concatenate(parts, axis=0)
        own = state_ref[field - 1] if field else mass_ref[0]
        result_ref[field] = own + lane_product(halo, ends)
        copy = pltpu.make_async_copy(result_ref.at[field], result_hbm.at[field], sems.at[field])
        copy.start()
        copies.append(copy)
    for copy in copies:
        copy.wait()


def pair_swap(value, axis, parity):
    count = lax.axis_size(axis)
    pairs = []
    for index in range(count):
        step = 1 if index % 2 == parity else -1
        pairs.append((index, (index + step) % count))
    return lax.ppermute(value, axis, pairs)


def diagonal_swap(value, parity):
    nx, nz = lax.axis_size("xi"), lax.axis_size("zeta")

    def send(shift):
        pairs = []
        for i in range(nx):
            partner = (i + (1 if i % 2 == parity else -1)) % nx
            for k in range(nz):
                pairs.append((i * nz + k, partner * nz + (k + shift) % nz))
        return lax.ppermute(value, ("xi", "zeta"), pairs)

    below = send(1)
    return (below, below) if nz == 2 else (below, send(-1))


def ring_swap(value, axis):
    count = lax.axis_size(axis)
    if count == 2:
        other = lax.ppermute(value, axis, [(0, 1), (1, 0)])
        return other, other
    up = [(index, (index + 1) % count) for index in range(count)]
    down = [(index, (index - 1) % count) for index in range(count)]
    return lax.ppermute(value, axis, up), lax.ppermute(value, axis, down)


HBM = pltpu.MemorySpace.HBM


def call(kernel, outs, *operands, scratch=(), cost=1.0, far=(), far_outs=()):
    shapes = [
        out if isinstance(out, jax.ShapeDtypeStruct) else jax.ShapeDtypeStruct(out, jnp.float32)
        for out in outs
    ]
    near = pltpu.MemorySpace.VMEM
    operands = [
        pltpu.with_memory_space_constraint(value, HBM) if index in far else value
        for index, value in enumerate(operands)
    ]
    return pl.pallas_call(
        kernel,
        out_shape=shapes,
        in_specs=[
            pl.BlockSpec(memory_space=HBM if index in far else near) for index in range(len(operands))
        ],
        out_specs=[
            pl.BlockSpec(memory_space=HBM if index in far_outs else near) for index in range(len(outs))
        ],
        scratch_shapes=scratch,
        cost_estimate=pl.CostEstimate(flops=0, transcendentals=0, bytes_accessed=int(cost * 3.6e6)),
        compiler_params=pltpu.CompilerParams(vmem_limit_bytes=20 * 2**20),
    )(*operands)


def like(value):
    return jax.ShapeDtypeStruct(value.shape, value.dtype)


def local(conserved_solution, metrics, jacobian):
    _, nx, ny, nz = conserved_solution.shape
    grid = Grid(nx, ny)
    rows = grid.rows
    u = conserved_solution.reshape(5, rows, nz)
    metrics = metrics.reshape(9, rows, nz)
    jacobian = jacobian.reshape(rows, nz)
    sums, tables = (jnp.asarray(table) for table in zeta_tables(nz))

    def exchange(eta_first, eta_second, xi_first, xi_second, zeta):
        eta_b = pair_swap(eta_second, "eta", 1)
        eta_a = pair_swap(eta_first, "eta", 0)
        xi_b = pair_swap(xi_second, "xi", 1)
        below, above = ring_swap(zeta, "zeta")
        xi_a = pair_swap(xi_first, "xi", 0)
        return (eta_a, eta_b, xi_b, xi_a), (below, above)

    block = (rows, nz)
    chunks = 2
    u, sums, metrics, prim, mass, *sends = call(
        functools.partial(primitive_kernel, grid),
        [like(u), like(sums), like(metrics), (4, *block), (3, *block)]
        + [(2 * 5, nx, nz)] * 2
        + [(2 * 5, ny, nz)] * 2
        + [(5, TILE, LANES)],
        u, sums, metrics,
        scratch=[pltpu.SemaphoreType.DMA((chunks,)), pltpu.SemaphoreType.DMA((10,))],
        far=(0, 1, 2),
    )
    tables, jacobian = call(
        functools.partial(fetch_kernel, 2),
        [like(tables), like(jacobian)],
        tables, jacobian, sends[-1],
        scratch=[pltpu.SemaphoreType.DMA((2,))],
        far=(0, 1),
    )
    sides, ends = exchange(*sends)
    xi_source, eta_source, own = call(
        functools.partial(primitive_source_kernel, grid), [(5, *block)] * 3, prim, mass, tables,
    )
    slopes, mass_total = call(
        functools.partial(slope_kernel, grid),
        [(2, 4, *block), block],
        xi_source, eta_source, own, *sides,
    )
    contra, mass, *eta_sends = call(
        functools.partial(flux_kernel, grid),
        [(3, 4, *block), block] + [(2 * 4 + WIDTH, nx, nz)] * 2,
        u, prim, metrics, jacobian, slopes, own, mass_total, *ends, tables,
        scratch=[pltpu.VMEM((4, *block), jnp.float32)],
    )
    sends = call(
        functools.partial(contra_sums_kernel, grid),
        [(2 * 4, ny, nz)] * 2 + [(4, TILE, LANES)],
        contra, sums,
    )
    sides, ends = exchange(*eta_sends, *sends)
    xi_source, eta_source, own = call(
        functools.partial(contra_source_kernel, grid), [(4, *block)] * 3, contra, tables,
    )
    (mass_source,) = call(
        functools.partial(source_kernel, grid, eta_sources), [(1, *block)], mass.reshape(1, *block),
    )
    (total,) = call(
        functools.partial(divergence_kernel, grid),
        [(4, *block)],
        xi_source, eta_source, own, *sides,
    )
    state, eta_first, eta_second = call(
        functools.partial(step_kernel, grid),
        [(4, *block)] + [(4 * WIDTH, nx, nz)] * 2,
        u, jacobian, total, *ends, tables,
    )
    eta_b = pair_swap(eta_second, "eta", 1)
    eta_a = pair_swap(eta_first, "eta", 0)
    mass, mass_source, xi_first, xi_second = call(
        functools.partial(face_kernel, grid),
        [(1, *block)] * 2 + [(5 * WIDTH, ny, nz)] * 2,
        state, mass_source, sides[0], sides[1],
    )
    xi_b = pair_swap(xi_second, "xi", 1)
    xi_a = pair_swap(xi_first, "xi", 0)
    (source,) = call(functools.partial(source_kernel, grid, eta_sources), [(4, *block)], state)
    layers = 5 * WIDTH * ny
    halo_first, halo_second = call(
        functools.partial(halo_source_kernel, grid),
        [(ny * PLANES, nz)] * 2,
        xi_a.reshape(layers, nz), xi_b.reshape(layers, nz),
    )
    edge_first, edge_second = call(
        functools.partial(edge_kernel, grid), [(2 * WIDTH * PLANES, nz)] * 2, source, eta_b, eta_a,
    )
    edge_b = pair_swap(edge_second, "xi", 1)
    edge_a = pair_swap(edge_first, "xi", 0)
    state, zeta, corner_first, corner_second = call(
        functools.partial(eta_filter_kernel, grid),
        [(4, *block), (nx * TILE, LANES)] + [(WIDTH, TILE, LANES)] * 2,
        source, mass, eta_a, eta_b,
    )
    ends = ring_swap(zeta, "zeta")
    edges_b = diagonal_swap(corner_second, 1)
    edges_a = diagonal_swap(corner_first, 0)
    (source,) = call(functools.partial(source_kernel, grid, xi_sources), [(4, *block)], state)
    (state,) = call(
        functools.partial(xi_filter_kernel, grid),
        [(4, *block)],
        source, halo_first, halo_second, edge_b, edge_a, tables,
        scratch=[pltpu.VMEM((PLANES * ny, nz), jnp.float32)] * 2,
    )
    (mass_part,) = call(
        functools.partial(mass_xi_kernel, grid), [(1, *block)], mass_source, xi_a, xi_b, tables, state,
    )
    edges = [edge.reshape(WIDTH * TILE, LANES) for edge in (*edges_a, *edges_b)]
    (result,) = call(
        functools.partial(zeta_filter_kernel, grid),
        [(5, *block)],
        mass_part, state, *edges[2:], *ends, *edges[:2], tables,
        scratch=[pltpu.VMEM((5, *block), jnp.float32), pltpu.SemaphoreType.DMA((5,))],
        far_outs=(0,),
    )
    return result.reshape(5, nx, ny, nz)


def solution(mesh):
    in_specs = (
        P(None, "xi", "eta", "zeta"),
        P(None, None, "xi", "eta", "zeta"),
        P("xi", "eta", "zeta"),
    )
    out_specs = P(None, "xi", "eta", "zeta")
    return jax.shard_map(local, mesh=mesh, in_specs=in_specs, out_specs=out_specs, check_vma=False)
```

```python
import functools

import jax
import jax.numpy as jnp
import numpy as np
from jax import lax
from jax.experimental import pallas as pl
from jax.experimental.pallas import tpu as pltpu
from jax.sharding import PartitionSpec as P

WIDTH = 5
LANES = 128
TILE = 8

viscosity = 0.15
conduction = 0.15 * 1.4 / (0.4 * 0.72)
step_duration = 0.08


def derivative_system(length):
    extent = length + 2 * WIDTH
    system = np.eye(extent)
    source = np.zeros((extent, extent))
    for position in range(2, extent - 2):
        system[position, position - 1] = 1.0 / 3.0
        system[position, position + 1] = 1.0 / 3.0
        source[position, position + 1] = 7.0 / 9.0
        source[position, position - 1] = -7.0 / 9.0
        source[position, position + 2] = 1.0 / 36.0
        source[position, position - 2] = -1.0 / 36.0
    source[1, 2] = 0.5
    source[1, 0] = -0.5
    source[extent - 2, extent - 1] = 0.5
    source[extent - 2, extent - 3] = -0.5
    source[0, 1] = 1.0
    source[0, 0] = -1.0
    source[extent - 1, extent - 1] = 1.0
    source[extent - 1, extent - 2] = -1.0
    return system, source


def filter_coefficients():
    strength = 0.4
    return [
        (193.0 + 126.0 * strength) / 256.0,
        (105.0 + 302.0 * strength) / 256.0,
        15.0 * (2.0 * strength - 1.0) / 64.0,
        45.0 * (1.0 - 2.0 * strength) / 512.0,
        5.0 * (2.0 * strength - 1.0) / 256.0,
        (1.0 - 2.0 * strength) / 512.0,
    ]


def filter_system(length):
    strength = 0.4
    coeffs = filter_coefficients()
    extent = length + 2 * WIDTH
    system = np.eye(extent)
    source = np.eye(extent)
    for position in range(5, extent - 5):
        system[position, position - 1] = strength
        system[position, position + 1] = strength
        source[position, position] = coeffs[0]
        for offset in range(1, 6):
            source[position, position + offset] = coeffs[offset] / 2.0
            source[position, position - offset] = coeffs[offset] / 2.0
    return system, source


def own_rows(system, source, length):
    return np.linalg.solve(system, source)[WIDTH : WIDTH + length]


def derivative_parts(length):
    system, source = derivative_system(length)
    halo = np.linalg.solve(system[:WIDTH, :WIDTH], source[:WIDTH])
    row = source[WIDTH] - system[WIDTH, WIDTH - 1] * halo[WIDTH - 1]
    pivots = [1.0]
    for position in range(3, WIDTH + length):
        pivots.append(1.0 - 1.0 / 9.0 / pivots[-1])
    return pivots[WIDTH - 2 :], row[:WIDTH], row[WIDTH : WIDTH + 3]


def pad_rows(table):
    return np.concatenate([table, np.zeros((LANES - table.shape[0], table.shape[1]))], axis=0)


def pad_columns(table):
    return np.concatenate([table, np.zeros((table.shape[0], LANES - table.shape[1]))], axis=1)


def zeta_tables(length):
    system, source = derivative_system(length)
    table = own_rows(system, source, length)
    _, edge, _ = derivative_parts(length)
    inverse = np.linalg.inv(system)
    extent = length + 2 * WIDTH
    sums = np.zeros((length, 4))
    sums[length - WIDTH :, 0] = edge
    sums[length - 1, 1] = 1.0
    sums[:WIDTH, 2] = -edge[::-1]
    sums[0, 3] = 1.0
    own = slice(WIDTH, WIDTH + length)
    back = np.stack(
        [
            inverse[own, WIDTH],
            -1.0 / 36.0 * inverse[own, WIDTH + 1],
            inverse[own, extent - WIDTH - 1],
            1.0 / 36.0 * inverse[own, extent - WIDTH - 2],
        ]
    )
    smooth = own_rows(*filter_system(length), length)
    ends = np.concatenate([smooth[:, :WIDTH], smooth[:, WIDTH + length :]], axis=1)
    tables = [table[:, own].T, pad_columns(sums), pad_rows(back), smooth[:, own].T, pad_rows(ends.T)]
    return tables.pop(1).astype(np.float32), np.stack(tables).astype(np.float32)


DERIVE, BACK, SMOOTH, ENDS = range(4)


def twisted_solve(rights, pivots, off):
    count = len(rights)
    half = count // 2
    low = [rights[0]]
    high = [rights[count - 1]]
    for step in range(1, half):
        factor = off / pivots[step - 1]
        low.append(rights[step] - factor * low[-1])
        high.append(rights[count - 1 - step] - factor * high[-1])
    middle = pivots[half - 1]
    det = middle * middle - off * off
    first, second = low[-1], high[-1]
    answer = [None] * count
    answer[half - 1] = (middle / det) * first - (off / det) * second
    answer[half] = (middle / det) * second - (off / det) * first
    for step in range(half - 2, -1, -1):
        scale = 1.0 / pivots[step]
        factor = off / pivots[step]
        answer[step] = scale * low[step] - factor * answer[step + 1]
        answer[count - 1 - step] = scale * high[step] - factor * answer[count - 2 - step]
    return answer


def derive_source(cells):
    count = len(cells)
    _, _, edge = derivative_parts(count)
    near, far = 7.0 / 9.0, 1.0 / 36.0
    rights = [None] * count
    rights[0] = edge[0] * cells[0] + edge[1] * cells[1] + edge[2] * cells[2]
    rights[1] = near * (cells[2] - cells[0]) + far * cells[3]
    for step in range(2, count - 2):
        rights[step] = near * (cells[step + 1] - cells[step - 1]) + far * (
            cells[step + 2] - cells[step - 2]
        )
    rights[count - 2] = near * (cells[count - 1] - cells[count - 3]) - far * cells[count - 4]
    rights[count - 1] = -(
        edge[0] * cells[count - 1] + edge[1] * cells[count - 2] + edge[2] * cells[count - 3]
    )
    return rights


def derive_solve(rights, below, above):
    pivots, _, _ = derivative_parts(len(rights))
    rights = list(rights)
    far = 1.0 / 36.0
    rights[0] = rights[0] + below[0]
    rights[1] = rights[1] - far * below[1]
    rights[-2] = rights[-2] + far * above[1]
    rights[-1] = rights[-1] + above[0]
    return twisted_solve(rights, pivots, 1.0 / 3.0)


def end_sums(cells):
    _, edge, _ = derivative_parts(16)
    total = edge[WIDTH - 1] * cells[0]
    for step in range(1, WIDTH):
        total = total + edge[WIDTH - 1 - step] * cells[step]
    return total, cells[0]


def smooth_source(cells):
    count = len(cells)
    coeffs = filter_coefficients()
    rights = []
    for step in range(count):
        total = coeffs[0] * cells[step]
        for offset in range(1, WIDTH + 1):
            around = [cells[i] for i in (step - offset, step + offset) if 0 <= i < count]
            around = around[0] + around[1] if len(around) == 2 else around[0]
            total = total + (0.5 * coeffs[offset]) * around
        rights.append(total)
    return rights


def smooth_solve(rights, below, above):
    count = len(rights)
    coeffs = filter_coefficients()
    rights = list(rights)
    for step in range(WIDTH):
        for cell in range(WIDTH - step):
            factor = 0.5 * coeffs[step + cell + 1]
            if step == 0 and cell == 0:
                factor = factor - 0.4
            rights[step] = rights[step] + factor * below[cell]
            rights[count - 1 - step] = rights[count - 1 - step] + factor * above[cell]
    pivots = [1.0]
    for _ in range(count):
        pivots.append(1.0 - 0.16 / pivots[-1])
    return twisted_solve(rights, pivots, 0.4)


def split_values(values):
    high = values.astype(jnp.bfloat16)
    low = (values - high.astype(jnp.float32)).astype(jnp.bfloat16)
    return jnp.concatenate([high, low], axis=1)


def split_weights(table):
    high = table.astype(jnp.bfloat16)
    low = (table - high.astype(jnp.float32)).astype(jnp.bfloat16)
    top = jnp.concatenate([high, low], axis=1)
    return jnp.concatenate([top, jnp.concatenate([high, jnp.zeros_like(low)], axis=1)], axis=0)


def lane_product(values, weights):
    both = jnp.dot(split_values(values), weights, preferred_element_type=jnp.float32)
    return both[:, :LANES] + both[:, LANES:]


class Grid:
    def __init__(self, nx, ny):
        self.nx, self.ny, self.rows = nx, ny, nx * ny
        self.eta_groups = ny // TILE
        self.xi_groups = nx // TILE

    def xi_tile(self, position, group):
        return pl.ds(position * self.ny + group * TILE, TILE)

    def eta_tile(self, position, group):
        return pl.ds(position + group * TILE * self.ny, TILE, stride=self.ny)

    def eta_major(self, position, group):
        return pl.ds(position * self.nx + group * TILE, TILE)


def group_rows(group):
    return pl.ds(group * TILE, TILE)


def odd(axis):
    return lax.rem(lax.axis_index(axis), 2) == 1


def send_sums(read, groups, count, flag, first_ref, second_ref, field):
    for group in range(groups):
        top = end_sums([read(count - 1 - step, group) for step in range(WIDTH)])
        low = end_sums([read(step, group) for step in range(WIDTH)])
        low = (-low[0], low[1])
        for part in range(2):
            first_ref[2 * field + part, group_rows(group), :] = jnp.where(flag, low[part], top[part])
            second_ref[2 * field + part, group_rows(group), :] = jnp.where(flag, top[part], low[part])


def take_sums(first_ref, second_ref, flag, field, group):
    below, above = [], []
    for part in range(2):
        first = first_ref[2 * field + part, group_rows(group), :]
        second = second_ref[2 * field + part, group_rows(group), :]
        below.append(jnp.where(flag, first, second))
        above.append(jnp.where(flag, second, first))
    return below, above


def pack_sums(values, weights, grid):
    sums = lane_product(values, weights)
    parts = []
    for group in range(grid.rows // TILE):
        part = sums[group * TILE : (group + 1) * TILE]
        parts.append(pltpu.roll(part, 4 * group, axis=1) if group else part)
    while len(parts) > 1:
        parts = [sum(parts[i + 1 : i + 2], parts[i]) for i in range(0, len(parts), 2)]
    return parts[0]


def unpack_sums(below, above, grid):
    lane = lax.broadcasted_iota(jnp.int32, below.shape, 1)
    packed = jnp.where(lax.rem(lane, 4) < 2, below, above)
    parts = [packed]
    for group in range(1, grid.rows // TILE):
        parts.append(pltpu.roll(packed, LANES - 4 * group, axis=1))
    return jnp.concatenate(parts, axis=0)


def primitive_kernel(
    grid,
    u_hbm, sums_hbm, metrics_hbm,
    u_ref, sums_ref, metrics_ref,
    prim_ref, mass_ref, eta_first, eta_second, xi_first, xi_second, zeta_ref,
    u_sems, late_sems,
):
    chunks = u_sems.shape[0]
    step = grid.rows // chunks
    weights = pltpu.make_async_copy(sums_hbm, sums_ref, late_sems.at[0])
    weights.start()
    copies = []
    for index in range(chunks):
        rows = pl.ds(index * step, step)
        copy = pltpu.make_async_copy(u_hbm.at[:, rows, :], u_ref.at[:, rows, :], u_sems.at[index])
        copy.start()
        copies.append(copy)
    late = [
        pltpu.make_async_copy(source, result, late_sems.at[index])
        for index, (source, result) in enumerate(
            [(sums_hbm, sums_ref)] + [(metrics_hbm, metrics_ref)]
        )
    ]
    for copy in late[1:]:
        copy.start()
    for index in range(chunks):
        copies[index].wait()
        rows = pl.ds(index * step, step)
        inverse = 1.0 / u_ref[0, rows, :]
        work = None
        for c in range(3):
            momentum = u_ref[1 + c, rows, :]
            speed = momentum * inverse
            prim_ref[c, rows, :] = speed
            work = momentum * speed if work is None else work + momentum * speed
        pressure = 0.4 * (u_ref[4, rows, :] - 0.5 * work)
        prim_ref[3, rows, :] = pressure * inverse

    def send(xi_value, eta_value, field):
        send_sums(
            lambda position, group: eta_value[grid.eta_tile(position, group), :],
            grid.xi_groups, grid.ny, odd("eta"), eta_first, eta_second, field,
        )
        send_sums(
            lambda position, group: xi_value[grid.xi_tile(position, group), :],
            grid.eta_groups, grid.nx, odd("xi"), xi_first, xi_second, field,
        )

    for field in range(4):
        send(prim_ref.at[field], prim_ref.at[field], field)
    weights.wait()
    sums = split_weights(sums_ref[...])
    for field in range(4):
        zeta_ref[field] = pack_sums(prim_ref[field], sums, grid)
    for copy in late[1:]:
        copy.wait()
    for k in range(3):
        for index in range(chunks):
            rows = pl.ds(index * step, step)
            mass_ref[k, rows, :] = (
                metrics_ref[3 * k, rows, :] * u_ref[1, rows, :]
                + metrics_ref[3 * k + 1, rows, :] * u_ref[2, rows, :]
                + metrics_ref[3 * k + 2, rows, :] * u_ref[3, rows, :]
            )
    send(mass_ref.at[0], mass_ref.at[1], 4)
    zeta_ref[4] = pack_sums(mass_ref[2], sums, grid)


def derive_sources(grid, xi_value, eta_value, field, xi_ref, eta_ref):
    for group in range(grid.eta_groups):
        cells = [xi_value[grid.xi_tile(i, group), :] for i in range(grid.nx)]
        for i, value in enumerate(derive_source(cells)):
            xi_ref[field, grid.xi_tile(i, group), :] = value
    for group in range(grid.xi_groups):
        cells = [eta_value[grid.eta_tile(i, group), :] for i in range(grid.ny)]
        for i, value in enumerate(derive_source(cells)):
            eta_ref[field, grid.eta_major(i, group), :] = value


def primitive_source_kernel(
    grid, prim_ref, mass_ref, tables_hbm, jacobian_hbm,
    xi_ref, eta_ref, zeta_ref, tables_ref, jacobian_ref, sems,
):
    copies = [
        pltpu.make_async_copy(tables_hbm, tables_ref, sems.at[0]),
        pltpu.make_async_copy(jacobian_hbm, jacobian_ref, sems.at[1]),
    ]
    for copy in copies:
        copy.start()
    for field in range(4):
        derive_sources(grid, prim_ref.at[field], prim_ref.at[field], field, xi_ref, eta_ref)
    derive_sources(grid, mass_ref.at[0], mass_ref.at[1], 4, xi_ref, eta_ref)
    copies[0].wait()
    derive = split_weights(tables_ref[DERIVE])
    for field in range(5):
        values = prim_ref[field] if field < 4 else mass_ref[2]
        zeta_ref[field] = lane_product(values, derive)
    copies[1].wait()


def contra_source_kernel(grid, contra_ref, tables_ref, xi_ref, eta_ref, zeta_ref):
    derive = split_weights(tables_ref[DERIVE])
    for field in range(4):
        zeta_ref[field] = lane_product(contra_ref[2, field], derive)
        derive_sources(grid, contra_ref.at[0, field], contra_ref.at[1, field], field, xi_ref, eta_ref)


def xi_derivative(grid, source_ref, xi_a, xi_b, field, group):
    below, above = take_sums(xi_a, xi_b, odd("xi"), field, group)
    rights = [source_ref[field, grid.xi_tile(i, group), :] for i in range(grid.nx)]
    return derive_solve(rights, below, above)


def eta_derivative(grid, source_ref, eta_a, eta_b, field, group):
    below, above = take_sums(eta_a, eta_b, odd("eta"), field, group)
    rights = [source_ref[field, grid.eta_major(i, group), :] for i in range(grid.ny)]
    return derive_solve(rights, below, above)


def eta_slope_kernel(grid, source_ref, own_ref, eta_a, eta_b, slope_ref, mass_total_ref):
    for field in range(5):
        for group in range(grid.xi_groups):
            for i, value in enumerate(eta_derivative(grid, source_ref, eta_a, eta_b, field, group)):
                rows = grid.eta_tile(i, group)
                if field < 4:
                    slope_ref[field, rows, :] = value
                else:
                    mass_total_ref[rows, :] = own_ref[4, rows, :] + value


def zeta_slope_kernel(grid, own_ref, part_ref, below_ref, above_ref, tables_ref, slope_ref, mass_total_ref):
    back = split_weights(tables_ref[BACK])
    for field in range(5):
        beyond = lane_product(unpack_sums(below_ref[field], above_ref[field], grid), back)
        if field < 4:
            slope_ref[field] = own_ref[field] + beyond
        else:
            mass_total_ref[...] = part_ref[...] + beyond


def xi_slope_kernel(grid, source_ref, part_ref, xi_b, xi_a, slope_ref, mass_total_ref):
    for field in range(5):
        for group in range(grid.eta_groups):
            for i, value in enumerate(xi_derivative(grid, source_ref, xi_a, xi_b, field, group)):
                rows = grid.xi_tile(i, group)
                if field < 4:
                    slope_ref[field, rows, :] = value
                else:
                    mass_total_ref[rows, :] = part_ref[rows, :] + value


def flux_kernel(
    grid,
    u_ref, prim_ref, metrics_ref, jacobian_ref, xi_slope_ref, eta_slope_ref, zeta_slope_ref, mass_total_ref,
    contra_ref, mass_ref, eta_first, eta_second,
):
    mass_ref[...] = u_ref[0] - (step_duration * jacobian_ref[...]) * mass_total_ref[...]
    send_cells(
        lambda position, group: mass_ref[grid.eta_tile(position, group), :],
        grid.xi_groups, grid.ny, odd("eta"), eta_first, eta_second, 2 * 4,
    )

    step = TILE

    def body(index, carry):
        rows = pl.ds(pl.multiple_of(index * step, step), step)
        u = [u_ref[c, rows, :] for c in range(5)]
        speed = [prim_ref[c, rows, :] for c in range(3)]
        pressure = prim_ref[3, rows, :] * u[0]
        metrics = [[metrics_ref[3 * k + j, rows, :] for j in range(3)] for k in range(3)]
        scaled = (viscosity * jacobian_ref[rows, :])
        scaled = [[scaled * metrics[k][j] for j in range(3)] for k in range(3)]
        physical = []
        for c in range(4):
            slopes = [ref[c, rows, :] for ref in (xi_slope_ref, eta_slope_ref, zeta_slope_ref)]
            physical.append(
                [
                    scaled[0][j] * slopes[0] + scaled[1][j] * slopes[1] + scaled[2][j] * slopes[2]
                    for j in range(3)
                ]
            )
        spread = (2.0 / 3.0) * (physical[0][0] + physical[1][1] + physical[2][2])
        stress = [[None] * 3 for _ in range(3)]
        momentum = [[None] * 3 for _ in range(3)]
        for c in range(3):
            stress[c][c] = (physical[c][c] + physical[c][c]) - spread
            momentum[c][c] = (u[1 + c] * speed[c] + pressure) - stress[c][c]
            for j in range(c):
                stress[c][j] = stress[j][c] = physical[c][j] + physical[j][c]
                momentum[c][j] = momentum[j][c] = u[1 + c] * speed[j] - stress[c][j]
        total = u[4] + pressure
        fluxes = []
        for j in range(3):
            worked = speed[0] * stress[0][j] + speed[1] * stress[1][j] + speed[2] * stress[2][j]
            energy = (total * speed[j] - worked) - (conduction / viscosity) * physical[3][j]
            fluxes.append([momentum[0][j], momentum[1][j], momentum[2][j], energy])
        for k in range(3):
            for f in range(4):
                contra_ref[k, f, rows, :] = (
                    metrics[k][0] * fluxes[0][f]
                    + metrics[k][1] * fluxes[1][f]
                    + metrics[k][2] * fluxes[2][f]
                )
        return carry

    lax.fori_loop(0, grid.rows // step, body, 0, unroll=4)
    for field in range(4):
        send_sums(
            lambda position, group: contra_ref[1, field, grid.eta_tile(position, group), :],
            grid.xi_groups, grid.ny, odd("eta"), eta_first, eta_second, field,
        )


def zeta_sums_kernel(grid, contra_ref, sums_ref, zeta_ref):
    sums = split_weights(sums_ref[...])
    for field in range(4):
        zeta_ref[field] = pack_sums(contra_ref[2, field], sums, grid)


def xi_sums_kernel(grid, contra_ref, order_ref, xi_first, xi_second):
    for field in range(4):
        send_sums(
            lambda position, group: contra_ref[0, field, grid.xi_tile(position, group), :],
            grid.eta_groups, grid.nx, odd("xi"), xi_first, xi_second, field,
        )


def xi_divergence_kernel(grid, source_ref, own_ref, xi_b, xi_a, total_ref):
    for field in range(4):
        for group in range(grid.eta_groups):
            for i, value in enumerate(xi_derivative(grid, source_ref, xi_a, xi_b, field, group)):
                rows = grid.xi_tile(i, group)
                total_ref[field, rows, :] = own_ref[field, rows, :] + value


def zeta_divergence_kernel(grid, part_ref, below_ref, above_ref, tables_ref, total_ref):
    back = split_weights(tables_ref[BACK])
    for field in range(4):
        beyond = lane_product(unpack_sums(below_ref[field], above_ref[field], grid), back)
        total_ref[field] = part_ref[field] + beyond


def step_kernel(
    grid, u_ref, jacobian_ref, source_ref, total_ref, eta_a, eta_b, state_ref, eta_first, eta_second
):
    scale = step_duration * jacobian_ref[...]
    for field in range(4):
        for group in range(grid.xi_groups):
            for i, value in enumerate(eta_derivative(grid, source_ref, eta_a, eta_b, field, group)):
                state_ref[field, grid.eta_tile(i, group), :] = value
        total = total_ref[field] + state_ref[field]
        state_ref[field] = u_ref[1 + field] - scale * total
        send_cells(
            lambda position, group: state_ref[field, grid.eta_tile(position, group), :],
            grid.xi_groups, grid.ny, odd("eta"), eta_first, eta_second, WIDTH * field,
        )


def send_cells(read, groups, count, flag, first_ref, second_ref, base):
    for group in range(groups):
        for step in range(WIDTH):
            low = read(step, group)
            top = read(count - 1 - step, group)
            first_ref[base + step, group_rows(group), :] = jnp.where(flag, low, top)
            second_ref[base + step, group_rows(group), :] = jnp.where(flag, top, low)


def take_cells(first_ref, second_ref, flag, base, group):
    below, above = [], []
    for step in range(WIDTH):
        first = first_ref[base + step, group_rows(group), :]
        second = second_ref[base + step, group_rows(group), :]
        below.append(jnp.where(flag, first, second))
        above.append(jnp.where(flag, second, first))
    return below, above


def send_faces(grid, read, flag, first_ref, second_ref, base):
    for group in range(grid.eta_groups):
        for step in range(WIDTH):
            low = read(step, group)
            top = read(grid.nx - WIDTH + step, group)
            first_ref[base + step, group_rows(group), :] = jnp.where(flag, low, top)
            second_ref[base + step, group_rows(group), :] = jnp.where(flag, top, low)


def take_faces(first_ref, second_ref, flag, base, group):
    below, above = [], []
    for step in range(WIDTH):
        low, top = base + step, base + WIDTH - 1 - step
        rows = group_rows(group)
        below.append(jnp.where(flag, first_ref[top, rows, :], second_ref[top, rows, :]))
        above.append(jnp.where(flag, second_ref[low, rows, :], first_ref[low, rows, :]))
    return below, above


def eta_sources(grid, state_ref, source_ref):
    for group in range(grid.xi_groups):
        cells = [state_ref[grid.eta_tile(i, group), :] for i in range(grid.ny)]
        for i, value in enumerate(smooth_source(cells)):
            source_ref[grid.eta_major(i, group), :] = value


def xi_sources(grid, state_ref, source_ref):
    for group in range(grid.eta_groups):
        cells = [state_ref[grid.xi_tile(i, group), :] for i in range(grid.nx)]
        for i, value in enumerate(smooth_source(cells)):
            source_ref[grid.xi_tile(i, group), :] = value


def eta_filter(grid, source_ref, eta_a, eta_b, base, result_ref):
    for group in range(grid.xi_groups):
        below, above = take_cells(eta_a, eta_b, odd("eta"), base, group)
        rights = [source_ref[grid.eta_major(i, group), :] for i in range(grid.ny)]
        for i, value in enumerate(smooth_solve(rights, below, above)):
            result_ref[grid.eta_tile(i, group), :] = value


def xi_filter(grid, source_ref, xi_a, xi_b, base, smooth, result_ref):
    for group in range(grid.eta_groups):
        below, above = take_faces(xi_a, xi_b, odd("xi"), base, group)
        rights = [source_ref[grid.xi_tile(i, group), :] for i in range(grid.nx)]
        for i, value in enumerate(smooth_solve(rights, below, above)):
            result_ref[grid.xi_tile(i, group), :] = value
    result_ref[...] = lane_product(result_ref[...], smooth)


def source_kernel(grid, form, state_ref, source_ref):
    for field in range(state_ref.shape[0]):
        form(grid, state_ref.at[field], source_ref.at[field])


def face_kernel(
    grid, state_ref, source_ref, eta_a, eta_b, result_ref, next_ref, xi_first, xi_second
):
    flag = odd("xi")
    eta_filter(grid, source_ref.at[0], eta_a, eta_b, 2 * 4, result_ref.at[0])
    for field in range(5):
        values = state_ref.at[field] if field < 4 else result_ref.at[0]
        send_faces(
            grid, lambda position, group: values[grid.xi_tile(position, group), :],
            flag, xi_first, xi_second, WIDTH * field,
        )
    xi_sources(grid, result_ref.at[0], next_ref.at[0])


PLANES = 3 * TILE


def halo_source_kernel(grid, first_ref, second_ref, first_source, second_source):
    for faces, source in ((first_ref, first_source), (second_ref, second_source)):
        for tile in range(PLANES // TILE):
            cells = [
                faces[pl.ds(tile * TILE * grid.ny + i, TILE, stride=grid.ny), :] for i in range(grid.ny)
            ]
            for i, value in enumerate(smooth_source(cells)):
                source[pl.ds(i * PLANES + tile * TILE, TILE), :] = value


def edge_kernel(grid, order_ref, eta_b, eta_a, first_ref, second_ref):
    flag = odd("xi")
    eta_flag = odd("eta")
    for side in range(2):
        for step in range(WIDTH):
            start = (side * WIDTH + step) * PLANES
            for field in range(4):
                one, other = eta_a[WIDTH * field + step], eta_b[WIDTH * field + step]
                cells = jnp.where(eta_flag, other, one) if side else jnp.where(eta_flag, one, other)
                low, top = cells[:WIDTH], cells[grid.nx - WIDTH :]
                rows = pl.ds(start + WIDTH * field, WIDTH)
                first_ref[rows, :] = jnp.where(flag, low, top)
                second_ref[rows, :] = jnp.where(flag, top, low)
            rest = pl.ds(start + 4 * WIDTH, PLANES - 4 * WIDTH)
            first_ref[rest, :] = jnp.zeros((PLANES - 4 * WIDTH, LANES), jnp.float32)
            second_ref[rest, :] = jnp.zeros((PLANES - 4 * WIDTH, LANES), jnp.float32)


def filter_halo(grid, source_ref, edge_ref, result_ref):
    for tile in range(PLANES // TILE):
        ends = [
            [edge_ref[pl.ds((side * WIDTH + i) * PLANES + tile * TILE, TILE), :] for i in range(WIDTH)]
            for side in range(2)
        ]
        rights = [source_ref[pl.ds(i * PLANES + tile * TILE, TILE), :] for i in range(grid.ny)]
        for i, value in enumerate(smooth_solve(rights, *ends)):
            result_ref[pl.ds(tile * TILE * grid.ny + i, TILE, stride=grid.ny), :] = value


def eta_filter_kernel(
    grid, source_ref, mass_ref, eta_a, eta_b,
    result_ref, zeta_ref, edge_first, edge_second,
):
    flag = odd("xi")
    for field in range(4):
        eta_filter(grid, source_ref.at[field], eta_a, eta_b, WIDTH * field, result_ref.at[field])
    lane = lax.broadcasted_iota(jnp.int32, (TILE, LANES), 1)
    for position in range(grid.nx):
        packed = None
        for slot in range(5 * grid.eta_groups):
            field, group = slot // grid.eta_groups, slot % grid.eta_groups
            rows = grid.xi_tile(position, group)
            part = result_ref[field - 1, rows, :] if field else mass_ref[0, rows, :]
            part = pltpu.roll(part, WIDTH * (2 * slot + 1), axis=1)
            packed = part if packed is None else jnp.where(lane >= 2 * WIDTH * slot, part, packed)
        zeta_ref[group_rows(position), :] = packed
    send_cells(
        lambda position, group: zeta_ref[group_rows(position), :],
        1, grid.nx, flag, edge_first, edge_second, 0,
    )


def mass_xi_kernel(grid, source_ref, xi_a, xi_b, tables_ref, result_ref):
    smooth = split_weights(tables_ref[SMOOTH])
    xi_filter(grid, source_ref.at[0], xi_a, xi_b, WIDTH * 4, smooth, result_ref.at[0])


def xi_filter_kernel(
    grid, source_ref, first_source, second_source, edge_b, edge_a, tables_ref, result_ref,
    first_ref, second_ref,
):
    smooth = split_weights(tables_ref[SMOOTH])
    filter_halo(grid, first_source, edge_a, first_ref)
    filter_halo(grid, second_source, edge_b, second_ref)

    class Layers:
        def __init__(self, ref):
            self.ref = ref

        def __getitem__(self, index):
            layer, rows, _ = index
            return self.ref[pl.ds(layer * grid.ny + rows.start, rows.size), :]

    for field in range(4):
        xi_filter(
            grid, source_ref.at[field], Layers(first_ref), Layers(second_ref), WIDTH * field, smooth,
            result_ref.at[field],
        )


def zeta_filter_kernel(
    grid,
    mass_ref, state_ref, b_below, b_above, below_ref, above_ref, a_below, a_above, tables_ref,
    result_hbm,
    result_ref, sems,
):
    ends = split_weights(tables_ref[ENDS])
    flag = odd("xi")
    lane = lax.broadcasted_iota(jnp.int32, (TILE, LANES), 1)
    from_below = lax.rem(lane, 2 * WIDTH) < WIDTH

    def merge(below, above, index):
        return jnp.where(from_below, below[group_rows(index), :], above[group_rows(index), :])

    low, high = [], []
    for step in range(WIDTH):
        first, second = merge(a_below, a_above, step), merge(b_below, b_above, step)
        low.append(jnp.where(flag, first, second))
        high.append(jnp.where(flag, second, first))
    cells = [merge(below_ref, above_ref, position) for position in range(grid.nx)]
    cells = smooth_solve(smooth_source(cells), low, high)
    copies = []
    for field in range(5):
        parts = []
        for packed in cells:
            for group in range(grid.eta_groups):
                slot = field * grid.eta_groups + group
                parts.append(pltpu.roll(packed, LANES - 2 * WIDTH * slot, axis=1) if slot else packed)
        halo = jnp.concatenate(parts, axis=0)
        own = state_ref[field - 1] if field else mass_ref[0]
        result_ref[field] = own + lane_product(halo, ends)
        copy = pltpu.make_async_copy(result_ref.at[field], result_hbm.at[field], sems.at[field])
        copy.start()
        copies.append(copy)
    for copy in copies:
        copy.wait()


def pair_swap(value, axis, parity):
    count = lax.axis_size(axis)
    pairs = []
    for index in range(count):
        step = 1 if index % 2 == parity else -1
        pairs.append((index, (index + step) % count))
    return lax.ppermute(value, axis, pairs)


def diagonal_swap(value, parity):
    nx, nz = lax.axis_size("xi"), lax.axis_size("zeta")

    def send(shift):
        pairs = []
        for i in range(nx):
            partner = (i + (1 if i % 2 == parity else -1)) % nx
            for k in range(nz):
                pairs.append((i * nz + k, partner * nz + (k + shift) % nz))
        return lax.ppermute(value, ("xi", "zeta"), pairs)

    below = send(1)
    return (below, below) if nz == 2 else (below, send(-1))


def ring_swap(value, axis):
    count = lax.axis_size(axis)
    if count == 2:
        other = lax.ppermute(value, axis, [(0, 1), (1, 0)])
        return other, other
    up = [(index, (index + 1) % count) for index in range(count)]
    down = [(index, (index - 1) % count) for index in range(count)]
    return lax.ppermute(value, axis, up), lax.ppermute(value, axis, down)


HBM = pltpu.MemorySpace.HBM


def call(kernel, outs, *operands, scratch=(), cost=1.0, far=(), far_outs=()):
    shapes = [
        out if isinstance(out, jax.ShapeDtypeStruct) else jax.ShapeDtypeStruct(out, jnp.float32)
        for out in outs
    ]
    near = pltpu.MemorySpace.VMEM
    operands = [
        pltpu.with_memory_space_constraint(value, HBM) if index in far else value
        for index, value in enumerate(operands)
    ]
    return pl.pallas_call(
        kernel,
        out_shape=shapes,
        in_specs=[
            pl.BlockSpec(memory_space=HBM if index in far else near) for index in range(len(operands))
        ],
        out_specs=[
            pl.BlockSpec(memory_space=HBM if index in far_outs else near) for index in range(len(outs))
        ],
        scratch_shapes=scratch,
        cost_estimate=pl.CostEstimate(flops=0, transcendentals=0, bytes_accessed=int(cost * 3.6e6)),
        compiler_params=pltpu.CompilerParams(vmem_limit_bytes=20 * 2**20),
    )(*operands)


def like(value):
    return jax.ShapeDtypeStruct(value.shape, value.dtype)


def local(conserved_solution, metrics, jacobian):
    _, nx, ny, nz = conserved_solution.shape
    grid = Grid(nx, ny)
    rows = grid.rows
    u = conserved_solution.reshape(5, rows, nz)
    metrics = metrics.reshape(9, rows, nz)
    jacobian = jacobian.reshape(rows, nz)
    sums, tables = (jnp.asarray(table) for table in zeta_tables(nz))

    def exchange(eta_first, eta_second, xi_first, xi_second, zeta):
        eta_b = pair_swap(eta_second, "eta", 1)
        eta_a = pair_swap(eta_first, "eta", 0)
        xi_b = pair_swap(xi_second, "xi", 1)
        below, above = ring_swap(zeta, "zeta")
        xi_a = pair_swap(xi_first, "xi", 0)
        return (eta_a, eta_b), (xi_b, xi_a), (below, above)

    block = (rows, nz)
    chunks = 2
    u, sums, metrics, prim, mass, *sends = call(
        functools.partial(primitive_kernel, grid),
        [like(u), like(sums), like(metrics), (4, *block), (3, *block)]
        + [(2 * 5, nx, nz)] * 2
        + [(2 * 5, ny, nz)] * 2
        + [(5, TILE, LANES)],
        u, sums, metrics,
        scratch=[pltpu.SemaphoreType.DMA((chunks,)), pltpu.SemaphoreType.DMA((10,))],
        far=(0, 1, 2),
    )
    eta_sides, xi_sides, ends = exchange(*sends)
    xi_source, eta_source, own, tables, jacobian = call(
        functools.partial(primitive_source_kernel, grid),
        [(5, *block)] * 3 + [like(tables), like(jacobian)],
        prim, mass, tables, jacobian,
        scratch=[pltpu.SemaphoreType.DMA((2,))],
        far=(2, 3),
    )
    eta_slope, mass_total = call(
        functools.partial(eta_slope_kernel, grid), [(4, *block), block], eta_source, own, *eta_sides,
    )
    xi_slope, mass_total = call(
        functools.partial(xi_slope_kernel, grid),
        [(4, *block), block],
        xi_source, mass_total, *xi_sides,
    )
    zeta_slope, mass_total = call(
        functools.partial(zeta_slope_kernel, grid),
        [(4, *block), block],
        own, mass_total, *ends, tables,
    )
    contra, mass, *eta_sends = call(
        functools.partial(flux_kernel, grid),
        [(3, 4, *block), block] + [(2 * 4 + WIDTH, nx, nz)] * 2,
        u, prim, metrics, jacobian, xi_slope, eta_slope, zeta_slope, mass_total,
    )
    (zeta,) = call(
        functools.partial(zeta_sums_kernel, grid), [(4, TILE, LANES)], contra, sums, cost=0.3,
    )
    sends = call(
        functools.partial(xi_sums_kernel, grid), [(2 * 4, ny, nz)] * 2, contra, zeta, cost=0.2,
    )
    eta_sides, xi_sides, ends = exchange(*eta_sends, *sends, zeta)
    xi_source, eta_source, own = call(
        functools.partial(contra_source_kernel, grid), [(4, *block)] * 3, contra, tables,
    )
    (mass_source,) = call(
        functools.partial(source_kernel, grid, eta_sources), [(1, *block)], mass.reshape(1, *block),
    )
    (total,) = call(
        functools.partial(xi_divergence_kernel, grid), [(4, *block)], xi_source, own, *xi_sides,
    )
    (total,) = call(
        functools.partial(zeta_divergence_kernel, grid), [(4, *block)], total, *ends, tables,
    )
    state, eta_first, eta_second = call(
        functools.partial(step_kernel, grid),
        [(4, *block)] + [(4 * WIDTH, nx, nz)] * 2,
        u, jacobian, eta_source, total, *eta_sides,
    )
    eta_b = pair_swap(eta_second, "eta", 1)
    eta_a = pair_swap(eta_first, "eta", 0)
    mass, mass_source, xi_first, xi_second = call(
        functools.partial(face_kernel, grid),
        [(1, *block)] * 2 + [(5 * WIDTH, ny, nz)] * 2,
        state, mass_source, *eta_sides,
    )
    xi_b = pair_swap(xi_second, "xi", 1)
    xi_a = pair_swap(xi_first, "xi", 0)
    (source,) = call(functools.partial(source_kernel, grid, eta_sources), [(4, *block)], state)
    (mass_part,) = call(
        functools.partial(mass_xi_kernel, grid), [(1, *block)], mass_source, xi_a, xi_b, tables,
    )
    layers = 5 * WIDTH * ny
    halo_first, halo_second = call(
        functools.partial(halo_source_kernel, grid),
        [(ny * PLANES, nz)] * 2,
        xi_a.reshape(layers, nz), xi_b.reshape(layers, nz),
    )
    edge_first, edge_second = call(
        functools.partial(edge_kernel, grid), [(2 * WIDTH * PLANES, nz)] * 2, source, eta_b, eta_a,
    )
    edge_b = pair_swap(edge_second, "xi", 1)
    edge_a = pair_swap(edge_first, "xi", 0)
    state, zeta, corner_first, corner_second = call(
        functools.partial(eta_filter_kernel, grid),
        [(4, *block), (nx * TILE, LANES)] + [(WIDTH, TILE, LANES)] * 2,
        source, mass, eta_a, eta_b,
    )
    ends = ring_swap(zeta, "zeta")
    edges_b = diagonal_swap(corner_second, 1)
    edges_a = diagonal_swap(corner_first, 0)
    (source,) = call(functools.partial(source_kernel, grid, xi_sources), [(4, *block)], state)
    (state,) = call(
        functools.partial(xi_filter_kernel, grid),
        [(4, *block)],
        source, halo_first, halo_second, edge_b, edge_a, tables,
        scratch=[pltpu.VMEM((PLANES * ny, nz), jnp.float32)] * 2,
    )
    edges = [edge.reshape(WIDTH * TILE, LANES) for edge in (*edges_a, *edges_b)]
    (result,) = call(
        functools.partial(zeta_filter_kernel, grid),
        [(5, *block)],
        mass_part, state, *edges[2:], *ends, *edges[:2], tables,
        scratch=[pltpu.VMEM((5, *block), jnp.float32), pltpu.SemaphoreType.DMA((5,))],
        far_outs=(0,),
    )
    return result.reshape(5, nx, ny, nz)


def solution(mesh):
    in_specs = (
        P(None, "xi", "eta", "zeta"),
        P(None, None, "xi", "eta", "zeta"),
        P("xi", "eta", "zeta"),
    )
    out_specs = P(None, "xi", "eta", "zeta")
    return jax.shard_map(local, mesh=mesh, in_specs=in_specs, out_specs=out_specs, check_vma=False)
```
